32 devices in a mesh: section: 4 (over y, x), dp: 8 (over z, core).
Axes of the slice: x: 2, y: 2, z: 4, core: 2. Of those that a mesh axis runs over, the one named last changes fastest.
Arguments:
- patches: bfloat16 [32, 256, 768], P(('section', 'dp')), may hold values from -6 to 6
- cotangent: bfloat16 [32, 256, 768], P(('section', 'dp')), may hold values from -6 to 6
- positions: int32 [32, 2, 256], P(('section', 'dp')), may hold values from 0 to 15, as said below
- kept_counts: int32 [32], P(('section', 'dp')), may hold values from 32 to 256, as said below
- norm_gain: float32 [4, 768], P('section'), may hold values from 0.5 to 1.5
- norm_bias: float32 [4, 768], P('section'), may hold values from -4 to 4
- w_main: bfloat16 [4, 768, 3072], P('section')
- b_main: float32 [4, 3072], P('section'), may hold values from -4 to 4
- section_vector: float32 [4, 768], P('section')
- w_down: bfloat16 [4, 1536, 768], P('section'), may hold values from -0.109375 to 0.109375
Outputs:
- outputs: bfloat16 [32, 256, 768], P(('section', 'dp'))
- input_grad: bfloat16 [32, 256, 768], P(('section', 'dp'))
- grad_norm_gain: float32 [4, 768], P('section')
- grad_norm_bias: float32 [4, 768], P('section')
- grad_w_main: float32 [4, 768, 3072], P('section')
- grad_b_main: float32 [4, 3072], P('section')
- grad_section_vector: float32 [4, 768], P('section')
- grad_w_down: float32 [4, 1536, 768], P('section')
The draws below stay inside these ranges and needn't reach their ends.
Inputs may be any that keep to these rules, and one draw needn't show every extreme that they name: `positions`: an image's first kept_counts slots hold its kept patches in raster order, the other slots its dropped patches in raster order; no patch appears twice in an image. `kept_counts`: some image keeps all 256 slots.
All inputs are finite; a program needn't handle non-finite values.
Results may differ from the reference program's by a relative error of at most 0.02.
Values may be sent and summed in bfloat16 or wider, within the bound.
A program may use at most 448 MiB of HBM per device.

```python
import jax
import jax.numpy as jnp
from jax import lax

D = 768
HEADS = 12
HEAD_DIM = 64
FF = 3072
GRID = 16
KEEP_MIN = 32
P_SIZE = 256
IMAGES = 32
N_SECTION = 4


def keep_sets(key):
    count_key, order_key, full_key = jax.random.split(key, 3)
    spread_draw = jax.random.randint(count_key, (IMAGES,), 0, P_SIZE - KEEP_MIN + 1)
    kept_total = P_SIZE - spread_draw * spread_draw // max(P_SIZE - KEEP_MIN, 1)
    chosen = jax.random.randint(full_key, (), 0, IMAGES)
    kept_total = jnp.where(jnp.arange(IMAGES) == chosen, P_SIZE, kept_total).astype(jnp.int32)
    order_keys = jax.random.split(order_key, IMAGES)
    orders = jax.vmap(lambda single_key: jax.random.permutation(single_key, P_SIZE))(order_keys).astype(jnp.int32)
    slot_ids = jnp.arange(P_SIZE, dtype=jnp.int32)[None, :]
    ranked = jnp.where(slot_ids < kept_total[:, None], orders, orders + P_SIZE)
    placed = jnp.sort(ranked, axis=1) % P_SIZE
    return (kept_total, placed)


def draw_positions(key, part):
    kept_total, placed = keep_sets(key)
    return jnp.stack([placed // GRID, placed % GRID], axis=1).astype(jnp.int32)


def draw_kept_counts(key, part):
    kept_total, placed = keep_sets(key)
    return kept_total


def draw_w_main(key, part):
    key = jax.random.fold_in(key, 7)
    standard = jax.random.normal(key, (N_SECTION, D, FF), jnp.float32) * D ** (-0.5)
    column = jnp.arange(FF)[None, None, :]
    section_ids = jnp.arange(N_SECTION)[:, None, None]
    boosted = jnp.where((column >= 3 * D) & (section_ids % 2 == 0), 6.0, 1.0)
    return (standard * boosted).astype(jnp.bfloat16)


def draw_section_vector(key, part):
    key = jax.random.fold_in(key, 13)
    size_key, sign_key, bias_key = jax.random.split(key, 3)
    magnitude = jnp.exp(jax.random.uniform(size_key, (N_SECTION, D), jnp.float32, jnp.log(0.03), jnp.log(1.5)))
    sign_values = jnp.where(jax.random.bernoulli(sign_key, 0.5, (N_SECTION, D)), 1.0, -1.0)
    biases = 0.3 * jax.random.normal(bias_key, (N_SECTION, D), jnp.float32)
    section_ids = jnp.arange(N_SECTION)[:, None]
    return jnp.where(section_ids % 2 == 0, magnitude * sign_values, biases).astype(jnp.float32)


def block_scale(key, shape, cuts, smallest, largest):
    loudness, own = 1.0, jax.random.fold_in(key, 6)
    for position, parts in cuts:
        steps = jnp.exp(jax.random.uniform(jax.random.fold_in(own, position), (parts,), jnp.float32, smallest / len(cuts), largest / len(cuts)))
        loudness = loudness * jnp.repeat(steps, shape[position] // parts).reshape([-1 if axis == position else 1 for axis in range(len(shape))])
    return loudness


def gaussian(own_key, extent, scale, most, cuts=(), held_as=jnp.bfloat16):
    entries = scale * jax.random.normal(own_key, extent, jnp.float32)
    if cuts:
        entries = entries * block_scale(own_key, extent, cuts, -0.22, 0.18)
    return jnp.clip(entries, -most, most).astype(held_as)


def setup_inputs(seed: int = 0) -> dict:
    seeds = jax.random.split(jax.random.key(seed), 11)
    return {
        "patches": gaussian(seeds[0], (IMAGES, P_SIZE, D), 1.0, 6.0, ((0, 32),)),
        "cotangent": gaussian(seeds[1], (IMAGES, P_SIZE, D), 1.0, 6.0, ((0, 32),)),
        "positions": draw_positions(jax.random.fold_in(seeds[10], 71), 0),
        "kept_counts": draw_kept_counts(jax.random.fold_in(seeds[10], 71), 0),
        "norm_gain": jnp.clip(1.0 + 0.1 * jax.random.normal(seeds[4], (N_SECTION, D), jnp.float32), 0.5, 1.5),
        "norm_bias": gaussian(seeds[5], (N_SECTION, D), 0.3, 4.0, ((0, 4),), jnp.float32),
        "w_main": draw_w_main(jax.random.fold_in(seeds[10], 71), 0),
        "b_main": gaussian(seeds[7], (N_SECTION, FF), 0.3, 4.0, ((0, 4),), jnp.float32),
        "section_vector": draw_section_vector(jax.random.fold_in(seeds[10], 71), 0),
        "w_down": gaussian(seeds[9], (N_SECTION, FF // 2, D), FF ** -0.5, 0.109375, ((0, 4),)),
    }


HIGHEST_PRECISION = lax.Precision.HIGHEST
block_images = 16

@jax.custom_vjp
def low(v):
    return lax.optimization_barrier(v.astype(jnp.bfloat16)).astype(jnp.float32)

@jax.custom_vjp
def low_back(v):
    return v

def low_keep(v):
    return (low(v), None)

def low_pass(kept, grad):
    return (grad,)

def back_keep(v):
    return (v, None)

def back_low(kept, grad):
    return (low(grad),)
low.defvjp(low_keep, low_pass)
low_back.defvjp(back_keep, back_low)

def layer_norm(values, norm_scale, norm_offset):
    average = lax.optimization_barrier(jnp.mean(values, axis=-1, keepdims=True))
    centered = values - average
    spread = lax.optimization_barrier(jnp.mean(centered * centered, axis=-1, keepdims=True))
    return centered * lax.rsqrt(spread + 1e-06) * norm_scale + norm_offset

def rotate(tensor, cosine, sine_part):
    half_width = tensor.shape[-1] // 2
    first_half = tensor[..., :half_width]
    second_half = tensor[..., half_width:]
    return jnp.concatenate([first_half * cosine - second_half * sine_part, first_half * sine_part + second_half * cosine], axis=-1)

def attention_section(hidden, valid_mask, grid_rows, grid_cols, norm_scale, norm_offset, matrix, biases, frequency):
    images, slot_count, model_width = hidden.shape
    half_width = HEAD_DIM // 2
    score_scale = HEAD_DIM ** (-0.5)
    normed = low(layer_norm(hidden, norm_scale, norm_offset))
    project = jnp.einsum('gpd,de->gpe', normed, matrix[:, :3 * model_width], precision=HIGHEST_PRECISION) + biases[:3 * model_width]
    project = low_back(project).reshape(images, slot_count, 3, HEADS, HEAD_DIM)
    freq_rows = frequency[:model_width // 2].reshape(HEADS, half_width)
    freq_cols = frequency[model_width // 2:].reshape(HEADS, half_width)
    angles = grid_rows[:, :, None, None] * freq_rows + grid_cols[:, :, None, None] * freq_cols
    cosine = jnp.cos(angles)
    sine_part = jnp.sin(angles)
    query_low = low(rotate(project[:, :, 0], cosine, sine_part))
    key_low = low(rotate(project[:, :, 1], cosine, sine_part))
    value_low = low(project[:, :, 2])
    scores = low_back(jnp.einsum('gqhe,gkhe->ghqk', query_low, key_low, precision=HIGHEST_PRECISION) * score_scale)
    scores = jnp.where(valid_mask[:, None, None, :] > 0.5, scores, -1e+30)
    attn_probs = jax.nn.softmax(scores, axis=-1)
    weights = low(attn_probs)
    context = jnp.einsum('ghqk,gkhe->gqhe', weights, value_low, precision=HIGHEST_PRECISION).reshape(images, slot_count, model_width)
    context = low_back(low(context))
    branch = jnp.einsum('gpd,de->gpe', context, matrix[:, 3 * model_width:], precision=HIGHEST_PRECISION) + biases[3 * model_width:]
    return low_back(low(hidden + valid_mask[..., None] * branch))

def dense_section(hidden, valid_mask, norm_scale, norm_offset, matrix, biases, down_full, down_bias):
    normed = low(layer_norm(hidden, norm_scale, norm_offset))
    pre_gelu = low_back(jnp.einsum('gpd,df->gpf', normed, matrix, precision=HIGHEST_PRECISION) + biases)
    activated = low(jax.nn.gelu(pre_gelu, approximate=False))
    branch = jnp.einsum('gpf,fd->gpd', activated, down_full, precision=HIGHEST_PRECISION) + down_bias
    return low_back(low(hidden + valid_mask[..., None] * branch))

def forward(params, hidden, valid_mask, grid_rows, grid_cols):
    gains, offsets, matrices, vectors, sides, downs = params
    for section_index in range(N_SECTION):
        if section_index % 2 == 0:
            hidden = attention_section(hidden, valid_mask, grid_rows, grid_cols, gains[section_index], offsets[section_index], matrices[section_index], vectors[section_index], sides[section_index])
        else:
            down_full = jnp.concatenate([downs[section_index - 1], downs[section_index]], axis=0)
            hidden = dense_section(hidden, valid_mask, gains[section_index], offsets[section_index], matrices[section_index], vectors[section_index], down_full, sides[section_index])
    return hidden

def reference(patches, cotangent, positions, kept_counts, norm_gain, norm_bias, w_main, b_main, section_vector, w_down):
    params = (norm_gain, norm_bias, w_main.astype(jnp.float32), b_main, section_vector, w_down.astype(jnp.float32))
    groups = IMAGES // block_images

    def regroup(array):
        return array.reshape((groups, block_images) + array.shape[1:])

    def one_block(totals, inputs):
        block_patches, block_cotangent, block_positions, block_counts = inputs
        slot_ids = jnp.arange(P_SIZE, dtype=jnp.int32)
        valid_mask = (slot_ids[None, :] < block_counts[:, None]).astype(jnp.float32)
        grid_rows = block_positions[:, 0, :].astype(jnp.float32)
        grid_cols = block_positions[:, 1, :].astype(jnp.float32)

        def forward_all(weights_all, hidden):
            return forward(weights_all, hidden, valid_mask, grid_rows, grid_cols)
        result, pullback = jax.vjp(forward_all, params, block_patches.astype(jnp.float32))
        gradients, patch_grad = pullback(block_cotangent.astype(jnp.float32))
        totals = jax.tree.map(lambda running, addend: running + addend, totals, gradients)
        return (totals, (result.astype(jnp.bfloat16), patch_grad.astype(jnp.bfloat16)))
    initial = jax.tree.map(jnp.zeros_like, params)
    totals, pieces = lax.scan(one_block, initial, (regroup(patches), regroup(cotangent), regroup(positions), regroup(kept_counts)))
    outputs = pieces[0].reshape(IMAGES, P_SIZE, D)
    input_grad = pieces[1].reshape(IMAGES, P_SIZE, D)
    return (outputs, input_grad, totals[0], totals[1], totals[2], totals[3], totals[4], totals[5])
```

```python
import functools

import jax
import jax.numpy as jnp
from jax import lax
from jax.experimental import pallas as pl
from jax.experimental.pallas import tpu as pltpu
from jax.sharding import PartitionSpec as P

HEADS = 12
HEAD_DIM = 64
GROUP = 256
EPS = 1e-06
MESH = pl.DeviceIdType.MESH
BF = jnp.bfloat16
F32 = jnp.float32
HI = lax.Precision.HIGHEST
LAG_SIB, LAG_ONE, LAG_TWO, LAG_END = 1, 2, 4, 6


def nn(a, b, precision=None):
    return lax.dot_general(a, b, (((1,), (0,)), ((), ())), precision=precision, preferred_element_type=F32)


def nt(a, b, precision=None):
    return lax.dot_general(a, b, (((1,), (1,)), ((), ())), precision=precision, preferred_element_type=F32)


def tn(a, b, precision=None):
    return lax.dot_general(a, b, (((0,), (0,)), ((), ())), precision=precision, preferred_element_type=F32)


def normalise(x):
    centered = x - jnp.mean(x, axis=-1, keepdims=True)
    scale = lax.rsqrt(jnp.mean(centered * centered, axis=-1, keepdims=True) + EPS)
    return centered * scale, scale


def relay(
    n_sec, lines, tokens, width, ff,
    patches, cot, tab, wm, wd, gain, bias, bm, sv,
    o_out, o_ig, o_w, o_d, o_small,
    hin, gin, act, big1, big2, big3, wv, dv, cs, tabs, hout, gout, perm, bqk, freq,
    mine, zin, pin, sib, tmp, sg, sg_sib, sg_one, sg_two,
    w_sem, hin_r, gin_r, tab_r, hop_s, gop_s, ini_s, wd_s, wd_r, out_r, ig_r,
    sib_s, sib_r, low_s, mine_r, za_s, zin_r, pb_s, pin_r, fin_l, fin_s, fin_r, sg_s, sg_r,
):
    s = lax.axis_index("section")
    d = lax.axis_index("dp")
    core = lax.rem(d, 2)
    other = d + 1 - 2 * core
    even = lax.rem(s, 2) == 0
    odd = lax.rem(s, 2) == 1
    last = n_sec - 1
    half = tokens // 2
    n_main = (width // 256) * (ff // width)
    n_low = (ff // 2) // 256
    n_chunk = n_main + n_low
    score_scale = HEAD_DIM ** (-0.5)

    def to_section(target):
        return {"section": target}

    def to_dp(target):
        return {"dp": target}

    def remote(src, dst, send, recv, device):
        return pltpu.make_async_remote_copy(
            src_ref=src, dst_ref=dst, send_sem=send, recv_sem=recv, device_id=device, device_id_type=MESH
        )

    spots = []
    for stride in lines:
        pos = lax.rem(d // stride, 4)
        near = d + (1 - 2 * lax.rem(pos, 2)) * stride
        across = d + (3 - 2 * pos) * stride
        inner = (pos == 1) | (pos == 2)
        outer = (pos == 0) | (pos == 3)
        spots.append((near, across, inner, outer))

    barrier = pltpu.get_barrier_semaphore()
    for step in range(1, n_sec):
        pl.semaphore_signal(barrier, inc=1, device_id=to_section(lax.rem(s + step, n_sec)), device_id_type=MESH)
    pl.semaphore_signal(barrier, inc=1, device_id=to_dp(other), device_id_type=MESH)
    for near, across, inner, outer in spots:
        pl.semaphore_signal(barrier, inc=1, device_id=to_dp(near), device_id_type=MESH)

        @pl.when(inner)
        def _():
            pl.semaphore_signal(barrier, inc=1, device_id=to_dp(across), device_id_type=MESH)

    load_w = pltpu.make_async_copy(wm.at[0], wv, w_sem.at[0])
    load_d = pltpu.make_async_copy(wd.at[0], dv.at[pl.ds(ff // 2, ff // 2)], w_sem.at[1])
    load_w.start()

    @pl.when(odd)
    def _():
        load_d.start()

    peers = n_sec + len(spots)
    for near, across, inner, outer in spots:
        peers = peers + jnp.where(inner, 1, 0)
    pl.semaphore_wait(barrier, peers)

    tab_sends = []
    for step in range(1, n_sec):
        tab_sends.append(
            remote(tab.at[0], tabs.at[s], ini_s.at[step - 1], tab_r.at[s], to_section(lax.rem(s + step, n_sec)))
        )
    for send in tab_sends:
        send.start()
    tab_own = pltpu.make_async_copy(tab.at[0], tabs.at[s], tab_r.at[s])
    tab_own.start()
    patch_send = remote(patches.at[0], hin.at[s], ini_s.at[n_sec], hin_r.at[s], to_section(0))
    patch_own = pltpu.make_async_copy(patches.at[0], hin.at[0], hin_r.at[0])
    cot_send = remote(cot.at[0], gin.at[s], ini_s.at[n_sec + 1], gin_r.at[s], to_section(last))
    cot_own = pltpu.make_async_copy(cot.at[0], gin.at[last], gin_r.at[last])

    @pl.when(s == 0)
    def _():
        patch_own.start()

    @pl.when(s != 0)
    def _():
        patch_send.start()

    @pl.when(s == last)
    def _():
        cot_own.start()

    down_half = (ff // 2) // 2
    mine_rows = pl.ds(pl.multiple_of(core * down_half, down_half), down_half)
    their_rows = pl.ds(pl.multiple_of((1 - core) * down_half, down_half), down_half)
    down_send = remote(
        wd.at[0, mine_rows], dv.at[mine_rows], wd_s.at[0], wd_r.at[0], to_section(lax.rem(s + 1, n_sec))
    )
    down_pass = remote(dv.at[mine_rows], dv.at[mine_rows], wd_s.at[1], wd_r.at[1], to_dp(other))
    down_pass_in = remote(dv.at[their_rows], dv.at[their_rows], wd_s.at[1], wd_r.at[1], to_dp(other))

    @pl.when(even)
    def _():
        down_send.start()

    sg[...] = jnp.zeros_like(sg)
    load_w.wait()

    @pl.when(even)
    def _():
        old = lax.broadcasted_iota(jnp.int32, (GROUP, GROUP), 0)
        new = lax.broadcasted_iota(jnp.int32, (GROUP, GROUP), 1)
        source = ((new & 127) >> 5) * 64 + (new >> 7) * 32 + (new & 31)
        perm[...] = jnp.where(old == source, 1.0, 0.0).astype(BF)
        table = perm[...]
        for block in range(2 * width // GROUP):
            columns = slice(block * GROUP, (block + 1) * GROUP)
            wv[:, columns] = nn(wv[:, columns], table).astype(BF)
            row = jnp.broadcast_to(bm[:, columns], (8, GROUP))
            bqk[:, columns] = nn(row, table.astype(F32), HI)
        freq[...] = jnp.zeros_like(freq)
        freq[0:1, :] = sv[:, : width // 2]
        freq[1:2, :] = sv[:, width // 2 :]

    lane = lax.broadcasted_iota(jnp.int32, (1, GROUP), 1)
    q_masks = [((lane & 127) >> 5) == e for e in range(4)]
    v_masks = [(lane >> 6) == e for e in range(4)]
    zero_low = jnp.zeros((), BF)

    def count_of(i):
        return tabs[i, 2:3, 0:1]

    def row_mask(i):
        ids = lax.broadcasted_iota(jnp.int32, (tokens, 1), 0).astype(F32)
        return jnp.where(ids < count_of(i), 1.0, 0.0)

    def key_mask(i):
        ids = lax.broadcasted_iota(jnp.int32, (1, tokens), 1).astype(F32)
        return ids < count_of(i)

    n_group = width // GROUP
    pairs = width // 2 // n_group

    def attention_forward(i, slot):
        x = hin[i].astype(F32)
        xhat, _ = normalise(x)
        a = (xhat * gain[...] + bias[...]).astype(BF)
        act[i] = a
        angle = nn(jnp.transpose(tabs[i]), freq[...], HI)
        cs[i, 0] = jnp.cos(angle)
        cs[i, 1] = jnp.sin(angle)
        keys_on = key_mask(i)
        for g in range(n_group):
            cosine = cs[i, 0, :, g * pairs : (g + 1) * pairs]
            sine = cs[i, 1, :, g * pairs : (g + 1) * pairs]
            turned = []
            for which in range(2):
                lo = which * width + g * GROUP
                t = nn(a, wv[:, lo : lo + GROUP]) + bqk[0:1, lo : lo + GROUP]
                t1, t2 = t[:, :128], t[:, 128:]
                r = jnp.concatenate([t1 * cosine - t2 * sine, t1 * sine + t2 * cosine], axis=1).astype(BF)
                big1[i, :, lo : lo + GROUP] = r
                turned.append(r)
            lo = 2 * width + g * GROUP
            value = (nn(a, wv[:, lo : lo + GROUP]) + bm[:, lo : lo + GROUP]).astype(BF)
            big1[i, :, lo : lo + GROUP] = value
            query, key = turned
            context = jnp.zeros((tokens, GROUP), F32)
            for e in range(4):
                scores = nt(jnp.where(q_masks[e], query, zero_low), key) * score_scale
                scores = jnp.where(keys_on, scores, -1e30)
                top = jnp.max(scores, axis=-1, keepdims=True)
                p = jnp.exp(scores - top)
                p = (p * (1.0 / jnp.sum(p, axis=-1, keepdims=True))).astype(BF)
                big2[i, :, (4 * g + e) * tokens : (4 * g + e + 1) * tokens] = p
                context = jnp.where(v_masks[e], nn(p, value), context)
            lo = 3 * width + g * GROUP
            big1[i, :, lo : lo + GROUP] = context.astype(BF)
        branch = nn(big1[i, :, 3 * width :], wv[:, 3 * width :]) + bm[:, 3 * width :]
        hout[slot] = (x + row_mask(i) * branch).astype(BF)

    def norm_backward(i, g_up, gact):
        xhat, scale = normalise(hin[i].astype(F32))
        sg[0:1, :] += jnp.sum(gact * xhat, axis=0, keepdims=True)
        sg[1:2, :] += jnp.sum(gact, axis=0, keepdims=True)
        gn = gact * gain[...]
        inside = gn - jnp.mean(gn, axis=-1, keepdims=True) - xhat * jnp.mean(gn * xhat, axis=-1, keepdims=True)
        return g_up + scale * inside

    def attention_backward(i, slot):
        g_up = gin[i].astype(F32)
        gb = row_mask(i) * g_up
        sg[6:7, :] += jnp.sum(gb, axis=0, keepdims=True)
        low = gb.astype(BF)
        dctx_all = nt(low, wv[:, 3 * width :]).astype(BF)
        for g in range(n_group):
            qlo, klo, vlo = g * GROUP, width + g * GROUP, 2 * width + g * GROUP
            query = big1[i, :, qlo : qlo + GROUP]
            key = big1[i, :, klo : klo + GROUP]
            value = big1[i, :, vlo : vlo + GROUP]
            dctx = dctx_all[:, g * GROUP : (g + 1) * GROUP]
            dq = jnp.zeros((tokens, GROUP), F32)
            dk = jnp.zeros((tokens, GROUP), F32)
            dval = jnp.zeros((tokens, GROUP), F32)
            for e in range(4):
                d_e = jnp.where(v_masks[e], dctx, zero_low)
                q_e = jnp.where(q_masks[e], query, zero_low)
                gw = nt(d_e, value)
                p_low = big2[i, :, (4 * g + e) * tokens : (4 * g + e + 1) * tokens]
                p = p_low.astype(F32)
                pg = p * gw
                gs = (pg - p * jnp.sum(pg, axis=-1, keepdims=True)).astype(BF)
                dq = jnp.where(q_masks[e], nn(gs, key), dq)
                dk = dk + tn(gs, q_e)
                dval = dval + tn(p_low, d_e)
            cosine = cs[i, 0, :, g * pairs : (g + 1) * pairs]
            sine = cs[i, 1, :, g * pairs : (g + 1) * pairs]
            turn = jnp.zeros((tokens, pairs), F32)
            for lo, grad, held in ((qlo, dq, query), (klo, dk, key)):
                g1, g2 = grad[:, :128] * score_scale, grad[:, 128:] * score_scale
                r = held.astype(F32)
                turn = turn + g2 * r[:, :128] - g1 * r[:, 128:]
                raw = jnp.concatenate([g1 * cosine + g2 * sine, g2 * cosine - g1 * sine], axis=1).astype(BF)
                big3[i, :, lo : lo + GROUP] = raw
                row = 3 if lo < width else 4
                at = g * GROUP
                sg[row : row + 1, at : at + GROUP] += jnp.sum(raw.astype(F32), axis=0, keepdims=True)
            raw = dval.astype(BF)
            big3[i, :, vlo : vlo + GROUP] = raw
            sg[5:6, g * GROUP : (g + 1) * GROUP] += jnp.sum(raw.astype(F32), axis=0, keepdims=True)
            sums = nn(tabs[i], turn, HI)
            at = g * pairs
            sg[2:3, at : at + pairs] += sums[0:1]
            at = width // 2 + g * pairs
            sg[2:3, at : at + pairs] += sums[1:2]
        gact = nt(big3[i, :, : 3 * width], wv[:, : 3 * width])
        gout[slot] = norm_backward(i, g_up, gact).astype(BF)
        gin[i] = low

    piece = 512

    def dense_forward(i, slot):
        x = hin[i].astype(F32)
        xhat, _ = normalise(x)
        a = (xhat * gain[...] + bias[...]).astype(BF)
        act[i] = a
        for k in range(ff // piece):
            lo = k * piece
            pre = nn(a, wv[:, lo : lo + piece]) + bm[:, lo : lo + piece]
            cdf = 0.5 + 0.5 * lax.erf(pre * (0.5**0.5))
            big1[i, :, lo : lo + piece] = (pre * cdf).astype(BF)
            pdf = jnp.exp(-0.5 * (pre * pre)) * 0.3989422804014327
            big2[i, :, lo : lo + piece] = (cdf + pre * pdf).astype(BF)

        @pl.when(i == 0)
        def _():
            load_d.wait()
            down_send.wait_recv()
            down_pass.start()
            down_pass_in.wait_recv()

        branch = nn(big1[i], dv[...]) + sv[...]
        hout[slot] = (x + row_mask(i) * branch).astype(BF)

    def dense_backward(i, slot):
        g_up = gin[i].astype(F32)
        gb = row_mask(i) * g_up
        sg[2:3, :] += jnp.sum(gb, axis=0, keepdims=True)
        low = gb.astype(BF)
        for k in range(ff // width):
            for m in range(width // GROUP):
                lo = k * width + m * GROUP
                gh = nt(low, dv[lo : lo + GROUP, :])
                gpre = (gh * big2[i, :, lo : lo + GROUP].astype(F32)).astype(BF)
                big3[i, :, lo : lo + GROUP] = gpre
                at = m * GROUP
                sg[3 + k : 4 + k, at : at + GROUP] += jnp.sum(gpre.astype(F32), axis=0, keepdims=True)
        gact = nt(big3[i], wv[...])
        gout[slot] = norm_backward(i, g_up, gact).astype(BF)
        gin[i] = low

    def hop_send(i, slot):
        return remote(hout.at[slot], hin.at[i], hop_s.at[i], hin_r.at[i], to_section(lax.rem(s + 1, n_sec)))

    def result_send(i, slot):
        return remote(hout.at[slot], o_out.at[0], hop_s.at[i], out_r, to_section(i))

    def back_send(i, slot):
        return remote(gout.at[slot], gin.at[i], gop_s.at[i], gin_r.at[i], to_section(lax.rem(s + last, n_sec)))

    def input_send(i, slot):
        return remote(gout.at[slot], o_ig.at[0], gop_s.at[i], ig_r, to_section(i))

    def forward(i):
        slot = lax.rem(i, 2)

        @pl.when(i >= 2)
        def _():
            hop_send(i - 2, slot).wait_send()

        hop_send(i, slot).wait_recv()
        tab_own_like = pltpu.make_async_copy(tab.at[0], tabs.at[i], tab_r.at[i])
        tab_own_like.wait()

        @pl.when(even)
        def _():
            attention_forward(i, slot)

        @pl.when(odd)
        def _():
            dense_forward(i, slot)

        @pl.when(s != last)
        def _():
            hop_send(i, slot).start()

        @pl.when((s == last) & (i != last))
        def _():
            result_send(i, slot).start()

        @pl.when((s == last) & (i == last))
        def _():
            pltpu.make_async_copy(hout.at[slot], o_out.at[0], out_r).start()

    def backward(i):
        slot = lax.rem(i, 2)

        @pl.when((i == 3) | ((i == 2) & (s != 0)))
        def _():
            back_send(i - 2, slot).wait_send()

        @pl.when((i == 2) & (s == 0))
        def _():
            pltpu.make_async_copy(gout.at[slot], o_ig.at[0], ig_r).wait()

        back_send(i, slot).wait_recv()

        @pl.when(even)
        def _():
            attention_backward(i, slot)

        @pl.when(odd)
        def _():
            dense_backward(i, slot)

        @pl.when(s != 0)
        def _():
            back_send(i, slot).start()

        @pl.when((s == 0) & (i != 0))
        def _():
            input_send(i, slot).start()

        @pl.when((s == 0) & (i == 0))
        def _():
            pltpu.make_async_copy(gout.at[slot], o_ig.at[0], ig_r).start()

    def tick(j, carry):
        @pl.when(j < n_sec)
        def _():
            forward(j)

        @pl.when((s != last) & (((s == 0) & (j == 2)) | ((s != 0) & (j == 0))))
        def _():
            cot_send.start()

        b = j - (last - s)

        @pl.when((b >= 0) & (b < n_sec))
        def _():
            backward(b)

        return carry

    lax.fori_loop(0, 2 * n_sec - 1, tick, 0)

    @pl.when(even)
    def _():
        back = perm[...].astype(F32)
        for block in range(2 * width // GROUP):
            row = 3 + block * GROUP // width
            lo = block * GROUP % width
            part = jnp.broadcast_to(sg[row : row + 1, lo : lo + GROUP], (8, GROUP))
            sg[row : row + 1, lo : lo + GROUP] = nt(part, back, HI)[0:1]

    my_half = pl.ds(pl.multiple_of(core * half, half), half)
    their_half = pl.ds(pl.multiple_of((1 - core) * half, half), half)
    shift = jnp.where(odd, n_low, 0)
    steps = n_chunk + n_low + len(lines) * LAG_END + 1

    def flat(ref):
        return ref.reshape(n_sec * tokens, ref.shape[-1])

    def sib_slot(c):
        return jnp.where(c < 0, n_chunk + n_low + c, c)

    def sib_copy(c):
        slot = lax.rem(c + n_low, 2)
        at = sib_slot(c)
        return remote(tmp.at[slot, their_half], sib.at[at], sib_s.at[slot], sib_r.at[at], to_dp(other))

    def low_copy(c):
        at = c + n_low
        return remote(
            sib.at[n_chunk + at], mine.at[n_main + at], low_s.at[at], mine_r.at[at], to_section(lax.rem(s + last, n_sec))
        )

    def make_block(c):
        slot = lax.rem(c + n_low, 2)

        @pl.when((even & (c >= 2)) | (odd & (c >= 2 - n_low)))
        def _():
            sib_copy(c - 2).wait_send()

        column = lax.rem(c, ff // width)
        row = c // (ff // width)
        is_main = (c >= 0) & (c < n_main)
        from_act = is_main & (odd | (column < 3))

        @pl.when(from_act)
        def _():
            rows = pl.ds(pl.multiple_of(row * 256, 256), 256)
            columns = pl.ds(pl.multiple_of(column * width, width), width)
            left = act[:, :, rows].reshape(n_sec * tokens, 256)
            right = big3[:, :, columns].reshape(n_sec * tokens, width)
            tmp[slot] = tn(left, right).astype(BF)

        @pl.when(from_act & even & (column < 2))
        def _():
            back = perm[...]
            for block in range(width // GROUP):
                at = slice(block * GROUP, (block + 1) * GROUP)
                tmp[slot, :, at] = nt(tmp[slot, :, at], back).astype(BF)

        @pl.when(jnp.logical_not(from_act))
        def _():
            down_row = jnp.where(c < 0, (c + n_low) * 256, ff // 2 + (c - n_main) * 256)
            start = jnp.where(even, 3 * width + row * 256, down_row)
            rows = pl.ds(pl.multiple_of(start, 256), 256)
            left = big1[:, :, rows].reshape(n_sec * tokens, 256)
            right = gin[...].reshape(n_sec * tokens, width)
            tmp[slot] = tn(left, right).astype(BF)

        sib_copy(c).start()

    def spot_copies(k, c):
        near, across, inner, outer = spots[k]
        to_near = remote(mine.at[c], zin.at[k, c], za_s.at[k, c], zin_r.at[k, c], to_dp(near))
        to_across = remote(zin.at[k, c], pin.at[k, c], pb_s.at[k, c], pin_r.at[k, c], to_dp(across))
        return to_near, to_across

    def result_place(c):
        return c

    def w_place(c):
        row = c // (ff // width)
        column = lax.rem(c, ff // width)
        rows = pl.ds(pl.multiple_of(row * 256 + core * half, half), half)
        columns = pl.ds(pl.multiple_of(column * width, width), width)
        return o_w.at[rows, columns]

    def d_place(c):
        rows = pl.ds(pl.multiple_of((c - n_main) * 256 + core * half, half), half)
        return o_d.at[rows, :]

    def finish_copies(c, place):
        here = pltpu.make_async_copy(mine.at[c], place, fin_l.at[c])
        there = remote(mine.at[c], place, fin_s.at[c], fin_r.at[c], to_dp(other))
        return here, there

    def finish(c):
        @pl.when(c < n_main)
        def _():
            here, there = finish_copies(c, w_place(c))
            here.start()
            there.start()

        @pl.when(c >= n_main)
        def _():
            here, there = finish_copies(c, d_place(c))
            here.start()
            there.start()

    def sum_step(t, carry):
        c = t - shift

        @pl.when((even & (c < n_main)) | (odd & (c < n_chunk)))
        def _():
            make_block(c)

        c1 = c - LAG_SIB

        @pl.when((even & (c1 >= 0) & (c1 < n_main)) | (odd & (c1 >= -n_low) & (c1 < n_chunk)))
        def _():
            slot = lax.rem(c1 + n_low, 2)
            at = sib_slot(c1)
            sib_copy(c1).wait_recv()
            total = (tmp[slot, my_half].astype(F32) + sib[at].astype(F32)).astype(BF)

            @pl.when(c1 < 0)
            def _():
                sib[at] = total
                low_copy(c1).start()

            @pl.when(c1 >= 0)
            def _():
                mine[c1] = total

        @pl.when(even & (c1 >= n_main) & (c1 < n_chunk))
        def _():
            low_copy(c1 - n_chunk).wait_recv()

        for k in range(len(lines)):
            near, across, inner, outer = spots[k]
            base = LAG_SIB + k * LAG_END
            c0 = c - base

            @pl.when(outer & (c0 >= 0) & (c0 < n_chunk))
            def _():
                to_near, _ = spot_copies(k, c0)
                to_near.start()

            c2 = c - base - LAG_ONE

            @pl.when(inner & (c2 >= 0) & (c2 < n_chunk))
            def _():
                to_near, to_across = spot_copies(k, c2)
                to_near.wait_recv()
                zin[k, c2] = (mine[c2].astype(F32) + zin[k, c2].astype(F32)).astype(BF)
                to_across.start()

            c3 = c - base - LAG_TWO

            @pl.when(inner & (c3 >= 0) & (c3 < n_chunk))
            def _():
                to_near, to_across = spot_copies(k, c3)
                to_across.wait_recv()
                mine[c3] = (zin[k, c3].astype(F32) + pin[k, c3].astype(F32)).astype(BF)
                to_near.start()
                if k == len(lines) - 1:
                    finish(c3)

            c4 = c - base - LAG_END

            @pl.when(outer & (c4 >= 0) & (c4 < n_chunk))
            def _():
                to_near, _ = spot_copies(k, c4)
                to_near.wait()
                mine[c4] = zin[k, c4]
                if k == len(lines) - 1:
                    finish(c4)

        return carry

    small_sib = remote(sg, sg_sib, sg_s.at[0], sg_r.at[0], to_dp(other))
    small_sib.start()
    small_sib.wait()
    sg[...] = sg[...] + sg_sib[...]

    def small_copies(k):
        near, across, inner, outer = spots[k]
        to_near = remote(sg, sg_one.at[k], sg_s.at[1 + 2 * k], sg_r.at[1 + 2 * k], to_dp(near))
        to_across = remote(sg_one.at[k], sg_two.at[k], sg_s.at[2 + 2 * k], sg_r.at[2 + 2 * k], to_dp(across))
        return to_near, to_across

    for k in range(len(lines)):
        near, across, inner, outer = spots[k]
        to_near, to_across = small_copies(k)

        @pl.when(outer)
        def _():
            to_near.start()
            to_near.wait()
            sg[...] = sg_one[k]

        @pl.when(inner)
        def _():
            to_near.wait_recv()
            sg_one[k] = sg[...] + sg_one[k]
            to_across.start()
            to_across.wait()
            sg[...] = sg_one[k] + sg_two[k]
            to_near.start()
            to_near.wait_send()

    o_small[...] = sg[...]

    lax.fori_loop(0, steps, sum_step, 0)

    for send in tab_sends:
        send.wait_send()

    @pl.when(s != 0)
    def _():
        patch_send.wait_send()

    @pl.when(s != last)
    def _():
        cot_send.wait_send()

    @pl.when(even)
    def _():
        down_send.wait_send()
        sib_copy(n_main - 2).wait_send()
        sib_copy(n_main - 1).wait_send()

    @pl.when(odd)
    def _():
        down_pass.wait_send()
        sib_copy(n_chunk - 2).wait_send()
        sib_copy(n_chunk - 1).wait_send()
        for c in range(-n_low, 0):
            low_copy(c).wait_send()

    hop_send(last - 1, (last - 1) % 2).wait_send()
    back_send(last - 1, (last - 1) % 2).wait_send()
    back_send(last, last % 2).wait_send()

    @pl.when(s != last)
    def _():
        hop_send(last, last % 2).wait_send()

    pltpu.make_async_copy(hout.at[0], o_out.at[0], out_r).wait()

    @pl.when(s != 0)
    def _():
        pltpu.make_async_copy(gout.at[0], o_ig.at[0], ig_r).wait()

    for k in range(len(lines)):
        near, across, inner, outer = spots[k]

        @pl.when(inner)
        def _():
            def drain(c, carry):
                to_near, to_across = spot_copies(k, c)
                to_near.wait_send()
                to_across.wait_send()
                return carry

            lax.fori_loop(0, n_chunk, drain, 0)

    def drain_main(c, carry):
        here, there = finish_copies(c, w_place(c))
        here.wait()
        there.wait()
        return carry

    def drain_down(c, carry):
        here, there = finish_copies(c, d_place(c))
        here.wait()
        there.wait()
        return carry

    lax.fori_loop(0, n_main, drain_main, 0)
    lax.fori_loop(n_main, n_chunk, drain_down, 0)


def line_strides(n_dp):
    chips, stride, strides = n_dp // 2, 2, []
    while chips > 1:
        assert chips % 4 == 0
        strides.append(stride)
        stride, chips = stride * 4, chips // 4
    return strides


def on_device(n_sec, n_dp, patches, cot, positions, counts, gain, bias, wm, bm, sv, wd):
    _, tokens, width = patches.shape
    ff = wm.shape[2]
    lines = line_strides(n_dp)
    n_low = (ff // 2) // 256
    n_chunk = (width // 256) * (ff // width) + n_low
    tab = jnp.concatenate(
        [
            positions[0].astype(F32),
            jnp.broadcast_to(counts.astype(F32)[:, None], (1, tokens)),
            jnp.zeros((5, tokens), F32),
        ],
        axis=0,
    )[None]
    any_spec = pl.BlockSpec(memory_space=pl.ANY)
    vmem_spec = pl.BlockSpec(memory_space=pltpu.VMEM)
    image = (n_sec, tokens, width)
    wide = (n_sec, tokens, ff)
    dma = pltpu.SemaphoreType.DMA
    n_line = len(lines)
    scratch = [
        pltpu.VMEM(image, BF),
        pltpu.VMEM(image, BF),
        pltpu.VMEM(image, BF),
        pltpu.VMEM(wide, BF),
        pltpu.VMEM(wide, BF),
        pltpu.VMEM(wide, BF),
        pltpu.VMEM((width, ff), BF),
        pltpu.VMEM((ff, width), BF),
        pltpu.VMEM((n_sec, 2, tokens, width // 2), F32),
        pltpu.VMEM((n_sec, 8, tokens), F32),
        pltpu.VMEM((2, tokens, width), BF),
        pltpu.VMEM((2, tokens, width), BF),
        pltpu.VMEM((GROUP, GROUP), BF),
        pltpu.VMEM((8, 2 * width), F32),
        pltpu.VMEM((8, width // 2), F32),
        pltpu.VMEM((n_chunk, tokens // 2, width), BF),
        pltpu.VMEM((n_line, n_chunk, tokens // 2, width), BF),
        pltpu.VMEM((n_line, n_chunk, tokens // 2, width), BF),
        pltpu.VMEM((n_chunk + n_low, tokens // 2, width), BF),
        pltpu.VMEM((2, tokens, width), BF),
        pltpu.VMEM((8, width), F32),
        pltpu.VMEM((8, width), F32),
        pltpu.VMEM((n_line, 8, width), F32),
        pltpu.VMEM((n_line, 8, width), F32),
        dma((2,)),
        dma((n_sec,)),
        dma((n_sec,)),
        dma((n_sec,)),
        dma((n_sec,)),
        dma((n_sec,)),
        dma((n_sec + 2,)),
        dma((2,)),
        dma((2,)),
        dma,
        dma,
        dma((2,)),
        dma((n_chunk + n_low,)),
        dma((n_low,)),
        dma((n_low,)),
        dma((n_line, n_chunk)),
        dma((n_line, n_chunk)),
        dma((n_line, n_chunk)),
        dma((n_line, n_chunk)),
        dma((n_chunk,)),
        dma((n_chunk,)),
        dma((n_chunk,)),
        dma((1 + 2 * n_line,)),
        dma((1 + 2 * n_line,)),
    ]
    out, ig, gw, gd, small = pl.pallas_call(
        functools.partial(relay, n_sec, lines, tokens, width, ff),
        out_shape=(
            jax.ShapeDtypeStruct((1, tokens, width), BF),
            jax.ShapeDtypeStruct((1, tokens, width), BF),
            jax.ShapeDtypeStruct((width, ff), BF),
            jax.ShapeDtypeStruct((ff // 2, width), BF),
            jax.ShapeDtypeStruct((8, width), F32),
        ),
        in_specs=[any_spec, any_spec, vmem_spec, any_spec, any_spec] + [vmem_spec] * 4,
        out_specs=(any_spec, any_spec, any_spec, any_spec, vmem_spec),
        scratch_shapes=scratch,
        compiler_params=pltpu.CompilerParams(
            collective_id=0, has_side_effects=True, vmem_limit_bytes=63 * 2**20
        ),
    )(patches, cot, tab, wm, wd, gain, bias, bm, sv)
    return (
        out,
        ig,
        small[0:1],
        small[1:2],
        gw.astype(F32)[None],
        small[3:7].reshape(1, ff),
        small[2:3],
        gd.astype(F32)[None],
    )


def solution(mesh):
    n_sec, n_dp = mesh.shape["section"], mesh.shape["dp"]
    images = P(("section", "dp"), None, None)
    row = P("section", None)
    block = P("section", None, None)
    return jax.shard_map(
        functools.partial(on_device, n_sec, n_dp),
        mesh=mesh,
        in_specs=(images, images, images, P(("section", "dp")), row, row, block, row, row, block),
        out_specs=(images, images, row, row, block, row, row, block),
        check_vma=False,
    )
```

```python
import functools

import jax
import jax.numpy as jnp
from jax import lax
from jax.experimental import pallas as pl
from jax.experimental.pallas import tpu as pltpu
from jax.sharding import PartitionSpec as P

HEADS = 12
HEAD_DIM = 64
GROUP = 256
EPS = 1e-06
MESH = pl.DeviceIdType.MESH
BF = jnp.bfloat16
F32 = jnp.float32
HI = lax.Precision.HIGHEST
LAG_SIB, LAG_ONE, LAG_TWO, LAG_END = 1, 3, 6, 9
N_SUB = 2


def nn(a, b, precision=None):
    return lax.dot_general(a, b, (((1,), (0,)), ((), ())), precision=precision, preferred_element_type=F32)


def nt(a, b, precision=None):
    return lax.dot_general(a, b, (((1,), (1,)), ((), ())), precision=precision, preferred_element_type=F32)


def tn(a, b, precision=None):
    return lax.dot_general(a, b, (((0,), (0,)), ((), ())), precision=precision, preferred_element_type=F32)


def normalise(x):
    centered = x - jnp.mean(x, axis=-1, keepdims=True)
    scale = lax.rsqrt(jnp.mean(centered * centered, axis=-1, keepdims=True) + EPS)
    return centered * scale, scale


def relay(
    n_sec, lines, tokens, width, ff,
    patches, cot, tab, wm, wd, gain, bias, bm, sv,
    o_out, o_ig, o_w, o_d, o_small,
    hin, gin, act, big1, big2, big3, wv, dv, cs, tabs, hout, gout, perm, bqk, freq,
    mine, zin, pin, sib, tmp, sg, sg_sib, sg_one, sg_two,
    w_sem, hin_r, gin_r, tab_r, hop_s, gop_s, ini_s, cot_r, wd_s, wd_r, out_r, ig_r,
    sib_s, sib_r, low_s, mine_r, za_s, zin_r, pb_s, pin_r, fin_l, fin_s, fin_r, sg_s, sg_r,
):
    s = lax.axis_index("section")
    d = lax.axis_index("dp")
    core = lax.rem(d, 2)
    other = d + 1 - 2 * core
    even = lax.rem(s, 2) == 0
    odd = lax.rem(s, 2) == 1
    last = n_sec - 1
    half = tokens // 2
    n_main = (width // 256) * (ff // width)
    n_low = (ff // 2) // 256
    n_chunk = n_main + n_low
    n_sub = N_SUB
    score_scale = HEAD_DIM ** (-0.5)

    def to_section(target):
        return {"section": target}

    def to_dp(target):
        return {"dp": target}

    def remote(src, dst, send, recv, device):
        return pltpu.make_async_remote_copy(
            src_ref=src, dst_ref=dst, send_sem=send, recv_sem=recv, device_id=device, device_id_type=MESH
        )

    spots = []
    for stride in lines:
        pos = lax.rem(d // stride, 4)
        near = d + (1 - 2 * lax.rem(pos, 2)) * stride
        across = d + (3 - 2 * pos) * stride
        inner = (pos == 1) | (pos == 2)
        outer = (pos == 0) | (pos == 3)
        spots.append((near, across, inner, outer))

    barrier = pltpu.get_barrier_semaphore()
    for step in range(1, n_sec):
        pl.semaphore_signal(barrier, inc=1, device_id=to_section(lax.rem(s + step, n_sec)), device_id_type=MESH)
    pl.semaphore_signal(barrier, inc=1, device_id=to_dp(other), device_id_type=MESH)
    for near, across, inner, outer in spots:
        pl.semaphore_signal(barrier, inc=1, device_id=to_dp(near), device_id_type=MESH)

        @pl.when(inner)
        def _():
            pl.semaphore_signal(barrier, inc=1, device_id=to_dp(across), device_id_type=MESH)

    load_w = pltpu.make_async_copy(wm.at[0], wv, w_sem.at[0])
    load_d = pltpu.make_async_copy(wd.at[0], dv.at[pl.ds(ff // 2, ff // 2)], w_sem.at[1])
    load_w.start()

    @pl.when(odd)
    def _():
        load_d.start()

    peers = n_sec + len(spots)
    for near, across, inner, outer in spots:
        peers = peers + jnp.where(inner, 1, 0)
    pl.semaphore_wait(barrier, peers)

    tab_sends = []
    for step in range(1, n_sec):
        tab_sends.append(
            remote(tab.at[0], tabs.at[s], ini_s.at[step - 1], tab_r.at[s], to_section(lax.rem(s + step, n_sec)))
        )
    for send in tab_sends:
        send.start()
    tab_own = pltpu.make_async_copy(tab.at[0], tabs.at[s], tab_r.at[s])
    tab_own.start()
    patch_send = remote(patches.at[0], hin.at[s], ini_s.at[n_sec], hin_r.at[s], to_section(0))
    patch_own = pltpu.make_async_copy(patches.at[0], hin.at[0], hin_r.at[0])
    cot_send = remote(cot.at[0], gin.at[s], ini_s.at[n_sec + 1], gin_r.at[s], to_section(last))
    cot_own = pltpu.make_async_copy(cot.at[0], gin.at[last], gin_r.at[last])
    cot_out = remote(cot.at[0], gout.at[0], ini_s.at[n_sec + 1], cot_r, to_section(last - 1))
    cot_on = remote(gout.at[0], gin.at[0], ini_s.at[n_sec + 2], gin_r.at[0], to_section(last))

    @pl.when(s == 0)
    def _():
        patch_own.start()
        cot_out.start()

    @pl.when(s != 0)
    def _():
        patch_send.start()

    @pl.when((s != 0) & (s != last))
    def _():
        cot_send.start()

    @pl.when(s == last)
    def _():
        cot_own.start()

    near0 = spots[0][0]
    side = lax.rem(d // lines[0], 2)
    n_part = 4
    part = (ff // 2) // 4 // n_part

    def down_rows(which_side, which_core, k):
        start = (which_side * 2 + which_core) * (n_part * part) + k * part
        return pl.ds(pl.multiple_of(start, part), part)

    def down_send(k):
        rows = down_rows(side, core, k)
        return remote(wd.at[0, rows], dv.at[rows], wd_s.at[0, k], wd_r.at[0, k], to_section(lax.rem(s + 1, n_sec)))

    def down_near(k):
        rows = down_rows(side, core, k)
        return remote(dv.at[rows], dv.at[rows], wd_s.at[1, k], wd_r.at[1, k], to_dp(near0))

    def down_pass(k):
        rows = down_rows(side, core, k)
        return remote(dv.at[rows], dv.at[rows], wd_s.at[2, k], wd_r.at[2, k], to_dp(other))

    def down_pass_far(k):
        rows = down_rows(1 - side, core, k)
        return remote(dv.at[rows], dv.at[rows], wd_s.at[3, k], wd_r.at[3, k], to_dp(other))

    @pl.when(even)
    def _():
        for k in range(n_part):
            down_send(k).start()

    def table(i):
        pltpu.make_async_copy(tab.at[0], tabs.at[i], tab_r.at[i]).wait()
        angle = nn(jnp.transpose(tabs[i]), freq[...], HI)
        cs[i, 0] = jnp.cos(angle)
        cs[i, 1] = jnp.sin(angle)

    ahead = (s == 0) & (core == 0)

    @pl.when(even)
    def _():
        freq[...] = jnp.zeros_like(freq)
        freq[0:1, :] = sv[:, : width // 2]
        freq[1:2, :] = sv[:, width // 2 :]

        def early(i, carry):
            @pl.when((i == 0) | jnp.logical_not(ahead))
            def _():
                table(i)

            return carry

        lax.fori_loop(0, n_sec, early, 0)

    @pl.when(odd)
    def _():
        for i in range(n_sec):
            pltpu.make_async_copy(tab.at[0], tabs.at[i], tab_r.at[i]).wait()

    sg[...] = jnp.zeros_like(sg)
    load_w.wait()

    @pl.when(even)
    def _():
        old = lax.broadcasted_iota(jnp.int32, (GROUP, GROUP), 0)
        new = lax.broadcasted_iota(jnp.int32, (GROUP, GROUP), 1)
        source = ((new & 127) >> 5) * 64 + (new >> 7) * 32 + (new & 31)
        perm[...] = jnp.where(old == source, 1.0, 0.0).astype(BF)
        table = perm[...]
        for block in range(2 * width // GROUP):
            columns = slice(block * GROUP, (block + 1) * GROUP)
            wv[:, columns] = nn(wv[:, columns], table).astype(BF)
            row = jnp.broadcast_to(bm[:, columns], (8, GROUP))
            bqk[:, columns] = nn(row, table.astype(F32), HI)

    @pl.when(s == last - 1)
    def _():
        cot_out.wait_recv()
        cot_on.start()

    @pl.when(odd)
    def _():
        for k in range(n_part):
            down_send(k).wait_recv()
            down_near(k).start()
            down_pass(k).start()

    lane = lax.broadcasted_iota(jnp.int32, (1, GROUP), 1)
    q_masks = [((lane & 127) >> 5) == e for e in range(4)]
    v_masks = [(lane >> 6) == e for e in range(4)]
    zero_low = jnp.zeros((), BF)

    def count_of(i):
        return tabs[i, 2:3, 0:1]

    def row_mask(i):
        ids = lax.broadcasted_iota(jnp.int32, (tokens, 1), 0).astype(F32)
        return jnp.where(ids < count_of(i), 1.0, 0.0)

    def key_mask(i):
        ids = lax.broadcasted_iota(jnp.int32, (1, tokens), 1).astype(F32)
        return ids < count_of(i)

    n_group = width // GROUP
    pairs = width // 2 // n_group

    def attention_forward(i, slot):
        x = hin[i].astype(F32)
        xhat, _ = normalise(x)
        a = (xhat * gain[...] + bias[...]).astype(BF)
        act[i] = a
        keys_on = key_mask(i)
        for g in range(n_group):
            cosine = cs[i, 0, :, g * pairs : (g + 1) * pairs]
            sine = cs[i, 1, :, g * pairs : (g + 1) * pairs]
            turned = []
            for which in range(2):
                lo = which * width + g * GROUP
                t = nn(a, wv[:, lo : lo + GROUP]) + bqk[0:1, lo : lo + GROUP]
                t1, t2 = t[:, :128], t[:, 128:]
                r = jnp.concatenate([t1 * cosine - t2 * sine, t1 * sine + t2 * cosine], axis=1).astype(BF)
                big1[i, :, lo : lo + GROUP] = r
                turned.append(r)
            lo = 2 * width + g * GROUP
            value = (nn(a, wv[:, lo : lo + GROUP]) + bm[:, lo : lo + GROUP]).astype(BF)
            big1[i, :, lo : lo + GROUP] = value
            query, key = turned
            context = jnp.zeros((tokens, GROUP), F32)
            for e in range(4):
                scores = nt(jnp.where(q_masks[e], query, zero_low), key) * score_scale
                scores = jnp.where(keys_on, scores, -1e30)
                top = jnp.max(scores, axis=-1, keepdims=True)
                p = jnp.exp(scores - top)
                p = (p * (1.0 / jnp.sum(p, axis=-1, keepdims=True))).astype(BF)
                big2[i, :, (4 * g + e) * tokens : (4 * g + e + 1) * tokens] = p
                context = jnp.where(v_masks[e], nn(p, value), context)
            lo = 3 * width + g * GROUP
            big1[i, :, lo : lo + GROUP] = context.astype(BF)
        branch = nn(big1[i, :, 3 * width :], wv[:, 3 * width :]) + bm[:, 3 * width :]
        hout[slot] = (x + row_mask(i) * branch).astype(BF)

    def norm_backward(i, g_up, gact):
        xhat, scale = normalise(hin[i].astype(F32))
        sg[0:1, :] += jnp.sum(gact * xhat, axis=0, keepdims=True)
        sg[1:2, :] += jnp.sum(gact, axis=0, keepdims=True)
        gn = gact * gain[...]
        inside = gn - jnp.mean(gn, axis=-1, keepdims=True) - xhat * jnp.mean(gn * xhat, axis=-1, keepdims=True)
        return g_up + scale * inside

    def attention_backward(i, slot):
        g_up = gin[i].astype(F32)
        gb = row_mask(i) * g_up
        sg[6:7, :] += jnp.sum(gb, axis=0, keepdims=True)
        low = gb.astype(BF)
        dctx_all = nt(low, wv[:, 3 * width :]).astype(BF)
        for g in range(n_group):
            qlo, klo, vlo = g * GROUP, width + g * GROUP, 2 * width + g * GROUP
            query = big1[i, :, qlo : qlo + GROUP]
            key = big1[i, :, klo : klo + GROUP]
            value = big1[i, :, vlo : vlo + GROUP]
            dctx = dctx_all[:, g * GROUP : (g + 1) * GROUP]
            dq = jnp.zeros((tokens, GROUP), F32)
            dk = jnp.zeros((tokens, GROUP), F32)
            dval = jnp.zeros((tokens, GROUP), F32)
            for e in range(4):
                d_e = jnp.where(v_masks[e], dctx, zero_low)
                q_e = jnp.where(q_masks[e], query, zero_low)
                gw = nt(d_e, value)
                p_low = big2[i, :, (4 * g + e) * tokens : (4 * g + e + 1) * tokens]
                p = p_low.astype(F32)
                pg = p * gw
                gs = (pg - p * jnp.sum(pg, axis=-1, keepdims=True)).astype(BF)
                dq = jnp.where(q_masks[e], nn(gs, key), dq)
                dk = dk + tn(gs, q_e)
                dval = dval + tn(p_low, d_e)
            cosine = cs[i, 0, :, g * pairs : (g + 1) * pairs]
            sine = cs[i, 1, :, g * pairs : (g + 1) * pairs]
            turn = jnp.zeros((tokens, pairs), F32)
            for lo, grad, held in ((qlo, dq, query), (klo, dk, key)):
                g1, g2 = grad[:, :128] * score_scale, grad[:, 128:] * score_scale
                r = held.astype(F32)
                turn = turn + g2 * r[:, :128] - g1 * r[:, 128:]
                raw = jnp.concatenate([g1 * cosine + g2 * sine, g2 * cosine - g1 * sine], axis=1).astype(BF)
                big3[i, :, lo : lo + GROUP] = raw
                row = 3 if lo < width else 4
                at = g * GROUP
                sg[row : row + 1, at : at + GROUP] += jnp.sum(raw.astype(F32), axis=0, keepdims=True)
            raw = dval.astype(BF)
            big3[i, :, vlo : vlo + GROUP] = raw
            sg[5:6, g * GROUP : (g + 1) * GROUP] += jnp.sum(raw.astype(F32), axis=0, keepdims=True)
            sums = nn(tabs[i], turn, HI)
            at = g * pairs
            sg[2:3, at : at + pairs] += sums[0:1]
            at = width // 2 + g * pairs
            sg[2:3, at : at + pairs] += sums[1:2]
        gact = nt(big3[i, :, : 3 * width], wv[:, : 3 * width])
        gout[slot] = norm_backward(i, g_up, gact).astype(BF)
        gin[i] = low

    piece = 512

    def dense_forward(i, slot):
        x = hin[i].astype(F32)
        xhat, _ = normalise(x)
        a = (xhat * gain[...] + bias[...]).astype(BF)
        act[i] = a
        for k in range(ff // piece):
            lo = k * piece
            pre = nn(a, wv[:, lo : lo + piece]) + bm[:, lo : lo + piece]
            cdf = 0.5 + 0.5 * lax.erf(pre * (0.5**0.5))
            big1[i, :, lo : lo + piece] = (pre * cdf).astype(BF)
            pdf = jnp.exp(-0.5 * (pre * pre)) * 0.3989422804014327
            big2[i, :, lo : lo + piece] = (cdf + pre * pdf).astype(BF)

        @pl.when(i == 0)
        def _():
            load_d.wait()
            for k in range(n_part):
                down_near(k).wait_recv()
                down_pass_far(k).start()
            for k in range(n_part):
                down_pass(k).wait_recv()
                down_pass_far(k).wait_recv()

        branch = nn(big1[i], dv[...]) + sv[...]
        hout[slot] = (x + row_mask(i) * branch).astype(BF)

    def dense_backward(i, slot):
        g_up = gin[i].astype(F32)
        gb = row_mask(i) * g_up
        sg[2:3, :] += jnp.sum(gb, axis=0, keepdims=True)
        low = gb.astype(BF)
        for k in range(ff // width):
            for m in range(width // GROUP):
                lo = k * width + m * GROUP
                gh = nt(low, dv[lo : lo + GROUP, :])
                gpre = (gh * big2[i, :, lo : lo + GROUP].astype(F32)).astype(BF)
                big3[i, :, lo : lo + GROUP] = gpre
                at = m * GROUP
                sg[3 + k : 4 + k, at : at + GROUP] += jnp.sum(gpre.astype(F32), axis=0, keepdims=True)
        gact = nt(big3[i], wv[...])
        gout[slot] = norm_backward(i, g_up, gact).astype(BF)
        gin[i] = low

    def hop_send(i, slot):
        return remote(hout.at[slot], hin.at[i], hop_s.at[i], hin_r.at[i], to_section(lax.rem(s + 1, n_sec)))

    def result_send(i, slot):
        return remote(hout.at[slot], o_out.at[0], hop_s.at[i], out_r, to_section(i))

    def back_send(i, slot):
        return remote(gout.at[slot], gin.at[i], gop_s.at[i], gin_r.at[i], to_section(lax.rem(s + last, n_sec)))

    def input_send(i, slot):
        return remote(gout.at[slot], o_ig.at[0], gop_s.at[i], ig_r, to_section(i))

    def forward(i):
        hop_send(i, i).wait_recv()

        @pl.when(even)
        def _():
            attention_forward(i, i)

        @pl.when(odd)
        def _():
            dense_forward(i, i)

        @pl.when((s != last) & (i >= 1))
        def _():
            hop_send(i - 1, i - 1).wait_send()

        @pl.when(s != last)
        def _():
            hop_send(i, i).start()

    def backward(i):
        slot = lax.rem(i, 2)

        @pl.when((i == 0) & (s == last - 1))
        def _():
            cot_on.wait_send()

        @pl.when((i == 2) & (s == 0))
        def _():
            pltpu.make_async_copy(gout.at[slot], o_ig.at[0], ig_r).wait()

        back_send(i, slot).wait_recv()

        @pl.when(even)
        def _():
            attention_backward(i, slot)

        @pl.when(odd)
        def _():
            dense_backward(i, slot)

        @pl.when((i >= 2) | ((i == 1) & (s != 0)))
        def _():
            back_send(i - 1, 1 - slot).wait_send()

        @pl.when(s != 0)
        def _():
            back_send(i, slot).start()

        @pl.when((s == 0) & (i != 0))
        def _():
            input_send(i, slot).start()

        @pl.when((s == 0) & (i == 0))
        def _():
            pltpu.make_async_copy(gout.at[slot], o_ig.at[0], ig_r).start()

    def tick(j, carry):
        is_forward = jnp.where(s == last, lax.rem(j, 2) == 0, j < n_sec)
        i = jnp.where(s == last, j // 2, lax.rem(j, n_sec))

        @pl.when(is_forward)
        def _():
            forward(i)

        @pl.when(ahead & (j == 0))
        def _():
            lax.fori_loop(1, n_sec, lambda i, carry: (table(i), carry)[1], 0)

        @pl.when(jnp.logical_not(is_forward))
        def _():
            backward(i)

        return carry

    lax.fori_loop(0, 2 * n_sec, tick, 0)

    @pl.when(s == last)
    def _():
        for i in range(last):
            result_send(i, i).start()
        pltpu.make_async_copy(hout.at[last], o_out.at[0], out_r).start()

    @pl.when(even)
    def _():
        back = perm[...].astype(F32)
        for block in range(2 * width // GROUP):
            row = 3 + block * GROUP // width
            lo = block * GROUP % width
            part = jnp.broadcast_to(sg[row : row + 1, lo : lo + GROUP], (8, GROUP))
            sg[row : row + 1, lo : lo + GROUP] = nt(part, back, HI)[0:1]

    my_half = pl.ds(core * n_sub, n_sub)
    their_half = pl.ds((1 - core) * n_sub, n_sub)
    shift = jnp.where(odd, n_low, 0)

    def sib_slot(c):
        return jnp.where(c < 0, n_chunk + n_low + c, c)

    def sib_copy(c):
        slot = lax.rem(c + n_low, 2)
        at = sib_slot(c)
        return remote(tmp.at[slot, their_half], sib.at[at], sib_s.at[slot], sib_r.at[at], to_dp(other))

    def low_copy(c):
        at = c + n_low
        return remote(
            sib.at[n_chunk + at],
            mine.at[pl.ds((n_main + at) * n_sub, n_sub)],
            low_s.at[at],
            mine_r.at[at],
            to_section(lax.rem(s + last, n_sec)),
        )

    def make_block(c):
        slot = lax.rem(c + n_low, 2)

        @pl.when((even & (c >= 2)) | (odd & (c >= 2 - n_low)))
        def _():
            sib_copy(c - 2).wait_send()

        column = lax.rem(c, ff // width)
        row = c // (ff // width)
        is_main = (c >= 0) & (c < n_main)
        from_act = is_main & (odd | (column < 3))

        def keep(block):
            tmp[slot] = block.astype(BF).reshape(2 * n_sub, half // n_sub, width)

        @pl.when(from_act)
        def _():
            rows = pl.ds(pl.multiple_of(row * 256, 256), 256)
            columns = pl.ds(pl.multiple_of(column * width, width), width)
            left = act[:, :, rows].reshape(n_sec * tokens, 256)
            right = big3[:, :, columns].reshape(n_sec * tokens, width)
            keep(tn(left, right))

        @pl.when(from_act & even & (column < 2))
        def _():
            back = perm[...]
            held = tmp[slot].reshape(2 * half, width)
            keep(
                jnp.concatenate(
                    [nt(held[:, k * GROUP : (k + 1) * GROUP], back) for k in range(width // GROUP)], axis=1
                )
            )

        @pl.when(jnp.logical_not(from_act))
        def _():
            down_row = jnp.where(c < 0, (c + n_low) * 256, ff // 2 + (c - n_main) * 256)
            start = jnp.where(even, 3 * width + row * 256, down_row)
            rows = pl.ds(pl.multiple_of(start, 256), 256)
            left = big1[:, :, rows].reshape(n_sec * tokens, 256)
            right = gin[...].reshape(n_sec * tokens, width)
            keep(tn(left, right))

        sib_copy(c).start()

    def spot_copies(k, u):
        near, across, inner, outer = spots[k]
        to_near = remote(mine.at[u], zin.at[k, u], za_s.at[k, u], zin_r.at[k, u], to_dp(near))
        to_across = remote(zin.at[k, u], pin.at[k, u], pb_s.at[k, u], pin_r.at[k, u], to_dp(across))
        return to_near, to_across

    piece_rows = half // n_sub

    def w_place(u):
        c = u // n_sub
        row = c // (ff // width)
        column = lax.rem(c, ff // width)
        start = row * 256 + core * half + lax.rem(u, n_sub) * piece_rows
        rows = pl.ds(pl.multiple_of(start, piece_rows), piece_rows)
        columns = pl.ds(pl.multiple_of(column * width, width), width)
        return o_w.at[rows, columns]

    def d_place(u):
        c = u // n_sub
        start = (c - n_main) * 256 + core * half + lax.rem(u, n_sub) * piece_rows
        return o_d.at[pl.ds(pl.multiple_of(start, piece_rows), piece_rows), :]

    def finish_copies(u, place):
        here = pltpu.make_async_copy(mine.at[u], place, fin_l.at[u])
        there = remote(mine.at[u], place, fin_s.at[u], fin_r.at[u], to_dp(other))
        return here, there

    def finish(u):
        @pl.when(u < n_main * n_sub)
        def _():
            here, there = finish_copies(u, w_place(u))
            here.start()
            there.start()

        @pl.when(u >= n_main * n_sub)
        def _():
            here, there = finish_copies(u, d_place(u))
            here.start()
            there.start()

    small_sib = remote(sg, sg_sib, sg_s.at[0], sg_r.at[0], to_dp(other))

    def small_copies(k):
        near, across, inner, outer = spots[k]
        to_near = remote(sg, sg_one.at[k], sg_s.at[1 + 2 * k], sg_r.at[1 + 2 * k], to_dp(near))
        to_across = remote(sg_one.at[k], sg_two.at[k], sg_s.at[2 + 2 * k], sg_r.at[2 + 2 * k], to_dp(across))
        return to_near, to_across

    n_unit = n_chunk * n_sub
    steps = n_unit + n_low * n_sub + n_sub * LAG_SIB + len(lines) * LAG_END + 1

    def sum_step(t, carry):
        v = t - shift * n_sub
        c = v // n_sub

        @pl.when((lax.rem(t, n_sub) == 0) & ((even & (c < n_main)) | (odd & (c < n_chunk))))
        def _():
            make_block(t // n_sub - shift)

        c1 = t // n_sub - shift - LAG_SIB
        first = lax.rem(t, n_sub) == 0

        @pl.when(first & ((even & (c1 >= 0) & (c1 < n_main)) | (odd & (c1 >= -n_low) & (c1 < n_chunk))))
        def _():
            slot = lax.rem(c1 + n_low, 2)
            at = sib_slot(c1)
            sib_copy(c1).wait_recv()
            total = (tmp[slot, my_half].astype(F32) + sib[at].astype(F32)).astype(BF)

            @pl.when(c1 < 0)
            def _():
                sib[at] = total
                low_copy(c1).start()

            @pl.when(c1 >= 0)
            def _():
                mine[pl.ds(c1 * n_sub, n_sub)] = total

        @pl.when(first & even & (c1 >= n_main) & (c1 < n_chunk))
        def _():
            low_copy(c1 - n_chunk).wait_recv()

        @pl.when(t == 0)
        def _():
            small_sib.start()

        @pl.when(t == 2)
        def _():
            small_sib.wait()
            sg[...] = sg[...] + sg_sib[...]

        for k in range(len(lines)):
            near, across, inner, outer = spots[k]
            small_near, small_across = small_copies(k)
            at = 2 + 9 * k

            @pl.when(outer & (t == at))
            def _():
                small_near.start()

            @pl.when(inner & (t == at + 3))
            def _():
                small_near.wait_recv()
                sg_one[k] = sg[...] + sg_one[k]
                small_across.start()

            @pl.when(inner & (t == at + 6))
            def _():
                small_across.wait()
                sg[...] = sg_one[k] + sg_two[k]
                small_near.start()
                small_near.wait_send()

            @pl.when(outer & (t == at + 9))
            def _():
                small_near.wait()
                sg[...] = sg_one[k]

        for k in range(len(lines)):
            near, across, inner, outer = spots[k]
            base = LAG_SIB * n_sub + k * LAG_END
            u0 = v - base

            @pl.when(outer & (u0 >= 0) & (u0 < n_unit))
            def _():
                to_near, _ = spot_copies(k, u0)
                to_near.start()

            u2 = v - base - LAG_ONE

            @pl.when(inner & (u2 >= 0) & (u2 < n_unit))
            def _():
                to_near, to_across = spot_copies(k, u2)
                to_near.wait_recv()
                zin[k, u2] = (mine[u2].astype(F32) + zin[k, u2].astype(F32)).astype(BF)
                to_across.start()

            u3 = v - base - LAG_TWO

            @pl.when(inner & (u3 >= 0) & (u3 < n_unit))
            def _():
                to_near, to_across = spot_copies(k, u3)
                to_across.wait_recv()
                mine[u3] = (zin[k, u3].astype(F32) + pin[k, u3].astype(F32)).astype(BF)
                to_near.start()
                if k == len(lines) - 1:
                    finish(u3)

            u4 = v - base - LAG_END

            @pl.when(outer & (u4 >= 0) & (u4 < n_unit))
            def _():
                to_near, _ = spot_copies(k, u4)
                to_near.wait()
                mine[u4] = zin[k, u4]
                if k == len(lines) - 1:
                    finish(u4)

        return carry

    lax.fori_loop(0, steps, sum_step, 0)
    o_small[...] = sg[...]

    for send in tab_sends:
        send.wait_send()

    @pl.when(s != 0)
    def _():
        patch_send.wait_send()

    @pl.when(s != last)
    def _():
        cot_send.wait_send()

    @pl.when(even)
    def _():
        for k in range(n_part):
            down_send(k).wait_send()
        sib_copy(n_main - 2).wait_send()
        sib_copy(n_main - 1).wait_send()

    @pl.when(odd)
    def _():
        for k in range(n_part):
            down_near(k).wait_send()
            down_pass(k).wait_send()
            down_pass_far(k).wait_send()
        sib_copy(n_chunk - 2).wait_send()
        sib_copy(n_chunk - 1).wait_send()
        for c in range(-n_low, 0):
            low_copy(c).wait_send()

    back_send(last, last % 2).wait_send()

    @pl.when(s != last)
    def _():
        hop_send(last, last).wait_send()

    @pl.when(s == last)
    def _():
        for i in range(last):
            result_send(i, i).wait_send()

    pltpu.make_async_copy(hout.at[0], o_out.at[0], out_r).wait()

    @pl.when(s != 0)
    def _():
        pltpu.make_async_copy(gout.at[0], o_ig.at[0], ig_r).wait()

    for k in range(len(lines)):
        near, across, inner, outer = spots[k]

        @pl.when(inner)
        def _():
            def drain(u, carry):
                to_near, to_across = spot_copies(k, u)
                to_near.wait_send()
                to_across.wait_send()
                return carry

            lax.fori_loop(0, n_unit, drain, 0)

    def drain_main(u, carry):
        here, there = finish_copies(u, w_place(u))
        here.wait()
        there.wait()
        return carry

    def drain_down(u, carry):
        here, there = finish_copies(u, d_place(u))
        here.wait()
        there.wait()
        return carry

    lax.fori_loop(0, n_main * n_sub, drain_main, 0)
    lax.fori_loop(n_main * n_sub, n_unit, drain_down, 0)


def line_strides(n_dp):
    chips, stride, strides = n_dp // 2, 2, []
    while chips > 1:
        assert chips % 4 == 0
        strides.append(stride)
        stride, chips = stride * 4, chips // 4
    return strides


def on_device(n_sec, n_dp, patches, cot, positions, counts, gain, bias, wm, bm, sv, wd):
    _, tokens, width = patches.shape
    ff = wm.shape[2]
    lines = line_strides(n_dp)
    n_low = (ff // 2) // 256
    n_chunk = (width // 256) * (ff // width) + n_low
    n_unit, rows = n_chunk * N_SUB, 128 // N_SUB
    tab = jnp.concatenate(
        [
            positions[0].astype(F32),
            jnp.broadcast_to(counts.astype(F32)[:, None], (1, tokens)),
            jnp.zeros((5, tokens), F32),
        ],
        axis=0,
    )[None]
    any_spec = pl.BlockSpec(memory_space=pl.ANY)
    vmem_spec = pl.BlockSpec(memory_space=pltpu.VMEM)
    image = (n_sec, tokens, width)
    wide = (n_sec, tokens, ff)
    dma = pltpu.SemaphoreType.DMA
    n_line = len(lines)
    scratch = [
        pltpu.VMEM(image, BF),
        pltpu.VMEM(image, BF),
        pltpu.VMEM(image, BF),
        pltpu.VMEM(wide, BF),
        pltpu.VMEM(wide, BF),
        pltpu.VMEM(wide, BF),
        pltpu.VMEM((width, ff), BF),
        pltpu.VMEM((ff, width), BF),
        pltpu.VMEM((n_sec, 2, tokens, width // 2), F32),
        pltpu.VMEM((n_sec, 8, tokens), F32),
        pltpu.VMEM(image, BF),
        pltpu.VMEM((2, tokens, width), BF),
        pltpu.VMEM((GROUP, GROUP), BF),
        pltpu.VMEM((8, 2 * width), F32),
        pltpu.VMEM((8, width // 2), F32),
        pltpu.VMEM((n_unit, rows, width), BF),
        pltpu.VMEM((n_line, n_unit, rows, width), BF),
        pltpu.VMEM((n_line, n_unit, rows, width), BF),
        pltpu.VMEM((n_chunk + n_low, N_SUB, rows, width), BF),
        pltpu.VMEM((2, 2 * N_SUB, rows, width), BF),
        pltpu.VMEM((8, width), F32),
        pltpu.VMEM((8, width), F32),
        pltpu.VMEM((n_line, 8, width), F32),
        pltpu.VMEM((n_line, 8, width), F32),
        dma((2,)),
        dma((n_sec,)),
        dma((n_sec,)),
        dma((n_sec,)),
        dma((n_sec,)),
        dma((n_sec,)),
        dma((n_sec + 3,)),
        dma,
        dma((4, 4)),
        dma((4, 4)),
        dma,
        dma,
        dma((2,)),
        dma((n_chunk + n_low,)),
        dma((n_low,)),
        dma((n_low,)),
        dma((n_line, n_unit)),
        dma((n_line, n_unit)),
        dma((n_line, n_unit)),
        dma((n_line, n_unit)),
        dma((n_unit,)),
        dma((n_unit,)),
        dma((n_unit,)),
        dma((1 + 2 * n_line,)),
        dma((1 + 2 * n_line,)),
    ]
    out, ig, gw, gd, small = pl.pallas_call(
        functools.partial(relay, n_sec, lines, tokens, width, ff),
        out_shape=(
            jax.ShapeDtypeStruct((1, tokens, width), BF),
            jax.ShapeDtypeStruct((1, tokens, width), BF),
            jax.ShapeDtypeStruct((width, ff), BF),
            jax.ShapeDtypeStruct((ff // 2, width), BF),
            jax.ShapeDtypeStruct((8, width), F32),
        ),
        in_specs=[any_spec, any_spec, vmem_spec, any_spec, any_spec] + [vmem_spec] * 4,
        out_specs=(any_spec, any_spec, any_spec, any_spec, vmem_spec),
        scratch_shapes=scratch,
        compiler_params=pltpu.CompilerParams(
            collective_id=0, has_side_effects=True, vmem_limit_bytes=63 * 2**20
        ),
    )(patches, cot, tab, wm, wd, gain, bias, bm, sv)
    return (
        out,
        ig,
        small[0:1],
        small[1:2],
        gw.astype(F32)[None],
        small[3:7].reshape(1, ff),
        small[2:3],
        gd.astype(F32)[None],
    )


def solution(mesh):
    n_sec, n_dp = mesh.shape["section"], mesh.shape["dp"]
    images = P(("section", "dp"), None, None)
    row = P("section", None)
    block = P("section", None, None)
    return jax.shard_map(
        functools.partial(on_device, n_sec, n_dp),
        mesh=mesh,
        in_specs=(images, images, images, P(("section", "dp")), row, row, block, row, row, block),
        out_specs=(images, images, row, row, block, row, row, block),
        check_vma=False,
    )
```

```python
import functools

import jax
import jax.numpy as jnp
from jax import lax
from jax.experimental import pallas as pl
from jax.experimental.pallas import tpu as pltpu
from jax.sharding import PartitionSpec as P

HEADS = 12
HEAD_DIM = 64
GROUP = 256
EPS = 1e-06
MESH = pl.DeviceIdType.MESH
BF = jnp.bfloat16
F32 = jnp.float32
HI = lax.Precision.HIGHEST
LAG_SIB, LAG_ONE, LAG_TWO, LAG_END = 1, 2, 4, 6
N_SUB = 2
SLOTS = 8
N_AWAY = 3


def nn(a, b, precision=None):
    return lax.dot_general(a, b, (((1,), (0,)), ((), ())), precision=precision, preferred_element_type=F32)


def nt(a, b, precision=None):
    return lax.dot_general(a, b, (((1,), (1,)), ((), ())), precision=precision, preferred_element_type=F32)


def tn(a, b, precision=None):
    return lax.dot_general(a, b, (((0,), (0,)), ((), ())), precision=precision, preferred_element_type=F32)


def normalise(x):
    centered = x - jnp.mean(x, axis=-1, keepdims=True)
    scale = lax.rsqrt(jnp.mean(centered * centered, axis=-1, keepdims=True) + EPS)
    return centered * scale, scale


def relay(
    n_sec, lines, tokens, width, ff,
    patches, cot, positions, counts, wm, wd, gain, bias, bm, sv,
    o_out, o_ig, o_w, o_d, o_small,
    hin, gin, act, big1, big2, big3, wv, dv, cs, tab, tabs, hout, gout, perm, bqk, freq,
    mine, zin, pin, sib, tmp, sg, sg_sib, sg_one, sg_two,
    w_sem, hin_r, gin_r, tab_r, hop_s, gop_s, ini_s, cot_r, wd_s, wd_r, det_s, det_r, out_r, ig_r,
    sib_s, sib_r, low_s, mine_r, za_s, zin_r, pb_s, pin_r, fin_l, fin_s, fin_r, guest_r, pass_s, pass_r, sg_s, sg_r,
):
    s = lax.axis_index("section")
    d = lax.axis_index("dp")
    core = lax.rem(d, 2)
    other = d + 1 - 2 * core
    even = lax.rem(s, 2) == 0
    odd = lax.rem(s, 2) == 1
    last = n_sec - 1
    half = tokens // 2
    n_main = (width // 256) * (ff // width)
    n_low = (ff // 2) // 256
    n_own = n_main + n_low
    n_chunk = n_own + n_low
    n_away = N_AWAY
    limit = jnp.where(
        s == 0, n_main, jnp.where(s == 1, n_own - n_away, jnp.where(s == last, n_chunk, n_own + n_away))
    )
    n_side = jnp.where(s == 1, n_low + n_away, jnp.where(s == last, n_low, 0))
    n_sub = N_SUB
    score_scale = HEAD_DIM ** (-0.5)

    def to_section(target):
        return {"section": target}

    def to_dp(target):
        return {"dp": target}

    def remote(src, dst, send, recv, device):
        return pltpu.make_async_remote_copy(
            src_ref=src, dst_ref=dst, send_sem=send, recv_sem=recv, device_id=device, device_id_type=MESH
        )

    spots = []
    for stride in lines:
        pos = lax.rem(d // stride, 4)
        near = d + (1 - 2 * lax.rem(pos, 2)) * stride
        across = d + (3 - 2 * pos) * stride
        inner = (pos == 1) | (pos == 2)
        outer = (pos == 0) | (pos == 3)
        spots.append((near, across, inner, outer))

    barrier = pltpu.get_barrier_semaphore()
    for step in range(1, n_sec):
        pl.semaphore_signal(barrier, inc=1, device_id=to_section(lax.rem(s + step, n_sec)), device_id_type=MESH)
    pl.semaphore_signal(barrier, inc=1, device_id=to_dp(other), device_id_type=MESH)
    for near, across, inner, outer in spots:
        pl.semaphore_signal(barrier, inc=1, device_id=to_dp(near), device_id_type=MESH)

        @pl.when(inner)
        def _():
            pl.semaphore_signal(barrier, inc=1, device_id=to_dp(across), device_id_type=MESH)

    load_w = pltpu.make_async_copy(wm.at[0], wv, w_sem.at[0])
    load_d = pltpu.make_async_copy(wd.at[0], dv.at[pl.ds(ff // 2, ff // 2)], w_sem.at[1])
    load_w.start()

    @pl.when(odd)
    def _():
        load_d.start()

    peers = n_sec + len(spots)
    for near, across, inner, outer in spots:
        peers = peers + jnp.where(inner, 1, 0)
    tab[...] = jnp.zeros_like(tab)
    tab[0, 0:2, :] = positions[0].astype(F32)
    tab[0, 2:3, :] = jnp.broadcast_to(counts[...].astype(F32), (1, tokens))
    pl.semaphore_wait(barrier, peers)

    tab_sends = []
    for step in range(1, n_sec):
        tab_sends.append(
            remote(tab.at[0], tabs.at[s], ini_s.at[step - 1], tab_r.at[s], to_section(lax.rem(s + step, n_sec)))
        )
    for send in tab_sends:
        send.start()
    tab_own = pltpu.make_async_copy(tab.at[0], tabs.at[s], tab_r.at[s])
    tab_own.start()
    patch_send = remote(patches.at[0], hin.at[s], ini_s.at[n_sec], hin_r.at[s], to_section(0))
    patch_own = pltpu.make_async_copy(patches.at[0], hin.at[0], hin_r.at[0])
    cot_send = remote(cot.at[0], gin.at[s], ini_s.at[n_sec + 1], gin_r.at[s], to_section(last))
    cot_own = pltpu.make_async_copy(cot.at[0], gin.at[last], gin_r.at[last])
    cot_out = remote(cot.at[0], gout.at[0], ini_s.at[n_sec + 1], cot_r, to_section(last - 1))
    cot_on = remote(gout.at[0], gin.at[0], ini_s.at[n_sec + 2], gin_r.at[0], to_section(last))

    @pl.when(s == 0)
    def _():
        patch_own.start()

    @pl.when(s != 0)
    def _():
        patch_send.start()

    @pl.when((s != 0) & (s != last))
    def _():
        cot_send.start()

    @pl.when(s == last)
    def _():
        cot_own.start()

    near0 = spots[0][0]
    side = lax.rem(d // lines[0], 2)
    n_part = 4
    part = (ff // 2) // 4 // n_part

    def down_rows(which_side, which_core, k):
        start = (which_side * 2 + which_core) * (n_part * part) + k * part
        return pl.ds(pl.multiple_of(start, part), part)

    def down_send(k):
        rows = down_rows(side, core, k)
        return remote(wd.at[0, rows], dv.at[rows], wd_s.at[0, k], wd_r.at[0, k], to_section(lax.rem(s + 1, n_sec)))

    def down_near(k):
        rows = down_rows(side, core, k)
        return remote(dv.at[rows], dv.at[rows], wd_s.at[1, k], wd_r.at[1, k], to_dp(near0))

    def down_pass(k):
        rows = down_rows(side, core, k)
        return remote(dv.at[rows], dv.at[rows], wd_s.at[2, k], wd_r.at[2, k], to_dp(other))

    def down_pass_far(k):
        rows = down_rows(1 - side, core, k)
        return remote(dv.at[rows], dv.at[rows], wd_s.at[3, k], wd_r.at[3, k], to_dp(other))

    n_direct = n_part // 2

    def down_out(k):
        to = hout.at[last, pl.ds((k - n_direct) * part, part)]
        send = remote(wd.at[0, down_rows(side, core, k)], to, wd_s.at[0, k], det_r.at[k - n_direct], to_section(last - 1))
        return send

    def down_on(k):
        held = hout.at[last, pl.ds((k - n_direct) * part, part)]
        to = dv.at[down_rows(side, core, k)]
        return remote(held, to, det_s.at[k - n_direct], wd_r.at[0, k], to_section(1))

    @pl.when(s == 0)
    def _():
        for k in range(n_direct):
            down_send(k).start()
            down_out(k + n_direct).start()

    def table(i):
        pltpu.make_async_copy(tab.at[0], tabs.at[i], tab_r.at[i]).wait()
        angle = nn(jnp.transpose(tabs[i]), freq[...], HI)
        cs[i, 0] = jnp.cos(angle)
        cs[i, 1] = jnp.sin(angle)

    ahead = (s == 0) & (core == 0)

    @pl.when(even)
    def _():
        freq[...] = jnp.zeros_like(freq)
        freq[0:1, :] = sv[:, : width // 2]
        freq[1:2, :] = sv[:, width // 2 :]

        def early(i, carry):
            @pl.when((i == 0) | jnp.logical_not(ahead))
            def _():
                table(i)

            return carry

        lax.fori_loop(0, n_sec, early, 0)

    @pl.when(odd)
    def _():
        for i in range(n_sec):
            pltpu.make_async_copy(tab.at[0], tabs.at[i], tab_r.at[i]).wait()

    sg[...] = jnp.zeros_like(sg)
    load_w.wait()

    @pl.when(even)
    def _():
        old = lax.broadcasted_iota(jnp.int32, (GROUP, GROUP), 0)
        new = lax.broadcasted_iota(jnp.int32, (GROUP, GROUP), 1)
        source = ((new & 127) >> 5) * 64 + (new >> 7) * 32 + (new & 31)
        perm[...] = jnp.where(old == source, 1.0, 0.0).astype(BF)
        table = perm[...]
        for block in range(2 * width // GROUP):
            columns = slice(block * GROUP, (block + 1) * GROUP)
            wv[:, columns] = nn(wv[:, columns], table).astype(BF)
            row = jnp.broadcast_to(bm[:, columns], (8, GROUP))
            bqk[:, columns] = nn(row, table.astype(F32), HI)

    @pl.when(s == last - 1)
    def _():
        for k in range(n_direct, n_part):
            down_out(k).wait_recv()
            down_on(k).start()
        for k in range(n_part):
            down_send(k).start()
        cot_out.wait_recv()
        cot_on.start()
        for k in range(n_direct, n_part):
            down_on(k).wait_send()

    @pl.when(odd)
    def _():
        for k in [0, 2, 1, 3]:
            down_send(k).wait_recv()
            down_near(k).start()
            down_pass(k).start()

    lane = lax.broadcasted_iota(jnp.int32, (1, GROUP), 1)
    q_masks = [((lane & 127) >> 5) == e for e in range(4)]
    v_masks = [(lane >> 6) == e for e in range(4)]
    zero_low = jnp.zeros((), BF)

    def count_of(i):
        return tabs[i, 2:3, 0:1]

    def row_mask(i):
        ids = lax.broadcasted_iota(jnp.int32, (tokens, 1), 0).astype(F32)
        return jnp.where(ids < count_of(i), 1.0, 0.0)

    def key_mask(i):
        ids = lax.broadcasted_iota(jnp.int32, (1, tokens), 1).astype(F32)
        return ids < count_of(i)

    n_group = width // GROUP
    pairs = width // 2 // n_group

    def attention_forward(i, slot):
        x = hin[i].astype(F32)
        xhat, _ = normalise(x)
        a = (xhat * gain[...] + bias[...]).astype(BF)
        act[i] = a
        keys_on = key_mask(i)
        for g in range(n_group):
            cosine = cs[i, 0, :, g * pairs : (g + 1) * pairs]
            sine = cs[i, 1, :, g * pairs : (g + 1) * pairs]
            turned = []
            for which in range(2):
                lo = which * width + g * GROUP
                t = nn(a, wv[:, lo : lo + GROUP]) + bqk[0:1, lo : lo + GROUP]
                t1, t2 = t[:, :128], t[:, 128:]
                r = jnp.concatenate([t1 * cosine - t2 * sine, t1 * sine + t2 * cosine], axis=1)
                r = (r * score_scale if which == 0 else r).astype(BF)
                big1[i, :, lo : lo + GROUP] = r
                turned.append(r)
            lo = 2 * width + g * GROUP
            value = (nn(a, wv[:, lo : lo + GROUP]) + bm[:, lo : lo + GROUP]).astype(BF)
            big1[i, :, lo : lo + GROUP] = value
            query, key = turned
            weights = []
            for e in range(4):
                scores = nt(jnp.where(q_masks[e], query, zero_low), key)
                scores = jnp.where(keys_on, scores, -1e30)
                top = jnp.max(scores, axis=-1, keepdims=True)
                p = jnp.exp(scores - top)
                p = (p * (1.0 / jnp.sum(p, axis=-1, keepdims=True))).astype(BF)
                big2[i, :, (4 * g + e) * tokens : (4 * g + e + 1) * tokens] = p
                weights.append(p)
            stacked = jnp.concatenate([jnp.where(v_masks[e], value, zero_low) for e in range(4)], axis=0)
            context = nn(jnp.concatenate(weights, axis=1), stacked)
            lo = 3 * width + g * GROUP
            big1[i, :, lo : lo + GROUP] = context.astype(BF)
        branch = nn(big1[i, :, 3 * width :], wv[:, 3 * width :]) + bm[:, 3 * width :]
        hout[slot] = (x + row_mask(i) * branch).astype(BF)

    def norm_backward(i, g_up, gact):
        xhat, scale = normalise(hin[i].astype(F32))
        sg[0:1, :] += jnp.sum(gact * xhat, axis=0, keepdims=True)
        sg[1:2, :] += jnp.sum(gact, axis=0, keepdims=True)
        gn = gact * gain[...]
        inside = gn - jnp.mean(gn, axis=-1, keepdims=True) - xhat * jnp.mean(gn * xhat, axis=-1, keepdims=True)
        return g_up + scale * inside

    def attention_backward(i, slot):
        g_up = gin[i].astype(F32)
        gb = row_mask(i) * g_up
        sg[6:7, :] += jnp.sum(gb, axis=0, keepdims=True)
        low = gb.astype(BF)
        dctx_all = nt(low, wv[:, 3 * width :]).astype(BF)
        for g in range(n_group):
            qlo, klo, vlo = g * GROUP, width + g * GROUP, 2 * width + g * GROUP
            query = big1[i, :, qlo : qlo + GROUP]
            key = big1[i, :, klo : klo + GROUP]
            value = big1[i, :, vlo : vlo + GROUP]
            dctx = dctx_all[:, g * GROUP : (g + 1) * GROUP]
            clo = 3 * width + g * GROUP
            both = dctx.astype(F32) * big1[i, :, clo : clo + GROUP].astype(F32)
            d_stack, p_stack, gs_list = [], [], []
            for e in range(4):
                d_e = jnp.where(v_masks[e], dctx, zero_low)
                gw = nt(d_e, value)
                p_low = big2[i, :, (4 * g + e) * tokens : (4 * g + e + 1) * tokens]
                inside = jnp.sum(jnp.where(v_masks[e], both, 0.0), axis=-1, keepdims=True)
                gs_list.append((p_low.astype(F32) * (gw - inside)).astype(BF))
                d_stack.append(d_e)
                p_stack.append(p_low)
            key_low = key * jnp.asarray(score_scale, BF)
            k_stack = jnp.concatenate([jnp.where(q_masks[e], key_low, zero_low) for e in range(4)], axis=0)
            q_stack = jnp.concatenate([jnp.where(q_masks[e], query, zero_low) for e in range(4)], axis=0)
            dq = nn(jnp.concatenate(gs_list, axis=1), k_stack)
            dk = tn(jnp.concatenate(gs_list, axis=0), q_stack)
            dval = tn(jnp.concatenate(p_stack, axis=0), jnp.concatenate(d_stack, axis=0))
            cosine = cs[i, 0, :, g * pairs : (g + 1) * pairs]
            sine = cs[i, 1, :, g * pairs : (g + 1) * pairs]
            turn = jnp.zeros((tokens, pairs), F32)
            for lo, grad, held, size in ((qlo, dq, query, 1.0 / score_scale), (klo, dk, key, 1.0)):
                g1, g2 = grad[:, :128], grad[:, 128:]
                r = held.astype(F32)
                turn = turn + (g2 * r[:, :128] - g1 * r[:, 128:]) * size
                raw = jnp.concatenate([g1 * cosine + g2 * sine, g2 * cosine - g1 * sine], axis=1).astype(BF)
                big3[i, :, lo : lo + GROUP] = raw
                row = 3 if lo < width else 4
                at = g * GROUP
                sg[row : row + 1, at : at + GROUP] += jnp.sum(raw.astype(F32), axis=0, keepdims=True)
            raw = dval.astype(BF)
            big3[i, :, vlo : vlo + GROUP] = raw
            sg[5:6, g * GROUP : (g + 1) * GROUP] += jnp.sum(raw.astype(F32), axis=0, keepdims=True)
            sums = nn(tabs[i], turn, HI)
            at = g * pairs
            sg[2:3, at : at + pairs] += sums[0:1]
            at = width // 2 + g * pairs
            sg[2:3, at : at + pairs] += sums[1:2]
        gact = nt(big3[i, :, : 3 * width], wv[:, : 3 * width])
        gout[slot] = norm_backward(i, g_up, gact).astype(BF)
        gin[i] = low

    piece = 512

    def dense_forward(i, slot):
        x = hin[i].astype(F32)
        xhat, _ = normalise(x)
        a = (xhat * gain[...] + bias[...]).astype(BF)
        act[i] = a
        for k in range(ff // piece):
            lo = k * piece
            pre = nn(a, wv[:, lo : lo + piece]) + bm[:, lo : lo + piece]
            cdf = 0.5 + 0.5 * lax.erf(pre * (0.5**0.5))
            big1[i, :, lo : lo + piece] = (pre * cdf).astype(BF)
            pdf = jnp.exp(-0.5 * (pre * pre)) * 0.3989422804014327
            big2[i, :, lo : lo + piece] = (cdf + pre * pdf).astype(BF)

        @pl.when(i == 0)
        def _():
            load_d.wait()
            for k in range(n_part):
                down_near(k).wait_recv()
                down_pass_far(k).start()
            for k in range(n_part):
                down_pass(k).wait_recv()
                down_pass_far(k).wait_recv()

        branch = nn(big1[i], dv[...]) + sv[...]
        hout[slot] = (x + row_mask(i) * branch).astype(BF)

    def dense_backward(i, slot):
        g_up = gin[i].astype(F32)
        gb = row_mask(i) * g_up
        sg[2:3, :] += jnp.sum(gb, axis=0, keepdims=True)
        low = gb.astype(BF)
        for k in range(ff // width):
            for m in range(width // GROUP):
                lo = k * width + m * GROUP
                gh = nt(low, dv[lo : lo + GROUP, :])
                gpre = (gh * big2[i, :, lo : lo + GROUP].astype(F32)).astype(BF)
                big3[i, :, lo : lo + GROUP] = gpre
                at = m * GROUP
                sg[3 + k : 4 + k, at : at + GROUP] += jnp.sum(gpre.astype(F32), axis=0, keepdims=True)
        gact = nt(big3[i], wv[...])
        gout[slot] = norm_backward(i, g_up, gact).astype(BF)
        gin[i] = low

    def hop_send(i, slot):
        return remote(hout.at[slot], hin.at[i], hop_s.at[i], hin_r.at[i], to_section(lax.rem(s + 1, n_sec)))

    def result_send(i, slot):
        return remote(hout.at[slot], o_out.at[0], hop_s.at[i], out_r, to_section(i))

    def back_send(i, slot):
        return remote(gout.at[slot], gin.at[i], gop_s.at[i], gin_r.at[i], to_section(lax.rem(s + last, n_sec)))

    def input_send(i, slot):
        return remote(gout.at[slot], o_ig.at[0], gop_s.at[i], ig_r, to_section(i))

    def forward(i):
        hop_send(i, i).wait_recv()

        @pl.when(even)
        def _():
            attention_forward(i, i)

        @pl.when(odd)
        def _():
            dense_forward(i, i)

        @pl.when((s != last) & (i >= 1))
        def _():
            hop_send(i - 1, i - 1).wait_send()

        @pl.when(s != last)
        def _():
            hop_send(i, i).start()

    def backward(i):
        slot = lax.rem(i, 2)

        @pl.when((i == 0) & (s == last - 1))
        def _():
            cot_on.wait_send()

        @pl.when((i == 2) & (s == 0))
        def _():
            pltpu.make_async_copy(gout.at[slot], o_ig.at[0], ig_r).wait()

        back_send(i, slot).wait_recv()

        @pl.when(even)
        def _():
            attention_backward(i, slot)

        @pl.when(odd)
        def _():
            dense_backward(i, slot)

        @pl.when((i >= 2) | ((i == 1) & (s != 0)))
        def _():
            back_send(i - 1, 1 - slot).wait_send()

        @pl.when(s != 0)
        def _():
            back_send(i, slot).start()

        @pl.when((s == 0) & (i != 0))
        def _():
            input_send(i, slot).start()

        @pl.when((s == 0) & (i == 0))
        def _():
            pltpu.make_async_copy(gout.at[slot], o_ig.at[0], ig_r).start()

    def tick(j, carry):
        is_forward = jnp.where(s == last, lax.rem(j, 2) == 0, j < n_sec)
        i = jnp.where(s == last, j // 2, lax.rem(j, n_sec))

        @pl.when(is_forward)
        def _():
            forward(i)

        @pl.when((s == 0) & (j == 0))
        def _():
            cot_out.start()

        @pl.when(ahead & (j == 0))
        def _():
            lax.fori_loop(1, n_sec, lambda i, carry: (table(i), carry)[1], 0)

        @pl.when(jnp.logical_not(is_forward))
        def _():
            backward(i)

        return carry

    lax.fori_loop(0, 2 * n_sec, tick, 0)

    @pl.when(s == last)
    def _():
        for i in range(last):
            result_send(i, i).start()
        pltpu.make_async_copy(hout.at[last], o_out.at[0], out_r).start()

    @pl.when(even)
    def _():
        back = perm[...].astype(F32)
        for block in range(2 * width // GROUP):
            row = 3 + block * GROUP // width
            lo = block * GROUP % width
            part = jnp.broadcast_to(sg[row : row + 1, lo : lo + GROUP], (8, GROUP))
            sg[row : row + 1, lo : lo + GROUP] = nt(part, back, HI)[0:1]

    my_half = pl.ds(core * n_sub, n_sub)
    their_half = pl.ds((1 - core) * n_sub, n_sub)

    def is_own(c):
        after = ((s == 1) & (c >= n_main) & (c < n_own - n_away)) | ((s == last) & (c >= n_own) & (c < n_chunk))
        return ((c >= 0) & (c < n_main)) | after

    def is_guest(c):
        return ((s >= 2) & (c >= n_main) & (c < n_own)) | ((s == last - 1) & (c >= n_own) & (c < n_own + n_away))

    def sib_slot(c):
        return jnp.where(c >= n_own, c - n_low, c)

    def sib_copy(c):
        slot = lax.rem(c, 2)
        at = sib_slot(c)
        return remote(tmp.at[slot, their_half], sib.at[at], sib_s.at[slot], sib_r.at[at], to_dp(other))

    def side_copy(b):
        slot = 2 + lax.rem(b, 2)
        at = n_own + b
        return remote(tmp.at[slot, their_half], sib.at[at], sib_s.at[slot], sib_r.at[at], to_dp(other))

    def side_send(b):
        to = jnp.where((s == 1) & (b < n_low), last, last - 1)
        return remote(
            sib.at[n_own + b], mine.at[pl.ds((n_main + b) * n_sub, n_sub)], low_s.at[b], mine_r.at[b], to_section(to)
        )

    def make_down(slot, row):
        rows = pl.ds(pl.multiple_of(row, 256), 256)
        left = big1[:, :, rows].reshape(n_sec * tokens, 256)
        right = gin[...].reshape(n_sec * tokens, width)
        keep(slot, tn(left, right))

    def keep(slot, block):
        tmp[slot] = block.astype(BF).reshape(2 * n_sub, half // n_sub, width)

    def make_side(b):
        slot = 2 + lax.rem(b, 2)

        @pl.when(b >= 2)
        def _():
            side_copy(b - 2).wait_send()

        make_down(slot, jnp.where(b < n_low, b, b + n_low - n_away) * 256)
        side_copy(b).start()

    def send_side(b):
        slot = 2 + lax.rem(b, 2)
        at = n_own + b
        side_copy(b).wait_recv()
        sib[at] = (tmp[slot, my_half].astype(F32) + sib[at].astype(F32)).astype(BF)
        side_send(b).start()

    def make_block(c):
        slot = lax.rem(c, 2)

        @pl.when(c >= 2)
        def _():
            sib_copy(c - 2).wait_send()

        column = lax.rem(c, ff // width)
        row = c // (ff // width)
        from_act = (c < n_main) & (odd | (column < 3))

        @pl.when(from_act)
        def _():
            rows = pl.ds(pl.multiple_of(row * 256, 256), 256)
            columns = pl.ds(pl.multiple_of(column * width, width), width)
            left = act[:, :, rows].reshape(n_sec * tokens, 256)
            right = big3[:, :, columns].reshape(n_sec * tokens, width)
            keep(slot, tn(left, right))

        @pl.when(from_act & even & (column < 2))
        def _():
            back = perm[...]
            held = tmp[slot].reshape(2 * half, width)
            keep(
                slot,
                jnp.concatenate(
                    [nt(held[:, k * GROUP : (k + 1) * GROUP], back) for k in range(width // GROUP)], axis=1
                ),
            )

        @pl.when(jnp.logical_not(from_act))
        def _():
            upper = ff // 2 + jnp.where(s == last, c - n_own, c - n_main) * 256
            make_down(slot, jnp.where(even, 3 * width + row * 256, upper))

        sib_copy(c).start()

    def spot_copies(k, u):
        near, across, inner, outer = spots[k]
        held = lax.rem(u, SLOTS)
        to_near = remote(mine.at[u], zin.at[k, held], za_s.at[k, u], zin_r.at[k, u], to_dp(near))
        to_across = remote(zin.at[k, held], pin.at[k, held], pb_s.at[k, u], pin_r.at[k, u], to_dp(across))
        return to_near, to_across

    piece_rows = half // n_sub

    def w_place(u):
        c = u // n_sub
        row = c // (ff // width)
        column = lax.rem(c, ff // width)
        start = row * 256 + core * half + lax.rem(u, n_sub) * piece_rows
        rows = pl.ds(pl.multiple_of(start, piece_rows), piece_rows)
        columns = pl.ds(pl.multiple_of(column * width, width), width)
        return o_w.at[rows, columns]

    def d_rows(block, sub):
        start = block * 256 + core * half + sub * piece_rows
        return o_d.at[pl.ds(pl.multiple_of(start, piece_rows), piece_rows), :]

    def d_place(u):
        c = u // n_sub
        late = jnp.where(s == last, c - n_own, c - n_own + n_low - n_away)
        return d_rows(jnp.where(c < n_own, c - n_main, late), lax.rem(u, n_sub))

    def finish_copies(u, place):
        here = pltpu.make_async_copy(mine.at[u], place, fin_l.at[u])
        there = remote(mine.at[u], place, fin_s.at[u], fin_r.at[u], to_dp(other))
        return here, there

    def is_away(u):
        return ((s == last) & (u < n_own * n_sub)) | ((s == last - 1) & (u >= n_own * n_sub))

    def guest_send(u):
        at = jnp.where(s == last, u - n_main * n_sub, u - n_own * n_sub)
        to = jnp.where(s == last, 0, 1)
        return remote(mine.at[u], d_place(u), fin_s.at[u], guest_r.at[at], to_section(to))

    def returned(g):
        block = g // n_sub + jnp.where(s == 0, 0, n_low - n_away)
        return d_rows(block, lax.rem(g, n_sub))

    def guest_take(g):
        return remote(mine.at[0], returned(g), pass_s.at[g], guest_r.at[g], to_dp(other))

    def guest_pass(g):
        return remote(returned(g), returned(g), pass_s.at[g], pass_r.at[g], to_dp(other))

    n_returned = jnp.where(s == 0, n_low * n_sub, jnp.where(s == 1, n_away * n_sub, 0))

    def finish(u):
        @pl.when(u < n_main * n_sub)
        def _():
            here, there = finish_copies(u, w_place(u))
            here.start()
            there.start()

        @pl.when((u >= n_main * n_sub) & jnp.logical_not(is_away(u)))
        def _():
            here, there = finish_copies(u, d_place(u))
            here.start()
            there.start()

        @pl.when((u >= n_main * n_sub) & is_away(u))
        def _():
            guest_send(u).start()

    small_sib = remote(sg, sg_sib, sg_s.at[0], sg_r.at[0], to_dp(other))

    def small_copies(k):
        near, across, inner, outer = spots[k]
        to_near = remote(sg, sg_one.at[k], sg_s.at[1 + 2 * k], sg_r.at[1 + 2 * k], to_dp(near))
        to_across = remote(sg_one.at[k], sg_two.at[k], sg_s.at[2 + 2 * k], sg_r.at[2 + 2 * k], to_dp(across))
        return to_near, to_across

    n_unit = n_chunk * n_sub
    my_units = limit * n_sub
    steps = my_units + n_sub * LAG_SIB + len(lines) * LAG_END + 1

    def sum_step(t, carry):
        c = t // n_sub
        first = lax.rem(t, n_sub) == 0
        second = lax.rem(t, n_sub) == 1

        @pl.when(first & is_own(c))
        def _():
            make_block(c)

        @pl.when(second & (c < n_side))
        def _():
            make_side(c)

        c1 = c - LAG_SIB

        @pl.when(first & is_own(c1))
        def _():
            slot = lax.rem(c1, 2)
            at = sib_slot(c1)
            sib_copy(c1).wait_recv()
            mine[pl.ds(c1 * n_sub, n_sub)] = (tmp[slot, my_half].astype(F32) + sib[at].astype(F32)).astype(BF)

        @pl.when(second & (c1 >= 0) & (c1 < n_side))
        def _():
            send_side(c1)

        @pl.when(first & is_guest(c1))
        def _():
            side_send(c1 - n_main).wait_recv()

        @pl.when(t == 0)
        def _():
            small_sib.start()

        @pl.when(t == 2)
        def _():
            small_sib.wait()
            sg[...] = sg[...] + sg_sib[...]

        for k in range(len(lines)):
            near, across, inner, outer = spots[k]
            small_near, small_across = small_copies(k)
            at = 2 + 9 * k

            @pl.when(outer & (t == at))
            def _():
                small_near.start()

            @pl.when(inner & (t == at + 3))
            def _():
                small_near.wait_recv()
                sg_one[k] = sg[...] + sg_one[k]
                small_across.start()

            @pl.when(inner & (t == at + 6))
            def _():
                small_across.wait()
                sg[...] = sg_one[k] + sg_two[k]
                small_near.start()
                small_near.wait_send()

            @pl.when(outer & (t == at + 9))
            def _():
                small_near.wait()
                sg[...] = sg_one[k]

        for k in range(len(lines)):
            near, across, inner, outer = spots[k]
            base = LAG_SIB * n_sub + k * LAG_END
            u0 = t - base

            @pl.when(outer & (u0 >= 0) & (u0 < my_units))
            def _():
                to_near, _ = spot_copies(k, u0)
                to_near.start()

            u2 = t - base - LAG_ONE

            @pl.when(inner & (u2 >= 0) & (u2 < my_units))
            def _():
                to_near, to_across = spot_copies(k, u2)
                to_near.wait_recv()
                held = lax.rem(u2, SLOTS)
                zin[k, held] = (mine[u2].astype(F32) + zin[k, held].astype(F32)).astype(BF)
                to_across.start()

            u3 = t - base - LAG_TWO

            @pl.when(inner & (u3 >= 0) & (u3 < my_units))
            def _():
                to_near, to_across = spot_copies(k, u3)
                to_across.wait()
                held = lax.rem(u3, SLOTS)
                mine[u3] = (zin[k, held].astype(F32) + pin[k, held].astype(F32)).astype(BF)
                to_near.start()
                if k == len(lines) - 1:
                    finish(u3)

            u4 = t - base - LAG_END

            @pl.when(outer & (u4 >= 0) & (u4 < my_units))
            def _():
                to_near, _ = spot_copies(k, u4)
                to_near.wait()
                mine[u4] = zin[k, lax.rem(u4, SLOTS)]
                if k == len(lines) - 1:
                    finish(u4)

        return carry

    lax.fori_loop(0, steps, sum_step, 0)

    def take(g, carry):
        guest_take(g).wait_recv()
        guest_pass(g).start()
        return carry

    lax.fori_loop(0, n_returned, take, 0)
    o_small[...] = sg[...]

    for send in tab_sends:
        send.wait_send()

    @pl.when(s != 0)
    def _():
        patch_send.wait_send()

    @pl.when(s != last)
    def _():
        cot_send.wait_send()

    @pl.when(even)
    def _():
        for k in range(n_part):
            down_send(k).wait_send()

    sib_copy(0).wait_send()
    sib_copy(1).wait_send()

    @pl.when(odd)
    def _():
        for k in range(n_part):
            down_near(k).wait_send()
            down_pass(k).wait_send()
            down_pass_far(k).wait_send()
        side_copy(0).wait_send()
        side_copy(1).wait_send()
        for b in range(n_low):
            side_send(b).wait_send()

    @pl.when(s == 1)
    def _():
        for b in range(n_low, n_low + n_away):
            side_send(b).wait_send()

    back_send(last, last % 2).wait_send()

    @pl.when(s != last)
    def _():
        hop_send(last, last).wait_send()

    @pl.when(s == last)
    def _():
        for i in range(last):
            result_send(i, i).wait_send()

    pltpu.make_async_copy(hout.at[0], o_out.at[0], out_r).wait()

    @pl.when(s != 0)
    def _():
        pltpu.make_async_copy(gout.at[0], o_ig.at[0], ig_r).wait()

    for k in range(len(lines)):
        near, across, inner, outer = spots[k]

        @pl.when(inner)
        def _():
            def drain(u, carry):
                to_near, _ = spot_copies(k, u)
                to_near.wait_send()
                return carry

            lax.fori_loop(0, my_units, drain, 0)

    def drain_main(u, carry):
        here, there = finish_copies(u, w_place(u))
        here.wait()
        there.wait()
        return carry

    def drain_down(u, carry):
        here, there = finish_copies(u, d_place(u))
        here.wait()
        there.wait()
        return carry

    def drain_guest(u, carry):
        guest_send(u).wait_send()
        return carry

    def drain_pass(g, carry):
        guest_pass(g).wait()
        return carry

    lax.fori_loop(0, n_main * n_sub, drain_main, 0)
    lax.fori_loop(0, n_returned, drain_pass, 0)

    @pl.when(s == 1)
    def _():
        lax.fori_loop(n_main * n_sub, (n_own - n_away) * n_sub, drain_down, 0)

    @pl.when(s == last - 1)
    def _():
        lax.fori_loop(n_main * n_sub, n_own * n_sub, drain_down, 0)
        lax.fori_loop(n_own * n_sub, (n_own + n_away) * n_sub, drain_guest, 0)

    @pl.when(s == last)
    def _():
        lax.fori_loop(n_main * n_sub, n_own * n_sub, drain_guest, 0)
        lax.fori_loop(n_own * n_sub, n_unit, drain_down, 0)


def line_strides(n_dp):
    chips, stride, strides = n_dp // 2, 2, []
    while chips > 1:
        assert chips % 4 == 0
        strides.append(stride)
        stride, chips = stride * 4, chips // 4
    return strides


def on_device(n_sec, n_dp, patches, cot, positions, counts, gain, bias, wm, bm, sv, wd):
    _, tokens, width = patches.shape
    ff = wm.shape[2]
    lines = line_strides(n_dp)
    n_low = (ff // 2) // 256
    n_own = (width // 256) * (ff // width) + n_low
    n_chunk = n_own + n_low
    n_unit, rows = n_chunk * N_SUB, 128 // N_SUB
    any_spec = pl.BlockSpec(memory_space=pl.ANY)
    vmem_spec = pl.BlockSpec(memory_space=pltpu.VMEM)
    image = (n_sec, tokens, width)
    wide = (n_sec, tokens, ff)
    dma = pltpu.SemaphoreType.DMA
    n_line = len(lines)
    scratch = [
        pltpu.VMEM(image, BF),
        pltpu.VMEM(image, BF),
        pltpu.VMEM(image, BF),
        pltpu.VMEM(wide, BF),
        pltpu.VMEM(wide, BF),
        pltpu.VMEM(wide, BF),
        pltpu.VMEM((width, ff), BF),
        pltpu.VMEM((ff, width), BF),
        pltpu.VMEM((n_sec, 2, tokens, width // 2), F32),
        pltpu.VMEM((1, 8, tokens), F32),
        pltpu.VMEM((n_sec, 8, tokens), F32),
        pltpu.VMEM(image, BF),
        pltpu.VMEM((2, tokens, width), BF),
        pltpu.VMEM((GROUP, GROUP), BF),
        pltpu.VMEM((8, 2 * width), F32),
        pltpu.VMEM((8, width // 2), F32),
        pltpu.VMEM((n_unit, rows, width), BF),
        pltpu.VMEM((n_line, SLOTS, rows, width), BF),
        pltpu.VMEM((n_line, SLOTS, rows, width), BF),
        pltpu.VMEM((n_own + n_low + N_AWAY, N_SUB, rows, width), BF),
        pltpu.VMEM((4, 2 * N_SUB, rows, width), BF),
        pltpu.VMEM((8, width), F32),
        pltpu.VMEM((8, width), F32),
        pltpu.VMEM((n_line, 8, width), F32),
        pltpu.VMEM((n_line, 8, width), F32),
        dma((2,)),
        dma((n_sec,)),
        dma((n_sec,)),
        dma((n_sec,)),
        dma((n_sec,)),
        dma((n_sec,)),
        dma((n_sec + 3,)),
        dma,
        dma((4, 4)),
        dma((4, 4)),
        dma((2,)),
        dma((2,)),
        dma,
        dma,
        dma((4,)),
        dma((n_own + n_low + N_AWAY,)),
        dma((n_low + N_AWAY,)),
        dma((n_low + N_AWAY,)),
        dma((n_line, n_unit)),
        dma((n_line, n_unit)),
        dma((n_line, n_unit)),
        dma((n_line, n_unit)),
        dma((n_unit,)),
        dma((n_unit,)),
        dma((n_unit,)),
        dma((n_low * N_SUB,)),
        dma((n_low * N_SUB,)),
        dma((n_low * N_SUB,)),
        dma((1 + 2 * n_line,)),
        dma((1 + 2 * n_line,)),
    ]
    out, ig, gw, gd, small = pl.pallas_call(
        functools.partial(relay, n_sec, lines, tokens, width, ff),
        out_shape=(
            jax.ShapeDtypeStruct((1, tokens, width), BF),
            jax.ShapeDtypeStruct((1, tokens, width), BF),
            jax.ShapeDtypeStruct((width, ff), BF),
            jax.ShapeDtypeStruct((ff // 2, width), BF),
            jax.ShapeDtypeStruct((8, width), F32),
        ),
        in_specs=[any_spec] * 2 + [vmem_spec] * 2 + [any_spec] * 2 + [vmem_spec] * 4,
        out_specs=(any_spec, any_spec, any_spec, any_spec, vmem_spec),
        scratch_shapes=scratch,
        compiler_params=pltpu.CompilerParams(
            collective_id=0, has_side_effects=True, vmem_limit_bytes=63 * 2**20
        ),
    )(patches, cot, positions, counts.reshape(1, 1), wm, wd, gain, bias, bm, sv)
    return (
        out,
        ig,
        small[0:1],
        small[1:2],
        gw.astype(F32)[None],
        small[3:7].reshape(1, ff),
        small[2:3],
        gd.astype(F32)[None],
    )


def solution(mesh):
    n_sec, n_dp = mesh.shape["section"], mesh.shape["dp"]
    images = P(("section", "dp"), None, None)
    row = P("section", None)
    block = P("section", None, None)
    return jax.shard_map(
        functools.partial(on_device, n_sec, n_dp),
        mesh=mesh,
        in_specs=(images, images, images, P(("section", "dp")), row, row, block, row, row, block),
        out_specs=(images, images, row, row, block, row, row, block),
        check_vma=False,
    )
```

```python
import functools

import jax
import jax.numpy as jnp
from jax import lax
from jax.experimental import pallas as pl
from jax.experimental.pallas import tpu as pltpu
from jax.sharding import PartitionSpec as P

HEADS = 12
HEAD_DIM = 64
GROUP = 256
EPS = 1e-06
MESH = pl.DeviceIdType.MESH
BF = jnp.bfloat16
F32 = jnp.float32
HI = lax.Precision.HIGHEST
LAG_SIB, LAG_ONE, LAG_TWO, LAG_END = 1, 2, 4, 6
N_SUB = 2
SLOTS = 8
N_AWAY = 1


def nn(a, b, precision=None):
    return lax.dot_general(a, b, (((1,), (0,)), ((), ())), precision=precision, preferred_element_type=F32)


def nt(a, b, precision=None):
    return lax.dot_general(a, b, (((1,), (1,)), ((), ())), precision=precision, preferred_element_type=F32)


def tn(a, b, precision=None):
    return lax.dot_general(a, b, (((0,), (0,)), ((), ())), precision=precision, preferred_element_type=F32)


def normalise(x):
    centered = x - jnp.mean(x, axis=-1, keepdims=True)
    scale = lax.rsqrt(jnp.mean(centered * centered, axis=-1, keepdims=True) + EPS)
    return centered * scale, scale


def relay(
    n_sec, lines, tokens, width, ff,
    patches, cot, positions, counts, wm, wd, gain, bias, bm, sv,
    o_out, o_ig, o_w, o_d, o_small,
    hin, gin, act, big1, big2, big3, wv, dv, cs, tab, tabs, hout, gout, perm, bqk, freq,
    mine, zin, pin, sib, tmp, sg, sg_sib, sg_one, sg_two,
    w_sem, hin_r, gin_r, tab_r, hop_s, gop_s, ini_s, cot_r, wd_s, wd_r, det_s, det_r, out_r, ig_r,
    sib_s, sib_r, low_s, mine_r, za_s, zin_r, pb_s, pin_r, fin_l, fin_s, fin_r, guest_r, pass_s, pass_r, sg_s, sg_r,
):
    s = lax.axis_index("section")
    d = lax.axis_index("dp")
    core = lax.rem(d, 2)
    other = d + 1 - 2 * core
    even = lax.rem(s, 2) == 0
    odd = lax.rem(s, 2) == 1
    last = n_sec - 1
    half = tokens // 2
    n_main = (width // 256) * (ff // width)
    n_low = (ff // 2) // 256
    n_own = n_main + n_low
    n_chunk = n_own + n_low
    n_away = N_AWAY
    limit = jnp.where(
        s == 0, n_main, jnp.where(s == 1, n_own - n_away, jnp.where(s == last, n_chunk, n_own + n_away))
    )
    n_side = jnp.where(s == 1, n_low + n_away, jnp.where(s == last, n_low, 0))
    n_sub = N_SUB
    score_scale = HEAD_DIM ** (-0.5)

    def to_section(target):
        return {"section": target}

    def to_dp(target):
        return {"dp": target}

    def remote(src, dst, send, recv, device):
        return pltpu.make_async_remote_copy(
            src_ref=src, dst_ref=dst, send_sem=send, recv_sem=recv, device_id=device, device_id_type=MESH
        )

    spots = []
    for stride in lines:
        pos = lax.rem(d // stride, 4)
        near = d + (1 - 2 * lax.rem(pos, 2)) * stride
        across = d + (3 - 2 * pos) * stride
        inner = (pos == 1) | (pos == 2)
        outer = (pos == 0) | (pos == 3)
        spots.append((near, across, inner, outer))

    barrier = pltpu.get_barrier_semaphore()
    for step in range(1, n_sec):
        pl.semaphore_signal(barrier, inc=1, device_id=to_section(lax.rem(s + step, n_sec)), device_id_type=MESH)
    pl.semaphore_signal(barrier, inc=1, device_id=to_dp(other), device_id_type=MESH)
    for near, across, inner, outer in spots:
        pl.semaphore_signal(barrier, inc=1, device_id=to_dp(near), device_id_type=MESH)

        @pl.when(inner)
        def _():
            pl.semaphore_signal(barrier, inc=1, device_id=to_dp(across), device_id_type=MESH)

    load_w = pltpu.make_async_copy(wm.at[0], wv, w_sem.at[0])
    load_d = pltpu.make_async_copy(wd.at[0], dv.at[pl.ds(ff // 2, ff // 2)], w_sem.at[1])
    load_w.start()

    @pl.when(odd)
    def _():
        load_d.start()

    peers = n_sec + len(spots)
    for near, across, inner, outer in spots:
        peers = peers + jnp.where(inner, 1, 0)
    tab[...] = jnp.zeros_like(tab)
    tab[0, 0:2, :] = positions[0].astype(F32)
    tab[0, 2:3, :] = jnp.broadcast_to(counts[...].astype(F32), (1, tokens))
    pl.semaphore_wait(barrier, peers)

    tab_sends = []
    for step in range(1, n_sec):
        tab_sends.append(
            remote(tab.at[0], tabs.at[s], ini_s.at[step - 1], tab_r.at[s], to_section(lax.rem(s + step, n_sec)))
        )
    for send in tab_sends:
        send.start()
    tab_own = pltpu.make_async_copy(tab.at[0], tabs.at[s], tab_r.at[s])
    tab_own.start()
    def rows_of(h):
        return pl.ds(h * half, half)

    def patch_send(h):
        r = rows_of(h)
        return remote(patches.at[0, r], hin.at[s, r], ini_s.at[n_sec + h], hin_r.at[s, h], to_section(0))

    def patch_own(h):
        r = rows_of(h)
        return pltpu.make_async_copy(patches.at[0, r], hin.at[0, r], hin_r.at[0, h])

    def cot_send(h):
        r = rows_of(h)
        return remote(cot.at[0, r], gin.at[s, r], ini_s.at[n_sec + 2 + h], gin_r.at[s, h], to_section(last))

    def cot_own(h):
        r = rows_of(h)
        return pltpu.make_async_copy(cot.at[0, r], gin.at[last, r], gin_r.at[last, h])

    cot_out = remote(cot.at[0], gout.at[0], ini_s.at[n_sec + 2], cot_r, to_section(last - 1))

    def cot_on(h):
        r = rows_of(h)
        return remote(gout.at[0, r], gin.at[0, r], ini_s.at[n_sec + 4 + h], gin_r.at[0, h], to_section(last))

    @pl.when(s == 0)
    def _():
        for h in range(2):
            patch_own(h).start()

    @pl.when(s != 0)
    def _():
        for h in range(2):
            patch_send(h).start()

    @pl.when((s != 0) & (s != last))
    def _():
        for h in range(2):
            cot_send(h).start()

    @pl.when(s == last)
    def _():
        for h in range(2):
            cot_own(h).start()

    near0 = spots[0][0]
    side = lax.rem(d // lines[0], 2)
    n_part = 4
    part = (ff // 2) // 4 // n_part

    def down_rows(which_side, which_core, k):
        start = (which_side * 2 + which_core) * (n_part * part) + k * part
        return pl.ds(pl.multiple_of(start, part), part)

    def down_send(k):
        rows = down_rows(side, core, k)
        return remote(wd.at[0, rows], dv.at[rows], wd_s.at[0, k], wd_r.at[0, k], to_section(lax.rem(s + 1, n_sec)))

    def down_near(k):
        rows = down_rows(side, core, k)
        return remote(dv.at[rows], dv.at[rows], wd_s.at[1, k], wd_r.at[1, k], to_dp(near0))

    def down_pass(k):
        rows = down_rows(side, core, k)
        return remote(dv.at[rows], dv.at[rows], wd_s.at[2, k], wd_r.at[2, k], to_dp(other))

    def down_pass_far(k):
        rows = down_rows(1 - side, core, k)
        return remote(dv.at[rows], dv.at[rows], wd_s.at[3, k], wd_r.at[3, k], to_dp(other))

    n_direct = n_part // 2

    def down_out(k):
        to = hout.at[last, pl.ds((k - n_direct) * part, part)]
        send = remote(wd.at[0, down_rows(side, core, k)], to, wd_s.at[0, k], det_r.at[k - n_direct], to_section(last - 1))
        return send

    def down_on(k):
        held = hout.at[last, pl.ds((k - n_direct) * part, part)]
        to = dv.at[down_rows(side, core, k)]
        return remote(held, to, det_s.at[k - n_direct], wd_r.at[0, k], to_section(1))

    @pl.when(s == 0)
    def _():
        for k in range(n_direct):
            down_send(k).start()
            down_out(k + n_direct).start()

    def table(i):
        pltpu.make_async_copy(tab.at[0], tabs.at[i], tab_r.at[i]).wait()
        angle = nn(jnp.transpose(tabs[i]), freq[...], HI)
        cs[i, 0] = jnp.cos(angle)
        cs[i, 1] = jnp.sin(angle)

    ahead = (s == 0) & (core == 0)

    @pl.when(even)
    def _():
        freq[...] = jnp.zeros_like(freq)
        freq[0:1, :] = sv[:, : width // 2]
        freq[1:2, :] = sv[:, width // 2 :]

        def early(i, carry):
            @pl.when((i == 0) | jnp.logical_not(ahead))
            def _():
                table(i)

            return carry

        lax.fori_loop(0, n_sec, early, 0)

    @pl.when(odd)
    def _():
        for i in range(n_sec):
            pltpu.make_async_copy(tab.at[0], tabs.at[i], tab_r.at[i]).wait()

    sg[...] = jnp.zeros_like(sg)
    load_w.wait()

    @pl.when(even)
    def _():
        old = lax.broadcasted_iota(jnp.int32, (GROUP, GROUP), 0)
        new = lax.broadcasted_iota(jnp.int32, (GROUP, GROUP), 1)
        source = ((new & 127) >> 5) * 64 + (new >> 7) * 32 + (new & 31)
        perm[...] = jnp.where(old == source, 1.0, 0.0).astype(BF)
        table = perm[...]
        for block in range(2 * width // GROUP):
            columns = slice(block * GROUP, (block + 1) * GROUP)
            wv[:, columns] = nn(wv[:, columns], table).astype(BF)
            row = jnp.broadcast_to(bm[:, columns], (8, GROUP))
            bqk[:, columns] = nn(row, table.astype(F32), HI)

    @pl.when(s == last - 1)
    def _():
        for k in range(n_direct, n_part):
            down_out(k).wait_recv()
            down_on(k).start()
        for k in range(n_part):
            down_send(k).start()
        cot_out.wait_recv()
        for h in range(2):
            cot_on(h).start()
        for k in range(n_direct, n_part):
            down_on(k).wait_send()

    @pl.when(odd)
    def _():
        for k in [0, 2, 1, 3]:
            down_send(k).wait_recv()
            down_near(k).start()
            down_pass(k).start()

    lane = lax.broadcasted_iota(jnp.int32, (1, GROUP), 1)
    q_masks = [((lane & 127) >> 5) == e for e in range(4)]
    v_masks = [(lane >> 6) == e for e in range(4)]
    zero_low = jnp.zeros((), BF)

    def count_of(i):
        return tabs[i, 2:3, 0:1]

    def row_mask(i):
        ids = lax.broadcasted_iota(jnp.int32, (tokens, 1), 0).astype(F32)
        return jnp.where(ids < count_of(i), 1.0, 0.0)

    def key_mask(i):
        ids = lax.broadcasted_iota(jnp.int32, (1, tokens), 1).astype(F32)
        return ids < count_of(i)

    n_group = width // GROUP
    pairs = width // 2 // n_group

    def attention_forward(i, slot):
        x = hin[i].astype(F32)
        xhat, _ = normalise(x)
        a = (xhat * gain[...] + bias[...]).astype(BF)
        act[i] = a
        keys_on = key_mask(i)
        for g in range(n_group):
            cosine = cs[i, 0, :, g * pairs : (g + 1) * pairs]
            sine = cs[i, 1, :, g * pairs : (g + 1) * pairs]
            turned = []
            for which in range(2):
                lo = which * width + g * GROUP
                t = nn(a, wv[:, lo : lo + GROUP]) + bqk[0:1, lo : lo + GROUP]
                t1, t2 = t[:, :128], t[:, 128:]
                r = jnp.concatenate([t1 * cosine - t2 * sine, t1 * sine + t2 * cosine], axis=1)
                r = (r * score_scale if which == 0 else r).astype(BF)
                big1[i, :, lo : lo + GROUP] = r
                turned.append(r)
            lo = 2 * width + g * GROUP
            value = (nn(a, wv[:, lo : lo + GROUP]) + bm[:, lo : lo + GROUP]).astype(BF)
            big1[i, :, lo : lo + GROUP] = value
            query, key = turned
            weights = []
            for e in range(4):
                scores = nt(jnp.where(q_masks[e], query, zero_low), key)
                scores = jnp.where(keys_on, scores, -1e30)
                top = jnp.max(scores, axis=-1, keepdims=True)
                p = jnp.exp(scores - top)
                p = (p * (1.0 / jnp.sum(p, axis=-1, keepdims=True))).astype(BF)
                big2[i, :, (4 * g + e) * tokens : (4 * g + e + 1) * tokens] = p
                weights.append(p)
            stacked = jnp.concatenate([jnp.where(v_masks[e], value, zero_low) for e in range(4)], axis=0)
            context = nn(jnp.concatenate(weights, axis=1), stacked)
            lo = 3 * width + g * GROUP
            big1[i, :, lo : lo + GROUP] = context.astype(BF)
        branch = nn(big1[i, :, 3 * width :], wv[:, 3 * width :]) + bm[:, 3 * width :]
        hout[slot] = (x + row_mask(i) * branch).astype(BF)

    def norm_backward(x, g_up, gact):
        xhat, scale = normalise(x.astype(F32))
        sg[0:1, :] += jnp.sum(gact * xhat, axis=0, keepdims=True)
        sg[1:2, :] += jnp.sum(gact, axis=0, keepdims=True)
        gn = gact * gain[...]
        inside = gn - jnp.mean(gn, axis=-1, keepdims=True) - xhat * jnp.mean(gn * xhat, axis=-1, keepdims=True)
        return g_up + scale * inside

    def attention_backward(i, slot):
        g_up = gin[i].astype(F32)
        gb = row_mask(i) * g_up
        sg[6:7, :] += jnp.sum(gb, axis=0, keepdims=True)
        low = gb.astype(BF)
        dctx_all = nt(low, wv[:, 3 * width :]).astype(BF)
        for g in range(n_group):
            qlo, klo, vlo = g * GROUP, width + g * GROUP, 2 * width + g * GROUP
            query = big1[i, :, qlo : qlo + GROUP]
            key = big1[i, :, klo : klo + GROUP]
            value = big1[i, :, vlo : vlo + GROUP]
            dctx = dctx_all[:, g * GROUP : (g + 1) * GROUP]
            clo = 3 * width + g * GROUP
            both = dctx.astype(F32) * big1[i, :, clo : clo + GROUP].astype(F32)
            d_stack, p_stack, gs_list = [], [], []
            for e in range(4):
                d_e = jnp.where(v_masks[e], dctx, zero_low)
                gw = nt(d_e, value)
                p_low = big2[i, :, (4 * g + e) * tokens : (4 * g + e + 1) * tokens]
                inside = jnp.sum(jnp.where(v_masks[e], both, 0.0), axis=-1, keepdims=True)
                gs_list.append((p_low.astype(F32) * (gw - inside)).astype(BF))
                d_stack.append(d_e)
                p_stack.append(p_low)
            key_low = key * jnp.asarray(score_scale, BF)
            k_stack = jnp.concatenate([jnp.where(q_masks[e], key_low, zero_low) for e in range(4)], axis=0)
            q_stack = jnp.concatenate([jnp.where(q_masks[e], query, zero_low) for e in range(4)], axis=0)
            dq = nn(jnp.concatenate(gs_list, axis=1), k_stack)
            dk = tn(jnp.concatenate(gs_list, axis=0), q_stack)
            dval = tn(jnp.concatenate(p_stack, axis=0), jnp.concatenate(d_stack, axis=0))
            cosine = cs[i, 0, :, g * pairs : (g + 1) * pairs]
            sine = cs[i, 1, :, g * pairs : (g + 1) * pairs]
            turn = jnp.zeros((tokens, pairs), F32)
            for lo, grad, held, size in ((qlo, dq, query, 1.0 / score_scale), (klo, dk, key, 1.0)):
                g1, g2 = grad[:, :128], grad[:, 128:]
                r = held.astype(F32)
                turn = turn + (g2 * r[:, :128] - g1 * r[:, 128:]) * size
                raw = jnp.concatenate([g1 * cosine + g2 * sine, g2 * cosine - g1 * sine], axis=1).astype(BF)
                big3[i, :, lo : lo + GROUP] = raw
                row = 3 if lo < width else 4
                at = g * GROUP
                sg[row : row + 1, at : at + GROUP] += jnp.sum(raw.astype(F32), axis=0, keepdims=True)
            raw = dval.astype(BF)
            big3[i, :, vlo : vlo + GROUP] = raw
            sg[5:6, g * GROUP : (g + 1) * GROUP] += jnp.sum(raw.astype(F32), axis=0, keepdims=True)
            sums = nn(tabs[i], turn, HI)
            at = g * pairs
            sg[2:3, at : at + pairs] += sums[0:1]
            at = width // 2 + g * pairs
            sg[2:3, at : at + pairs] += sums[1:2]
        gact = nt(big3[i, :, : 3 * width], wv[:, : 3 * width])
        gout[slot] = norm_backward(hin[i], g_up, gact).astype(BF)
        gin[i] = low

    piece = 512

    def down_ready(i):
        @pl.when(i == 0)
        def _():
            load_d.wait()
            for k in range(n_part):
                down_near(k).wait_recv()
                down_pass_far(k).start()
            for k in range(n_part):
                down_pass(k).wait_recv()
                down_pass_far(k).wait_recv()

    def dense_forward(i, h):
        r = slice(h * half, (h + 1) * half)
        x = hin[i, r].astype(F32)
        xhat, _ = normalise(x)
        a = (xhat * gain[...] + bias[...]).astype(BF)
        act[i, r] = a
        for k in range(ff // piece):
            lo = k * piece
            pre = nn(a, wv[:, lo : lo + piece]) + bm[:, lo : lo + piece]
            cdf = 0.5 + 0.5 * lax.erf(pre * (0.5**0.5))
            big1[i, r, lo : lo + piece] = (pre * cdf).astype(BF)
            pdf = jnp.exp(-0.5 * (pre * pre)) * 0.3989422804014327
            big2[i, r, lo : lo + piece] = (cdf + pre * pdf).astype(BF)
        if h == 0:
            down_ready(i)
        branch = nn(big1[i, r], dv[...]) + sv[...]
        hout[i, r] = (x + row_mask(i)[r] * branch).astype(BF)

    def dense_backward(i, slot):
        g_up = gin[i].astype(F32)
        gb = row_mask(i) * g_up
        sg[2:3, :] += jnp.sum(gb, axis=0, keepdims=True)
        low = gb.astype(BF)
        for k in range(ff // width):
            for m in range(width // GROUP):
                lo = k * width + m * GROUP
                gh = nt(low, dv[lo : lo + GROUP, :])
                gpre = (gh * big2[i, :, lo : lo + GROUP].astype(F32)).astype(BF)
                big3[i, :, lo : lo + GROUP] = gpre
                at = m * GROUP
                sg[3 + k : 4 + k, at : at + GROUP] += jnp.sum(gpre.astype(F32), axis=0, keepdims=True)
        gact = nt(big3[i], wv[...])
        gout[slot] = norm_backward(hin[i], g_up, gact).astype(BF)
        gin[i] = low

    def hop_send(i, h):
        r = rows_of(h)
        to = to_section(lax.rem(s + 1, n_sec))
        return remote(hout.at[i, r], hin.at[i, r], hop_s.at[i, h], hin_r.at[i, h], to)

    def result_send(i):
        return remote(hout.at[i], o_out.at[0], hop_s.at[i, 0], out_r, to_section(i))

    def back_send(i, slot, h):
        r = rows_of(h)
        to = to_section(lax.rem(s + last, n_sec))
        return remote(gout.at[slot, r], gin.at[i, r], gop_s.at[i, h], gin_r.at[i, h], to)

    def input_send(i, slot):
        return remote(gout.at[slot], o_ig.at[0], gop_s.at[i, 0], ig_r, to_section(i))

    def send_hop(i, h):
        @pl.when((s != last) & (i >= 1))
        def _():
            hop_send(i - 1, h).wait_send()

        @pl.when(s != last)
        def _():
            hop_send(i, h).start()

    def send_back(i, slot, h):
        @pl.when((s != 0) & (i >= 1))
        def _():
            back_send(i - 1, 1 - slot, h).wait_send()

        @pl.when(s != 0)
        def _():
            back_send(i, slot, h).start()

    def forward(i):
        @pl.when(even)
        def _():
            for h in range(2):
                hop_send(i, h).wait_recv()
            attention_forward(i, i)
            for h in range(2):
                send_hop(i, h)

        @pl.when(odd)
        def _():
            for h in range(2):
                hop_send(i, h).wait_recv()
                dense_forward(i, h)
                send_hop(i, h)

    def backward(i):
        slot = lax.rem(i, 2)

        @pl.when((i == 0) & (s == last - 1))
        def _():
            for h in range(2):
                cot_on(h).wait_send()

        @pl.when((i == 2) & (s == 0))
        def _():
            pltpu.make_async_copy(gout.at[slot], o_ig.at[0], ig_r).wait()

        @pl.when(even)
        def _():
            for h in range(2):
                back_send(i, slot, h).wait_recv()
            attention_backward(i, slot)
            for h in range(2):
                send_back(i, slot, h)

        @pl.when(odd)
        def _():
            for h in range(2):
                back_send(i, slot, h).wait_recv()
            dense_backward(i, slot)
            for h in range(2):
                send_back(i, slot, h)

        @pl.when((s == 0) & (i >= 2))
        def _():
            input_send(i - 1, 1 - slot).wait_send()

        @pl.when((s == 0) & (i != 0))
        def _():
            input_send(i, slot).start()

        @pl.when((s == 0) & (i == 0))
        def _():
            pltpu.make_async_copy(gout.at[slot], o_ig.at[0], ig_r).start()

    def tick(j, carry):
        is_forward = jnp.where(s == last, lax.rem(j, 2) == 0, j < n_sec)
        i = jnp.where(s == last, j // 2, lax.rem(j, n_sec))

        @pl.when(is_forward)
        def _():
            forward(i)

        @pl.when((s == 0) & (j == 0))
        def _():
            cot_out.start()

        @pl.when(ahead & (j == 0))
        def _():
            lax.fori_loop(1, n_sec, lambda i, carry: (table(i), carry)[1], 0)

        @pl.when(jnp.logical_not(is_forward))
        def _():
            backward(i)

        return carry

    lax.fori_loop(0, 2 * n_sec, tick, 0)

    @pl.when(s == last)
    def _():
        for i in range(last):
            result_send(i).start()
        pltpu.make_async_copy(hout.at[last], o_out.at[0], out_r).start()

    @pl.when(even)
    def _():
        back = perm[...].astype(F32)
        for block in range(2 * width // GROUP):
            row = 3 + block * GROUP // width
            lo = block * GROUP % width
            part = jnp.broadcast_to(sg[row : row + 1, lo : lo + GROUP], (8, GROUP))
            sg[row : row + 1, lo : lo + GROUP] = nt(part, back, HI)[0:1]

    my_half = pl.ds(core * n_sub, n_sub)
    their_half = pl.ds((1 - core) * n_sub, n_sub)

    def is_own(c):
        after = ((s == 1) & (c >= n_main) & (c < n_own - n_away)) | ((s == last) & (c >= n_own) & (c < n_chunk))
        return ((c >= 0) & (c < n_main)) | after

    def is_guest(c):
        return ((s >= 2) & (c >= n_main) & (c < n_own)) | ((s == last - 1) & (c >= n_own) & (c < n_own + n_away))

    def sib_slot(c):
        return jnp.where(c >= n_own, c - n_low, c)

    def sib_copy(c):
        slot = lax.rem(c, 2)
        at = sib_slot(c)
        return remote(tmp.at[slot, their_half], sib.at[at], sib_s.at[slot], sib_r.at[at], to_dp(other))

    def side_copy(b):
        slot = 2 + lax.rem(b, 2)
        at = n_own + b
        return remote(tmp.at[slot, their_half], sib.at[at], sib_s.at[slot], sib_r.at[at], to_dp(other))

    def side_send(b):
        to = jnp.where((s == 1) & (b < n_low), last, last - 1)
        return remote(
            sib.at[n_own + b], mine.at[pl.ds((n_main + b) * n_sub, n_sub)], low_s.at[b], mine_r.at[b], to_section(to)
        )

    def make_down(slot, row):
        rows = pl.ds(pl.multiple_of(row, 256), 256)
        left = big1[:, :, rows].reshape(n_sec * tokens, 256)
        right = gin[...].reshape(n_sec * tokens, width)
        keep(slot, tn(left, right))

    def keep(slot, block):
        tmp[slot] = block.astype(BF).reshape(2 * n_sub, half // n_sub, width)

    def make_side(b):
        slot = 2 + lax.rem(b, 2)

        @pl.when(b >= 2)
        def _():
            side_copy(b - 2).wait_send()

        make_down(slot, jnp.where(b < n_low, b, b + n_low - n_away) * 256)
        side_copy(b).start()

    def send_side(b):
        slot = 2 + lax.rem(b, 2)
        at = n_own + b
        side_copy(b).wait_recv()
        sib[at] = (tmp[slot, my_half].astype(F32) + sib[at].astype(F32)).astype(BF)
        side_send(b).start()

    def make_block(c):
        slot = lax.rem(c, 2)

        @pl.when(c >= 2)
        def _():
            sib_copy(c - 2).wait_send()

        column = lax.rem(c, ff // width)
        row = c // (ff // width)
        from_act = (c < n_main) & (odd | (column < 3))

        @pl.when(from_act)
        def _():
            rows = pl.ds(pl.multiple_of(row * 256, 256), 256)
            columns = pl.ds(pl.multiple_of(column * width, width), width)
            left = act[:, :, rows].reshape(n_sec * tokens, 256)
            right = big3[:, :, columns].reshape(n_sec * tokens, width)
            keep(slot, tn(left, right))

        @pl.when(from_act & even & (column < 2))
        def _():
            back = perm[...]
            held = tmp[slot].reshape(2 * half, width)
            keep(
                slot,
                jnp.concatenate(
                    [nt(held[:, k * GROUP : (k + 1) * GROUP], back) for k in range(width // GROUP)], axis=1
                ),
            )

        @pl.when(jnp.logical_not(from_act))
        def _():
            upper = ff // 2 + jnp.where(s == last, c - n_own, c - n_main) * 256
            make_down(slot, jnp.where(even, 3 * width + row * 256, upper))

        sib_copy(c).start()

    def spot_copies(k, u):
        near, across, inner, outer = spots[k]
        held = lax.rem(u, SLOTS)
        to_near = remote(mine.at[u], zin.at[k, held], za_s.at[k, u], zin_r.at[k, u], to_dp(near))
        to_across = remote(zin.at[k, held], pin.at[k, held], pb_s.at[k, u], pin_r.at[k, u], to_dp(across))
        return to_near, to_across

    piece_rows = half // n_sub

    def w_place(u):
        c = u // n_sub
        row = c // (ff // width)
        column = lax.rem(c, ff // width)
        start = row * 256 + core * half + lax.rem(u, n_sub) * piece_rows
        rows = pl.ds(pl.multiple_of(start, piece_rows), piece_rows)
        columns = pl.ds(pl.multiple_of(column * width, width), width)
        return o_w.at[rows, columns]

    def d_rows(block, sub):
        start = block * 256 + core * half + sub * piece_rows
        return o_d.at[pl.ds(pl.multiple_of(start, piece_rows), piece_rows), :]

    def d_place(u):
        c = u // n_sub
        late = jnp.where(s == last, c - n_own, c - n_own + n_low - n_away)
        return d_rows(jnp.where(c < n_own, c - n_main, late), lax.rem(u, n_sub))

    def finish_copies(u, place):
        here = pltpu.make_async_copy(mine.at[u], place, fin_l.at[u])
        there = remote(mine.at[u], place, fin_s.at[u], fin_r.at[u], to_dp(other))
        return here, there

    def is_away(u):
        return ((s == last) & (u < n_own * n_sub)) | ((s == last - 1) & (u >= n_own * n_sub))

    def guest_send(u):
        at = jnp.where(s == last, u - n_main * n_sub, u - n_own * n_sub)
        to = jnp.where(s == last, 0, 1)
        return remote(mine.at[u], d_place(u), fin_s.at[u], guest_r.at[at], to_section(to))

    def returned(g):
        block = g // n_sub + jnp.where(s == 0, 0, n_low - n_away)
        return d_rows(block, lax.rem(g, n_sub))

    def guest_take(g):
        return remote(mine.at[0], returned(g), pass_s.at[g], guest_r.at[g], to_dp(other))

    def guest_pass(g):
        return remote(returned(g), returned(g), pass_s.at[g], pass_r.at[g], to_dp(other))

    n_returned = jnp.where(s == 0, n_low * n_sub, jnp.where(s == 1, n_away * n_sub, 0))

    def finish(u):
        @pl.when(u < n_main * n_sub)
        def _():
            here, there = finish_copies(u, w_place(u))
            here.start()
            there.start()

        @pl.when((u >= n_main * n_sub) & jnp.logical_not(is_away(u)))
        def _():
            here, there = finish_copies(u, d_place(u))
            here.start()
            there.start()

        @pl.when((u >= n_main * n_sub) & is_away(u))
        def _():
            guest_send(u).start()

    small_sib = remote(sg, sg_sib, sg_s.at[0], sg_r.at[0], to_dp(other))

    def small_copies(k):
        near, across, inner, outer = spots[k]
        to_near = remote(sg, sg_one.at[k], sg_s.at[1 + 2 * k], sg_r.at[1 + 2 * k], to_dp(near))
        to_across = remote(sg_one.at[k], sg_two.at[k], sg_s.at[2 + 2 * k], sg_r.at[2 + 2 * k], to_dp(across))
        return to_near, to_across

    n_unit = n_chunk * n_sub
    my_units = limit * n_sub
    steps = my_units + n_sub * LAG_SIB + len(lines) * LAG_END + 1

    def sum_step(t, carry):
        c = t // n_sub
        first = lax.rem(t, n_sub) == 0
        second = lax.rem(t, n_sub) == 1

        @pl.when(first & is_own(c))
        def _():
            make_block(c)

        @pl.when(second & (c < n_side))
        def _():
            make_side(c)

        c1 = c - LAG_SIB

        @pl.when(first & is_own(c1))
        def _():
            slot = lax.rem(c1, 2)
            at = sib_slot(c1)
            sib_copy(c1).wait_recv()
            mine[pl.ds(c1 * n_sub, n_sub)] = (tmp[slot, my_half].astype(F32) + sib[at].astype(F32)).astype(BF)

        @pl.when(second & (c1 >= 0) & (c1 < n_side))
        def _():
            send_side(c1)

        @pl.when(first & is_guest(c1))
        def _():
            side_send(c1 - n_main).wait_recv()

        @pl.when(t == 0)
        def _():
            small_sib.start()

        @pl.when(t == 2)
        def _():
            small_sib.wait()
            sg[...] = sg[...] + sg_sib[...]

        for k in range(len(lines)):
            near, across, inner, outer = spots[k]
            small_near, small_across = small_copies(k)
            at = 2 + 9 * k

            @pl.when(outer & (t == at))
            def _():
                small_near.start()

            @pl.when(inner & (t == at + 3))
            def _():
                small_near.wait_recv()
                sg_one[k] = sg[...] + sg_one[k]
                small_across.start()

            @pl.when(inner & (t == at + 6))
            def _():
                small_across.wait()
                sg[...] = sg_one[k] + sg_two[k]
                small_near.start()
                small_near.wait_send()

            @pl.when(outer & (t == at + 9))
            def _():
                small_near.wait()
                sg[...] = sg_one[k]

        for k in range(len(lines)):
            near, across, inner, outer = spots[k]
            base = LAG_SIB * n_sub + k * LAG_END
            u0 = t - base

            @pl.when(outer & (u0 >= 0) & (u0 < my_units))
            def _():
                to_near, _ = spot_copies(k, u0)
                to_near.start()

            u2 = t - base - LAG_ONE

            @pl.when(inner & (u2 >= 0) & (u2 < my_units))
            def _():
                to_near, to_across = spot_copies(k, u2)
                to_near.wait_recv()
                held = lax.rem(u2, SLOTS)
                zin[k, held] = (mine[u2].astype(F32) + zin[k, held].astype(F32)).astype(BF)
                to_across.start()

            u3 = t - base - LAG_TWO

            @pl.when(inner & (u3 >= 0) & (u3 < my_units))
            def _():
                to_near, to_across = spot_copies(k, u3)
                to_across.wait()
                held = lax.rem(u3, SLOTS)
                mine[u3] = (zin[k, held].astype(F32) + pin[k, held].astype(F32)).astype(BF)
                to_near.start()
                if k == len(lines) - 1:
                    finish(u3)

            u4 = t - base - LAG_END

            @pl.when(outer & (u4 >= 0) & (u4 < my_units))
            def _():
                to_near, _ = spot_copies(k, u4)
                to_near.wait()
                mine[u4] = zin[k, lax.rem(u4, SLOTS)]
                if k == len(lines) - 1:
                    finish(u4)

        return carry

    lax.fori_loop(0, steps, sum_step, 0)

    def take(g, carry):
        guest_take(g).wait_recv()
        guest_pass(g).start()
        return carry

    lax.fori_loop(0, n_returned, take, 0)
    o_small[...] = sg[...]

    for send in tab_sends:
        send.wait_send()

    @pl.when(s != 0)
    def _():
        for h in range(2):
            patch_send(h).wait_send()

    @pl.when(s == 0)
    def _():
        cot_out.wait_send()

    @pl.when((s != 0) & (s != last))
    def _():
        for h in range(2):
            cot_send(h).wait_send()

    @pl.when(even)
    def _():
        for k in range(n_part):
            down_send(k).wait_send()

    sib_copy(0).wait_send()
    sib_copy(1).wait_send()

    @pl.when(odd)
    def _():
        for k in range(n_part):
            down_near(k).wait_send()
            down_pass(k).wait_send()
            down_pass_far(k).wait_send()
        side_copy(0).wait_send()
        side_copy(1).wait_send()
        for b in range(n_low):
            side_send(b).wait_send()

    @pl.when(s == 1)
    def _():
        for b in range(n_low, n_low + n_away):
            side_send(b).wait_send()

    @pl.when(s == 0)
    def _():
        input_send(last, last % 2).wait_send()

    @pl.when(s != 0)
    def _():
        for h in range(2):
            back_send(last, last % 2, h).wait_send()

    @pl.when(s != last)
    def _():
        for h in range(2):
            hop_send(last, h).wait_send()

    @pl.when(s == last)
    def _():
        for i in range(last):
            result_send(i).wait_send()

    pltpu.make_async_copy(hout.at[0], o_out.at[0], out_r).wait()

    @pl.when(s != 0)
    def _():
        pltpu.make_async_copy(gout.at[0], o_ig.at[0], ig_r).wait()

    for k in range(len(lines)):
        near, across, inner, outer = spots[k]

        @pl.when(inner)
        def _():
            def drain(u, carry):
                to_near, _ = spot_copies(k, u)
                to_near.wait_send()
                return carry

            lax.fori_loop(0, my_units, drain, 0)

    def drain_main(u, carry):
        here, there = finish_copies(u, w_place(u))
        here.wait()
        there.wait()
        return carry

    def drain_down(u, carry):
        here, there = finish_copies(u, d_place(u))
        here.wait()
        there.wait()
        return carry

    def drain_guest(u, carry):
        guest_send(u).wait_send()
        return carry

    def drain_pass(g, carry):
        guest_pass(g).wait()
        return carry

    lax.fori_loop(0, n_main * n_sub, drain_main, 0)
    lax.fori_loop(0, n_returned, drain_pass, 0)

    @pl.when(s == 1)
    def _():
        lax.fori_loop(n_main * n_sub, (n_own - n_away) * n_sub, drain_down, 0)

    @pl.when(s == last - 1)
    def _():
        lax.fori_loop(n_main * n_sub, n_own * n_sub, drain_down, 0)
        lax.fori_loop(n_own * n_sub, (n_own + n_away) * n_sub, drain_guest, 0)

    @pl.when(s == last)
    def _():
        lax.fori_loop(n_main * n_sub, n_own * n_sub, drain_guest, 0)
        lax.fori_loop(n_own * n_sub, n_unit, drain_down, 0)


def line_strides(n_dp):
    chips, stride, strides = n_dp // 2, 2, []
    while chips > 1:
        assert chips % 4 == 0
        strides.append(stride)
        stride, chips = stride * 4, chips // 4
    return strides


def on_device(n_sec, n_dp, patches, cot, positions, counts, gain, bias, wm, bm, sv, wd):
    _, tokens, width = patches.shape
    ff = wm.shape[2]
    lines = line_strides(n_dp)
    n_low = (ff // 2) // 256
    n_own = (width // 256) * (ff // width) + n_low
    n_chunk = n_own + n_low
    n_unit, rows = n_chunk * N_SUB, 128 // N_SUB
    any_spec = pl.BlockSpec(memory_space=pl.ANY)
    vmem_spec = pl.BlockSpec(memory_space=pltpu.VMEM)
    image = (n_sec, tokens, width)
    wide = (n_sec, tokens, ff)
    dma = pltpu.SemaphoreType.DMA
    n_line = len(lines)
    scratch = [
        pltpu.VMEM(image, BF),
        pltpu.VMEM(image, BF),
        pltpu.VMEM(image, BF),
        pltpu.VMEM(wide, BF),
        pltpu.VMEM(wide, BF),
        pltpu.VMEM(wide, BF),
        pltpu.VMEM((width, ff), BF),
        pltpu.VMEM((ff, width), BF),
        pltpu.VMEM((n_sec, 2, tokens, width // 2), F32),
        pltpu.VMEM((1, 8, tokens), F32),
        pltpu.VMEM((n_sec, 8, tokens), F32),
        pltpu.VMEM(image, BF),
        pltpu.VMEM((2, tokens, width), BF),
        pltpu.VMEM((GROUP, GROUP), BF),
        pltpu.VMEM((8, 2 * width), F32),
        pltpu.VMEM((8, width // 2), F32),
        pltpu.VMEM((n_unit, rows, width), BF),
        pltpu.VMEM((n_line, SLOTS, rows, width), BF),
        pltpu.VMEM((n_line, SLOTS, rows, width), BF),
        pltpu.VMEM((n_own + n_low + N_AWAY, N_SUB, rows, width), BF),
        pltpu.VMEM((4, 2 * N_SUB, rows, width), BF),
        pltpu.VMEM((8, width), F32),
        pltpu.VMEM((8, width), F32),
        pltpu.VMEM((n_line, 8, width), F32),
        pltpu.VMEM((n_line, 8, width), F32),
        dma((2,)),
        dma((n_sec, 2)),
        dma((n_sec, 2)),
        dma((n_sec,)),
        dma((n_sec, 2)),
        dma((n_sec, 2)),
        dma((n_sec + 6,)),
        dma,
        dma((4, 4)),
        dma((4, 4)),
        dma((2,)),
        dma((2,)),
        dma,
        dma,
        dma((4,)),
        dma((n_own + n_low + N_AWAY,)),
        dma((n_low + N_AWAY,)),
        dma((n_low + N_AWAY,)),
        dma((n_line, n_unit)),
        dma((n_line, n_unit)),
        dma((n_line, n_unit)),
        dma((n_line, n_unit)),
        dma((n_unit,)),
        dma((n_unit,)),
        dma((n_unit,)),
        dma((n_low * N_SUB,)),
        dma((n_low * N_SUB,)),
        dma((n_low * N_SUB,)),
        dma((1 + 2 * n_line,)),
        dma((1 + 2 * n_line,)),
    ]
    out, ig, gw, gd, small = pl.pallas_call(
        functools.partial(relay, n_sec, lines, tokens, width, ff),
        out_shape=(
            jax.ShapeDtypeStruct((1, tokens, width), BF),
            jax.ShapeDtypeStruct((1, tokens, width), BF),
            jax.ShapeDtypeStruct((width, ff), BF),
            jax.ShapeDtypeStruct((ff // 2, width), BF),
            jax.ShapeDtypeStruct((8, width), F32),
        ),
        in_specs=[any_spec] * 2 + [vmem_spec] * 2 + [any_spec] * 2 + [vmem_spec] * 4,
        out_specs=(any_spec, any_spec, any_spec, any_spec, vmem_spec),
        scratch_shapes=scratch,
        compiler_params=pltpu.CompilerParams(
            collective_id=0, has_side_effects=True, vmem_limit_bytes=63 * 2**20
        ),
    )(patches, cot, positions, counts.reshape(1, 1), wm, wd, gain, bias, bm, sv)
    return (
        out,
        ig,
        small[0:1],
        small[1:2],
        gw.astype(F32)[None],
        small[3:7].reshape(1, ff),
        small[2:3],
        gd.astype(F32)[None],
    )


def solution(mesh):
    n_sec, n_dp = mesh.shape["section"], mesh.shape["dp"]
    images = P(("section", "dp"), None, None)
    row = P("section", None)
    block = P("section", None, None)
    return jax.shard_map(
        functools.partial(on_device, n_sec, n_dp),
        mesh=mesh,
        in_specs=(images, images, images, P(("section", "dp")), row, row, block, row, row, block),
        out_specs=(images, images, row, row, block, row, row, block),
        check_vma=False,
    )
```

```python
import functools

import jax
import jax.numpy as jnp
from jax import lax
from jax.experimental import pallas as pl
from jax.experimental.pallas import tpu as pltpu
from jax.sharding import PartitionSpec as P

HEADS = 12
HEAD_DIM = 64
GROUP = 256
EPS = 1e-06
MESH = pl.DeviceIdType.MESH
BF = jnp.bfloat16
F32 = jnp.float32
HI = lax.Precision.HIGHEST
LAG_SIB, LAG_ONE, LAG_TWO, LAG_END = 1, 2, 4, 6
N_SUB = 2
SLOTS = 8
N_AWAY = 1


def nn(a, b, precision=None):
    return lax.dot_general(a, b, (((1,), (0,)), ((), ())), precision=precision, preferred_element_type=F32)


def nt(a, b, precision=None):
    return lax.dot_general(a, b, (((1,), (1,)), ((), ())), precision=precision, preferred_element_type=F32)


def tn(a, b, precision=None):
    return lax.dot_general(a, b, (((0,), (0,)), ((), ())), precision=precision, preferred_element_type=F32)


def normalise(x):
    centered = x - jnp.mean(x, axis=-1, keepdims=True)
    scale = lax.rsqrt(jnp.mean(centered * centered, axis=-1, keepdims=True) + EPS)
    return centered * scale, scale


def relay(
    n_sec, lines, tokens, width, ff,
    patches, cot, positions, counts, wm, wd, gain, bias, bm, sv,
    o_out, o_ig, o_w, o_d, o_small,
    hin, gin, act, big1, big2, big3, wv, dv, cs, tab, tabs, hout, gout, perm, bqk, freq,
    mine, zin, pin, sib, tmp, sg, sg_sib, sg_one, sg_two,
    w_sem, hin_r, gin_r, tab_r, hop_s, gop_s, ini_s, cot_r, wd_s, wd_r, det_s, det_r, out_r, ig_r,
    sib_s, sib_r, low_s, mine_r, za_s, zin_r, pb_s, pin_r, fin_l, fin_s, fin_r, guest_r, pass_s, pass_r, sg_s, sg_r,
):
    s = lax.axis_index("section")
    d = lax.axis_index("dp")
    core = lax.rem(d, 2)
    other = d + 1 - 2 * core
    even = lax.rem(s, 2) == 0
    odd = lax.rem(s, 2) == 1
    last = n_sec - 1
    half = tokens // 2
    n_main = (width // 256) * (ff // width)
    n_low = (ff // 2) // 256
    n_own = n_main + n_low
    n_chunk = n_own + n_low
    n_away = N_AWAY
    limit = jnp.where(
        s == 0, n_main, jnp.where(s == 1, n_own - n_away, jnp.where(s == last, n_chunk, n_own + n_away))
    )
    n_side = jnp.where(s == 1, n_low + n_away, jnp.where(s == last, n_low, 0))
    n_sub = N_SUB
    score_scale = HEAD_DIM ** (-0.5)

    def to_section(target):
        return {"section": target}

    def to_dp(target):
        return {"dp": target}

    def remote(src, dst, send, recv, device):
        return pltpu.make_async_remote_copy(
            src_ref=src, dst_ref=dst, send_sem=send, recv_sem=recv, device_id=device, device_id_type=MESH
        )

    spots = []
    for stride in lines:
        pos = lax.rem(d // stride, 4)
        near = d + (1 - 2 * lax.rem(pos, 2)) * stride
        across = d + (3 - 2 * pos) * stride
        inner = (pos == 1) | (pos == 2)
        outer = (pos == 0) | (pos == 3)
        spots.append((near, across, inner, outer))

    barrier = pltpu.get_barrier_semaphore()
    for step in range(1, n_sec):
        pl.semaphore_signal(barrier, inc=1, device_id=to_section(lax.rem(s + step, n_sec)), device_id_type=MESH)
    pl.semaphore_signal(barrier, inc=1, device_id=to_dp(other), device_id_type=MESH)
    for near, across, inner, outer in spots:
        pl.semaphore_signal(barrier, inc=1, device_id=to_dp(near), device_id_type=MESH)

        @pl.when(inner)
        def _():
            pl.semaphore_signal(barrier, inc=1, device_id=to_dp(across), device_id_type=MESH)

    load_w = pltpu.make_async_copy(wm.at[0], wv, w_sem.at[0])
    load_d = pltpu.make_async_copy(wd.at[0], dv.at[pl.ds(ff // 2, ff // 2)], w_sem.at[1])
    load_w.start()

    @pl.when(odd)
    def _():
        load_d.start()

    peers = n_sec + len(spots)
    for near, across, inner, outer in spots:
        peers = peers + jnp.where(inner, 1, 0)
    tab[...] = jnp.zeros_like(tab)
    tab[0, 0:2, :] = positions[0].astype(F32)
    tab[0, 2:3, :] = jnp.broadcast_to(counts[...].astype(F32), (1, tokens))
    pl.semaphore_wait(barrier, peers)

    tab_sends = []
    for step in range(1, n_sec):
        tab_sends.append(
            remote(tab.at[0], tabs.at[s], ini_s.at[step - 1], tab_r.at[s], to_section(lax.rem(s + step, n_sec)))
        )
    for send in tab_sends:
        send.start()
    tab_own = pltpu.make_async_copy(tab.at[0], tabs.at[s], tab_r.at[s])
    tab_own.start()
    def rows_of(h):
        return pl.ds(h * half, half)

    def patch_send(h):
        r = rows_of(h)
        return remote(patches.at[0, r], hin.at[s, r], ini_s.at[n_sec + h], hin_r.at[s, h], to_section(0))

    def patch_own(h):
        r = rows_of(h)
        return pltpu.make_async_copy(patches.at[0, r], hin.at[0, r], hin_r.at[0, h])

    def cot_send(h):
        r = rows_of(h)
        return remote(cot.at[0, r], gin.at[s, r], ini_s.at[n_sec + 2 + h], gin_r.at[s, h], to_section(last))

    def cot_own(h):
        r = rows_of(h)
        return pltpu.make_async_copy(cot.at[0, r], gin.at[last, r], gin_r.at[last, h])

    cot_out = remote(cot.at[0], gout.at[0], ini_s.at[n_sec + 2], cot_r, to_section(last - 1))

    def cot_on(h):
        r = rows_of(h)
        return remote(gout.at[0, r], gin.at[0, r], ini_s.at[n_sec + 4 + h], gin_r.at[0, h], to_section(last))

    @pl.when(s == 0)
    def _():
        for h in range(2):
            patch_own(h).start()

    @pl.when(s != 0)
    def _():
        for h in range(2):
            patch_send(h).start()

    @pl.when((s != 0) & (s != last))
    def _():
        for h in range(2):
            cot_send(h).start()

    @pl.when(s == last)
    def _():
        for h in range(2):
            cot_own(h).start()

    near0 = spots[0][0]
    side = lax.rem(d // lines[0], 2)
    n_part = 4
    part = (ff // 2) // 4 // n_part

    def down_rows(which_side, which_core, k):
        start = (which_side * 2 + which_core) * (n_part * part) + k * part
        return pl.ds(pl.multiple_of(start, part), part)

    def down_send(k):
        rows = down_rows(side, core, k)
        return remote(wd.at[0, rows], dv.at[rows], wd_s.at[0, k], wd_r.at[0, k], to_section(lax.rem(s + 1, n_sec)))

    def down_near(k):
        rows = down_rows(side, core, k)
        return remote(dv.at[rows], dv.at[rows], wd_s.at[1, k], wd_r.at[1, k], to_dp(near0))

    def down_pass(k):
        rows = down_rows(side, core, k)
        return remote(dv.at[rows], dv.at[rows], wd_s.at[2, k], wd_r.at[2, k], to_dp(other))

    def down_pass_far(k):
        rows = down_rows(1 - side, core, k)
        return remote(dv.at[rows], dv.at[rows], wd_s.at[3, k], wd_r.at[3, k], to_dp(other))

    n_direct = n_part // 2

    def down_out(k):
        to = hout.at[last, pl.ds((k - n_direct) * part, part)]
        send = remote(wd.at[0, down_rows(side, core, k)], to, wd_s.at[0, k], det_r.at[k - n_direct], to_section(last - 1))
        return send

    def down_on(k):
        held = hout.at[last, pl.ds((k - n_direct) * part, part)]
        to = dv.at[down_rows(side, core, k)]
        return remote(held, to, det_s.at[k - n_direct], wd_r.at[0, k], to_section(1))

    @pl.when(s == 0)
    def _():
        for k in range(n_direct):
            down_send(k).start()
            down_out(k + n_direct).start()

    @pl.when(s == last - 1)
    def _():
        for k in range(n_direct, n_part):
            down_out(k).wait_recv()
            down_on(k).start()
        for k in range(n_part):
            down_send(k).start()

    def table(i):
        pltpu.make_async_copy(tab.at[0], tabs.at[i], tab_r.at[i]).wait()
        angle = nn(jnp.transpose(tabs[i]), freq[...], HI)
        cs[i, 0] = jnp.cos(angle)
        cs[i, 1] = jnp.sin(angle)

    ahead = (s == 0) & (core == 0)

    @pl.when(even)
    def _():
        freq[...] = jnp.zeros_like(freq)
        freq[0:1, :] = sv[:, : width // 2]
        freq[1:2, :] = sv[:, width // 2 :]

        def early(i, carry):
            @pl.when((i == 0) | jnp.logical_not(ahead))
            def _():
                table(i)

            return carry

        lax.fori_loop(0, n_sec, early, 0)

    @pl.when(odd)
    def _():
        for i in range(n_sec):
            pltpu.make_async_copy(tab.at[0], tabs.at[i], tab_r.at[i]).wait()

    sg[...] = jnp.zeros_like(sg)

    @pl.when(even)
    def _():
        old = lax.broadcasted_iota(jnp.int32, (GROUP, GROUP), 0)
        new = lax.broadcasted_iota(jnp.int32, (GROUP, GROUP), 1)
        source = ((new & 127) >> 5) * 64 + (new >> 7) * 32 + (new & 31)
        perm[...] = jnp.where(old == source, 1.0, 0.0).astype(BF)
        moved = perm[...].astype(F32)
        for block in range(2 * width // GROUP):
            columns = slice(block * GROUP, (block + 1) * GROUP)
            row = jnp.broadcast_to(bm[:, columns], (8, GROUP))
            bqk[:, columns] = nn(row, moved, HI)

    load_w.wait()

    @pl.when(even)
    def _():
        moved = perm[...]
        for block in range(2 * width // GROUP):
            columns = slice(block * GROUP, (block + 1) * GROUP)
            wv[:, columns] = nn(wv[:, columns], moved).astype(BF)

    @pl.when(s == last - 1)
    def _():
        cot_out.wait_recv()
        for h in range(2):
            cot_on(h).start()
        for k in range(n_direct, n_part):
            down_on(k).wait_send()

    @pl.when(odd)
    def _():
        for k in [0, 2, 1, 3]:
            down_send(k).wait_recv()
            down_near(k).start()
            down_pass(k).start()

    lane = lax.broadcasted_iota(jnp.int32, (1, GROUP), 1)
    q_masks = [((lane & 127) >> 5) == e for e in range(4)]
    v_masks = [(lane >> 6) == e for e in range(4)]
    zero_low = jnp.zeros((), BF)

    def count_of(i):
        return tabs[i, 2:3, 0:1]

    def row_mask(i):
        ids = lax.broadcasted_iota(jnp.int32, (tokens, 1), 0).astype(F32)
        return jnp.where(ids < count_of(i), 1.0, 0.0)

    def key_mask(i):
        ids = lax.broadcasted_iota(jnp.int32, (1, tokens), 1).astype(F32)
        return ids < count_of(i)

    n_group = width // GROUP
    pairs = width // 2 // n_group

    def attention_forward(i, slot):
        x = hin[i].astype(F32)
        xhat, _ = normalise(x)
        a = (xhat * gain[...] + bias[...]).astype(BF)
        act[i] = a
        keys_on = key_mask(i)
        for g in range(n_group):
            cosine = cs[i, 0, :, g * pairs : (g + 1) * pairs]
            sine = cs[i, 1, :, g * pairs : (g + 1) * pairs]
            turned = []
            for which in range(2):
                lo = which * width + g * GROUP
                t = nn(a, wv[:, lo : lo + GROUP]) + bqk[0:1, lo : lo + GROUP]
                t1, t2 = t[:, :128], t[:, 128:]
                r = jnp.concatenate([t1 * cosine - t2 * sine, t1 * sine + t2 * cosine], axis=1)
                r = (r * score_scale if which == 0 else r).astype(BF)
                big1[i, :, lo : lo + GROUP] = r
                turned.append(r)
            lo = 2 * width + g * GROUP
            value = (nn(a, wv[:, lo : lo + GROUP]) + bm[:, lo : lo + GROUP]).astype(BF)
            big1[i, :, lo : lo + GROUP] = value
            query, key = turned
            weights = []
            for e in range(4):
                scores = nt(jnp.where(q_masks[e], query, zero_low), key)
                scores = jnp.where(keys_on, scores, -1e30)
                top = jnp.max(scores, axis=-1, keepdims=True)
                p = jnp.exp(scores - top)
                p = (p * (1.0 / jnp.sum(p, axis=-1, keepdims=True))).astype(BF)
                big2[i, :, (4 * g + e) * tokens : (4 * g + e + 1) * tokens] = p
                weights.append(p)
            stacked = jnp.concatenate([jnp.where(v_masks[e], value, zero_low) for e in range(4)], axis=0)
            context = nn(jnp.concatenate(weights, axis=1), stacked)
            lo = 3 * width + g * GROUP
            big1[i, :, lo : lo + GROUP] = context.astype(BF)
        branch = nn(big1[i, :, 3 * width :], wv[:, 3 * width :]) + bm[:, 3 * width :]
        hout[slot] = (x + row_mask(i) * branch).astype(BF)

    def norm_backward(x, g_up, gact):
        xhat, scale = normalise(x.astype(F32))
        sg[0:1, :] += jnp.sum(gact * xhat, axis=0, keepdims=True)
        sg[1:2, :] += jnp.sum(gact, axis=0, keepdims=True)
        gn = gact * gain[...]
        inside = gn - jnp.mean(gn, axis=-1, keepdims=True) - xhat * jnp.mean(gn * xhat, axis=-1, keepdims=True)
        return g_up + scale * inside

    def attention_backward(i, slot):
        g_up = gin[i].astype(F32)
        gb = row_mask(i) * g_up
        low = gb.astype(BF)
        dctx_all = nt(low, wv[:, 3 * width :]).astype(BF)
        for g in range(n_group):
            qlo, klo, vlo = g * GROUP, width + g * GROUP, 2 * width + g * GROUP
            query = big1[i, :, qlo : qlo + GROUP]
            key = big1[i, :, klo : klo + GROUP]
            value = big1[i, :, vlo : vlo + GROUP]
            dctx = dctx_all[:, g * GROUP : (g + 1) * GROUP]
            clo = 3 * width + g * GROUP
            both = dctx.astype(F32) * big1[i, :, clo : clo + GROUP].astype(F32)
            d_stack, p_stack, gs_list = [], [], []
            for e in range(4):
                d_e = jnp.where(v_masks[e], dctx, zero_low)
                gw = nt(d_e, value)
                p_low = big2[i, :, (4 * g + e) * tokens : (4 * g + e + 1) * tokens]
                inside = jnp.sum(jnp.where(v_masks[e], both, 0.0), axis=-1, keepdims=True)
                gs_list.append((p_low.astype(F32) * (gw - inside)).astype(BF))
                d_stack.append(d_e)
                p_stack.append(p_low)
            key_low = key * jnp.asarray(score_scale, BF)
            k_stack = jnp.concatenate([jnp.where(q_masks[e], key_low, zero_low) for e in range(4)], axis=0)
            q_stack = jnp.concatenate([jnp.where(q_masks[e], query, zero_low) for e in range(4)], axis=0)
            dq = nn(jnp.concatenate(gs_list, axis=1), k_stack)
            dk = tn(jnp.concatenate(gs_list, axis=0), q_stack)
            dval = tn(jnp.concatenate(p_stack, axis=0), jnp.concatenate(d_stack, axis=0))
            cosine = cs[i, 0, :, g * pairs : (g + 1) * pairs]
            sine = cs[i, 1, :, g * pairs : (g + 1) * pairs]
            turn = jnp.zeros((tokens, pairs), F32)
            for lo, grad, held, size in ((qlo, dq, query, 1.0 / score_scale), (klo, dk, key, 1.0)):
                g1, g2 = grad[:, :128], grad[:, 128:]
                r = held.astype(F32)
                turn = turn + (g2 * r[:, :128] - g1 * r[:, 128:]) * size
                raw = jnp.concatenate([g1 * cosine + g2 * sine, g2 * cosine - g1 * sine], axis=1).astype(BF)
                big3[i, :, lo : lo + GROUP] = raw
            big3[i, :, vlo : vlo + GROUP] = dval.astype(BF)
            sums = nn(tabs[i], turn, HI)
            at = g * pairs
            sg[2:3, at : at + pairs] += sums[0:1]
            at = width // 2 + g * pairs
            sg[2:3, at : at + pairs] += sums[1:2]
        gact = nt(big3[i, :, : 3 * width], wv[:, : 3 * width])
        gout[slot] = norm_backward(hin[i], g_up, gact).astype(BF)
        gin[i] = low

    piece = 512

    def down_ready(i):
        @pl.when(i == 0)
        def _():
            load_d.wait()
            for k in range(n_part):
                down_near(k).wait_recv()
                down_pass_far(k).start()
            for k in range(n_part):
                down_pass(k).wait_recv()
                down_pass_far(k).wait_recv()

    def dense_forward(i, h):
        r = slice(h * half, (h + 1) * half)
        x = hin[i, r].astype(F32)
        xhat, _ = normalise(x)
        a = (xhat * gain[...] + bias[...]).astype(BF)
        act[i, r] = a
        for k in range(ff // piece):
            lo = k * piece
            pre = nn(a, wv[:, lo : lo + piece]) + bm[:, lo : lo + piece]
            cdf = 0.5 + 0.5 * lax.erf(pre * (0.5**0.5))
            big1[i, r, lo : lo + piece] = (pre * cdf).astype(BF)
            pdf = jnp.exp(-0.5 * (pre * pre)) * 0.3989422804014327
            big2[i, r, lo : lo + piece] = (cdf + pre * pdf).astype(BF)
        if h == 0:
            down_ready(i)
        branch = nn(big1[i, r], dv[...]) + sv[...]
        hout[i, r] = (x + row_mask(i)[r] * branch).astype(BF)

    def dense_backward(i, slot):
        g_up = gin[i].astype(F32)
        gb = row_mask(i) * g_up
        low = gb.astype(BF)
        for k in range(ff // width):
            for m in range(width // GROUP):
                lo = k * width + m * GROUP
                gh = nt(low, dv[lo : lo + GROUP, :])
                gpre = (gh * big2[i, :, lo : lo + GROUP].astype(F32)).astype(BF)
                big3[i, :, lo : lo + GROUP] = gpre
        gact = nt(big3[i], wv[...])
        gout[slot] = norm_backward(hin[i], g_up, gact).astype(BF)
        gin[i] = low

    def hop_send(i, h):
        r = rows_of(h)
        to = to_section(lax.rem(s + 1, n_sec))
        return remote(hout.at[i, r], hin.at[i, r], hop_s.at[i, h], hin_r.at[i, h], to)

    def result_send(i):
        return remote(hout.at[i], o_out.at[0], hop_s.at[i, 0], out_r, to_section(i))

    def back_send(i, slot, h):
        r = rows_of(h)
        to = to_section(lax.rem(s + last, n_sec))
        return remote(gout.at[slot, r], gin.at[i, r], gop_s.at[i, h], gin_r.at[i, h], to)

    def input_send(i, slot):
        return remote(gout.at[slot], o_ig.at[0], gop_s.at[i, 0], ig_r, to_section(i))

    def send_hop(i, h):
        @pl.when((s != last) & (i >= 1))
        def _():
            hop_send(i - 1, h).wait_send()

        @pl.when(s != last)
        def _():
            hop_send(i, h).start()

    def send_back(i, slot, h):
        @pl.when((s != 0) & (i >= 1))
        def _():
            back_send(i - 1, 1 - slot, h).wait_send()

        @pl.when(s != 0)
        def _():
            back_send(i, slot, h).start()

    def forward(i):
        @pl.when(even)
        def _():
            for h in range(2):
                hop_send(i, h).wait_recv()
            attention_forward(i, i)
            for h in range(2):
                send_hop(i, h)

        @pl.when(odd)
        def _():
            for h in range(2):
                hop_send(i, h).wait_recv()
                dense_forward(i, h)
                send_hop(i, h)

    def backward(i):
        slot = lax.rem(i, 2)

        @pl.when((i == 0) & (s == last - 1))
        def _():
            for h in range(2):
                cot_on(h).wait_send()

        @pl.when((i == 2) & (s == 0))
        def _():
            pltpu.make_async_copy(gout.at[slot], o_ig.at[0], ig_r).wait()

        @pl.when(even)
        def _():
            for h in range(2):
                back_send(i, slot, h).wait_recv()
            attention_backward(i, slot)
            for h in range(2):
                send_back(i, slot, h)

        @pl.when(odd)
        def _():
            for h in range(2):
                back_send(i, slot, h).wait_recv()
            dense_backward(i, slot)
            for h in range(2):
                send_back(i, slot, h)

        @pl.when((s == 0) & (i >= 2))
        def _():
            input_send(i - 1, 1 - slot).wait_send()

        @pl.when((s == 0) & (i != 0))
        def _():
            input_send(i, slot).start()

        @pl.when((s == 0) & (i == 0))
        def _():
            pltpu.make_async_copy(gout.at[slot], o_ig.at[0], ig_r).start()

    def tick(j, carry):
        is_forward = jnp.where(s == last, lax.rem(j, 2) == 0, j < n_sec)
        i = jnp.where(s == last, j // 2, lax.rem(j, n_sec))

        @pl.when(is_forward)
        def _():
            forward(i)

        @pl.when((s == 0) & (j == 0))
        def _():
            cot_out.start()

        @pl.when(ahead & (j == 0))
        def _():
            lax.fori_loop(1, n_sec, lambda i, carry: (table(i), carry)[1], 0)

        @pl.when(jnp.logical_not(is_forward))
        def _():
            backward(i)

        return carry

    lax.fori_loop(0, 2 * n_sec, tick, 0)

    @pl.when(s == last)
    def _():
        for i in range(last):
            result_send(i).start()
        pltpu.make_async_copy(hout.at[last], o_out.at[0], out_r).start()

    def bias_sums():
        ones = jnp.ones((16, n_sec * tokens), BF)

        def column_sum(held):
            return nn(ones, held.reshape(n_sec * tokens, width))[0:1]

        masked = column_sum(gin[...])
        for k in range(3):
            sg[3 + k : 4 + k, :] = column_sum(big3[:, :, k * width : (k + 1) * width])

        @pl.when(odd)
        def _():
            sg[2:3, :] = masked
            sg[6:7, :] = column_sum(big3[:, :, 3 * width :])

        @pl.when(even)
        def _():
            sg[6:7, :] = masked
            back = perm[...].astype(F32)
            for block in range(2 * width // GROUP):
                row = 3 + block * GROUP // width
                lo = block * GROUP % width
                part = jnp.broadcast_to(sg[row : row + 1, lo : lo + GROUP], (8, GROUP))
                sg[row : row + 1, lo : lo + GROUP] = nt(part, back, HI)[0:1]

    my_half = pl.ds(core * n_sub, n_sub)
    their_half = pl.ds((1 - core) * n_sub, n_sub)

    def is_own(c):
        after = ((s == 1) & (c >= n_main) & (c < n_own - n_away)) | ((s == last) & (c >= n_own) & (c < n_chunk))
        return ((c >= 0) & (c < n_main)) | after

    def is_guest(c):
        return ((s >= 2) & (c >= n_main) & (c < n_own)) | ((s == last - 1) & (c >= n_own) & (c < n_own + n_away))

    def sib_slot(c):
        return jnp.where(c >= n_own, c - n_low, c)

    def sib_copy(c):
        slot = lax.rem(c, 2)
        at = sib_slot(c)
        return remote(tmp.at[slot, their_half], sib.at[at], sib_s.at[slot], sib_r.at[at], to_dp(other))

    def side_copy(b):
        slot = 2 + lax.rem(b, 2)
        at = n_own + b
        return remote(tmp.at[slot, their_half], sib.at[at], sib_s.at[slot], sib_r.at[at], to_dp(other))

    def side_send(b):
        to = jnp.where((s == 1) & (b < n_low), last, last - 1)
        return remote(
            sib.at[n_own + b], mine.at[pl.ds((n_main + b) * n_sub, n_sub)], low_s.at[b], mine_r.at[b], to_section(to)
        )

    def make_down(slot, row):
        rows = pl.ds(pl.multiple_of(row, 256), 256)
        left = big1[:, :, rows].reshape(n_sec * tokens, 256)
        right = gin[...].reshape(n_sec * tokens, width)
        keep(slot, tn(left, right))

    def keep(slot, block):
        tmp[slot] = block.astype(BF).reshape(2 * n_sub, half // n_sub, width)

    def make_side(b):
        slot = 2 + lax.rem(b, 2)

        @pl.when(b >= 2)
        def _():
            side_copy(b - 2).wait_send()

        make_down(slot, jnp.where(b < n_low, b, b + n_low - n_away) * 256)
        side_copy(b).start()

    def send_side(b):
        slot = 2 + lax.rem(b, 2)
        at = n_own + b
        side_copy(b).wait_recv()
        sib[at] = (tmp[slot, my_half].astype(F32) + sib[at].astype(F32)).astype(BF)
        side_send(b).start()

    def make_block(c):
        slot = lax.rem(c, 2)

        @pl.when(c >= 2)
        def _():
            sib_copy(c - 2).wait_send()

        column = lax.rem(c, ff // width)
        row = c // (ff // width)
        from_act = (c < n_main) & (odd | (column < 3))

        @pl.when(from_act)
        def _():
            rows = pl.ds(pl.multiple_of(row * 256, 256), 256)
            columns = pl.ds(pl.multiple_of(column * width, width), width)
            left = act[:, :, rows].reshape(n_sec * tokens, 256)
            right = big3[:, :, columns].reshape(n_sec * tokens, width)
            keep(slot, tn(left, right))

        @pl.when(from_act & even & (column < 2))
        def _():
            back = perm[...]
            held = tmp[slot].reshape(2 * half, width)
            keep(
                slot,
                jnp.concatenate(
                    [nt(held[:, k * GROUP : (k + 1) * GROUP], back) for k in range(width // GROUP)], axis=1
                ),
            )

        @pl.when(jnp.logical_not(from_act))
        def _():
            upper = ff // 2 + jnp.where(s == last, c - n_own, c - n_main) * 256
            make_down(slot, jnp.where(even, 3 * width + row * 256, upper))

        sib_copy(c).start()

    def spot_copies(k, u):
        near, across, inner, outer = spots[k]
        held = lax.rem(u, SLOTS)
        to_near = remote(mine.at[u], zin.at[k, held], za_s.at[k, u], zin_r.at[k, u], to_dp(near))
        to_across = remote(zin.at[k, held], pin.at[k, held], pb_s.at[k, u], pin_r.at[k, u], to_dp(across))
        return to_near, to_across

    piece_rows = half // n_sub

    def w_place(u):
        c = u // n_sub
        row = c // (ff // width)
        column = lax.rem(c, ff // width)
        start = row * 256 + core * half + lax.rem(u, n_sub) * piece_rows
        rows = pl.ds(pl.multiple_of(start, piece_rows), piece_rows)
        columns = pl.ds(pl.multiple_of(column * width, width), width)
        return o_w.at[rows, columns]

    def d_rows(block, sub):
        start = block * 256 + core * half + sub * piece_rows
        return o_d.at[pl.ds(pl.multiple_of(start, piece_rows), piece_rows), :]

    def d_place(u):
        c = u // n_sub
        late = jnp.where(s == last, c - n_own, c - n_own + n_low - n_away)
        return d_rows(jnp.where(c < n_own, c - n_main, late), lax.rem(u, n_sub))

    def finish_copies(u, place):
        here = pltpu.make_async_copy(mine.at[u], place, fin_l.at[u])
        there = remote(mine.at[u], place, fin_s.at[u], fin_r.at[u], to_dp(other))
        return here, there

    def is_away(u):
        return ((s == last) & (u < n_own * n_sub)) | ((s == last - 1) & (u >= n_own * n_sub))

    def guest_send(u):
        at = jnp.where(s == last, u - n_main * n_sub, u - n_own * n_sub)
        to = jnp.where(s == last, 0, 1)
        return remote(mine.at[u], d_place(u), fin_s.at[u], guest_r.at[at], to_section(to))

    def returned(g):
        block = g // n_sub + jnp.where(s == 0, 0, n_low - n_away)
        return d_rows(block, lax.rem(g, n_sub))

    def guest_take(g):
        return remote(mine.at[0], returned(g), pass_s.at[g], guest_r.at[g], to_dp(other))

    def guest_pass(g):
        return remote(returned(g), returned(g), pass_s.at[g], pass_r.at[g], to_dp(other))

    n_returned = jnp.where(s == 0, n_low * n_sub, jnp.where(s == 1, n_away * n_sub, 0))

    def finish(u):
        @pl.when(u < n_main * n_sub)
        def _():
            here, there = finish_copies(u, w_place(u))
            here.start()
            there.start()

        @pl.when((u >= n_main * n_sub) & jnp.logical_not(is_away(u)))
        def _():
            here, there = finish_copies(u, d_place(u))
            here.start()
            there.start()

        @pl.when((u >= n_main * n_sub) & is_away(u))
        def _():
            guest_send(u).start()

    small_sib = remote(sg, sg_sib, sg_s.at[0], sg_r.at[0], to_dp(other))

    def small_copies(k):
        near, across, inner, outer = spots[k]
        to_near = remote(sg, sg_one.at[k], sg_s.at[1 + 2 * k], sg_r.at[1 + 2 * k], to_dp(near))
        to_across = remote(sg_one.at[k], sg_two.at[k], sg_s.at[2 + 2 * k], sg_r.at[2 + 2 * k], to_dp(across))
        return to_near, to_across

    n_unit = n_chunk * n_sub
    my_units = limit * n_sub
    steps = my_units + n_sub * LAG_SIB + len(lines) * LAG_END + 1

    def sum_step(t, carry):
        c = t // n_sub
        first = lax.rem(t, n_sub) == 0
        second = lax.rem(t, n_sub) == 1

        @pl.when(first & is_own(c))
        def _():
            make_block(c)

        @pl.when(second & (c < n_side))
        def _():
            make_side(c)

        c1 = c - LAG_SIB

        @pl.when(first & is_own(c1))
        def _():
            slot = lax.rem(c1, 2)
            at = sib_slot(c1)
            sib_copy(c1).wait_recv()
            mine[pl.ds(c1 * n_sub, n_sub)] = (tmp[slot, my_half].astype(F32) + sib[at].astype(F32)).astype(BF)

        @pl.when(second & (c1 >= 0) & (c1 < n_side))
        def _():
            send_side(c1)

        @pl.when(first & is_guest(c1))
        def _():
            side_send(c1 - n_main).wait_recv()

        @pl.when(t == 5)
        def _():
            bias_sums()
            small_sib.start()

        @pl.when(t == 8)
        def _():
            small_sib.wait()
            sg[...] = sg[...] + sg_sib[...]

        for k in range(len(lines)):
            near, across, inner, outer = spots[k]
            small_near, small_across = small_copies(k)
            at = 8 + 9 * k

            @pl.when(outer & (t == at))
            def _():
                small_near.start()

            @pl.when(inner & (t == at + 3))
            def _():
                small_near.wait_recv()
                sg_one[k] = sg[...] + sg_one[k]
                small_across.start()

            @pl.when(inner & (t == at + 6))
            def _():
                small_across.wait()
                sg[...] = sg_one[k] + sg_two[k]
                small_near.start()
                small_near.wait_send()

            @pl.when(outer & (t == at + 9))
            def _():
                small_near.wait()
                sg[...] = sg_one[k]

        for k in range(len(lines)):
            near, across, inner, outer = spots[k]
            base = LAG_SIB * n_sub + k * LAG_END
            u0 = t - base

            @pl.when(outer & (u0 >= 0) & (u0 < my_units))
            def _():
                to_near, _ = spot_copies(k, u0)
                to_near.start()

            u2 = t - base - LAG_ONE

            @pl.when(inner & (u2 >= 0) & (u2 < my_units))
            def _():
                to_near, to_across = spot_copies(k, u2)
                to_near.wait_recv()
                held = lax.rem(u2, SLOTS)
                zin[k, held] = (mine[u2].astype(F32) + zin[k, held].astype(F32)).astype(BF)
                to_across.start()

            u3 = t - base - LAG_TWO

            @pl.when(inner & (u3 >= 0) & (u3 < my_units))
            def _():
                to_near, to_across = spot_copies(k, u3)
                to_across.wait()
                held = lax.rem(u3, SLOTS)
                mine[u3] = (zin[k, held].astype(F32) + pin[k, held].astype(F32)).astype(BF)
                to_near.start()
                if k == len(lines) - 1:
                    finish(u3)

            u4 = t - base - LAG_END

            @pl.when(outer & (u4 >= 0) & (u4 < my_units))
            def _():
                to_near, _ = spot_copies(k, u4)
                to_near.wait()
                mine[u4] = zin[k, lax.rem(u4, SLOTS)]
                if k == len(lines) - 1:
                    finish(u4)

        return carry

    lax.fori_loop(0, steps, sum_step, 0)

    def take(g, carry):
        guest_take(g).wait_recv()
        guest_pass(g).start()
        return carry

    lax.fori_loop(0, n_returned, take, 0)
    o_small[...] = sg[...]

    for send in tab_sends:
        send.wait_send()

    @pl.when(s != 0)
    def _():
        for h in range(2):
            patch_send(h).wait_send()

    @pl.when(s == 0)
    def _():
        cot_out.wait_send()

    @pl.when((s != 0) & (s != last))
    def _():
        for h in range(2):
            cot_send(h).wait_send()

    @pl.when(even)
    def _():
        for k in range(n_part):
            down_send(k).wait_send()

    sib_copy(0).wait_send()
    sib_copy(1).wait_send()

    @pl.when(odd)
    def _():
        for k in range(n_part):
            down_near(k).wait_send()
            down_pass(k).wait_send()
            down_pass_far(k).wait_send()
        side_copy(0).wait_send()
        side_copy(1).wait_send()
        for b in range(n_low):
            side_send(b).wait_send()

    @pl.when(s == 1)
    def _():
        for b in range(n_low, n_low + n_away):
            side_send(b).wait_send()

    @pl.when(s == 0)
    def _():
        input_send(last, last % 2).wait_send()

    @pl.when(s != 0)
    def _():
        for h in range(2):
            back_send(last, last % 2, h).wait_send()

    @pl.when(s != last)
    def _():
        for h in range(2):
            hop_send(last, h).wait_send()

    @pl.when(s == last)
    def _():
        for i in range(last):
            result_send(i).wait_send()

    pltpu.make_async_copy(hout.at[0], o_out.at[0], out_r).wait()

    @pl.when(s != 0)
    def _():
        pltpu.make_async_copy(gout.at[0], o_ig.at[0], ig_r).wait()

    for k in range(len(lines)):
        near, across, inner, outer = spots[k]

        @pl.when(inner)
        def _():
            def drain(u, carry):
                to_near, _ = spot_copies(k, u)
                to_near.wait_send()
                return carry

            lax.fori_loop(0, my_units, drain, 0)

    def drain_main(u, carry):
        here, there = finish_copies(u, w_place(u))
        here.wait()
        there.wait()
        return carry

    def drain_down(u, carry):
        here, there = finish_copies(u, d_place(u))
        here.wait()
        there.wait()
        return carry

    def drain_guest(u, carry):
        guest_send(u).wait_send()
        return carry

    def drain_pass(g, carry):
        guest_pass(g).wait()
        return carry

    lax.fori_loop(0, n_main * n_sub, drain_main, 0)
    lax.fori_loop(0, n_returned, drain_pass, 0)

    @pl.when(s == 1)
    def _():
        lax.fori_loop(n_main * n_sub, (n_own - n_away) * n_sub, drain_down, 0)

    @pl.when(s == last - 1)
    def _():
        lax.fori_loop(n_main * n_sub, n_own * n_sub, drain_down, 0)
        lax.fori_loop(n_own * n_sub, (n_own + n_away) * n_sub, drain_guest, 0)

    @pl.when(s == last)
    def _():
        lax.fori_loop(n_main * n_sub, n_own * n_sub, drain_guest, 0)
        lax.fori_loop(n_own * n_sub, n_unit, drain_down, 0)


def line_strides(n_dp):
    chips, stride, strides = n_dp // 2, 2, []
    while chips > 1:
        assert chips % 4 == 0
        strides.append(stride)
        stride, chips = stride * 4, chips // 4
    return strides


def on_device(n_sec, n_dp, patches, cot, positions, counts, gain, bias, wm, bm, sv, wd):
    _, tokens, width = patches.shape
    ff = wm.shape[2]
    lines = line_strides(n_dp)
    n_low = (ff // 2) // 256
    n_own = (width // 256) * (ff // width) + n_low
    n_chunk = n_own + n_low
    n_unit, rows = n_chunk * N_SUB, 128 // N_SUB
    any_spec = pl.BlockSpec(memory_space=pl.ANY)
    vmem_spec = pl.BlockSpec(memory_space=pltpu.VMEM)
    image = (n_sec, tokens, width)
    wide = (n_sec, tokens, ff)
    dma = pltpu.SemaphoreType.DMA
    n_line = len(lines)
    scratch = [
        pltpu.VMEM(image, BF),
        pltpu.VMEM(image, BF),
        pltpu.VMEM(image, BF),
        pltpu.VMEM(wide, BF),
        pltpu.VMEM(wide, BF),
        pltpu.VMEM(wide, BF),
        pltpu.VMEM((width, ff), BF),
        pltpu.VMEM((ff, width), BF),
        pltpu.VMEM((n_sec, 2, tokens, width // 2), F32),
        pltpu.VMEM((1, 8, tokens), F32),
        pltpu.VMEM((n_sec, 8, tokens), F32),
        pltpu.VMEM(image, BF),
        pltpu.VMEM((2, tokens, width), BF),
        pltpu.VMEM((GROUP, GROUP), BF),
        pltpu.VMEM((8, 2 * width), F32),
        pltpu.VMEM((8, width // 2), F32),
        pltpu.VMEM((n_unit, rows, width), BF),
        pltpu.VMEM((n_line, SLOTS, rows, width), BF),
        pltpu.VMEM((n_line, SLOTS, rows, width), BF),
        pltpu.VMEM((n_own + n_low + N_AWAY, N_SUB, rows, width), BF),
        pltpu.VMEM((4, 2 * N_SUB, rows, width), BF),
        pltpu.VMEM((8, width), F32),
        pltpu.VMEM((8, width), F32),
        pltpu.VMEM((n_line, 8, width), F32),
        pltpu.VMEM((n_line, 8, width), F32),
        dma((2,)),
        dma((n_sec, 2)),
        dma((n_sec, 2)),
        dma((n_sec,)),
        dma((n_sec, 2)),
        dma((n_sec, 2)),
        dma((n_sec + 6,)),
        dma,
        dma((4, 4)),
        dma((4, 4)),
        dma((2,)),
        dma((2,)),
        dma,
        dma,
        dma((4,)),
        dma((n_own + n_low + N_AWAY,)),
        dma((n_low + N_AWAY,)),
        dma((n_low + N_AWAY,)),
        dma((n_line, n_unit)),
        dma((n_line, n_unit)),
        dma((n_line, n_unit)),
        dma((n_line, n_unit)),
        dma((n_unit,)),
        dma((n_unit,)),
        dma((n_unit,)),
        dma((n_low * N_SUB,)),
        dma((n_low * N_SUB,)),
        dma((n_low * N_SUB,)),
        dma((1 + 2 * n_line,)),
        dma((1 + 2 * n_line,)),
    ]
    out, ig, gw, gd, small = pl.pallas_call(
        functools.partial(relay, n_sec, lines, tokens, width, ff),
        out_shape=(
            jax.ShapeDtypeStruct((1, tokens, width), BF),
            jax.ShapeDtypeStruct((1, tokens, width), BF),
            jax.ShapeDtypeStruct((width, ff), BF),
            jax.ShapeDtypeStruct((ff // 2, width), BF),
            jax.ShapeDtypeStruct((8, width), F32),
        ),
        in_specs=[any_spec] * 2 + [vmem_spec] * 2 + [any_spec] * 2 + [vmem_spec] * 4,
        out_specs=(any_spec, any_spec, any_spec, any_spec, vmem_spec),
        scratch_shapes=scratch,
        compiler_params=pltpu.CompilerParams(
            collective_id=0, has_side_effects=True, vmem_limit_bytes=63 * 2**20
        ),
    )(patches, cot, positions, counts.reshape(1, 1), wm, wd, gain, bias, bm, sv)
    return (
        out,
        ig,
        small[0:1],
        small[1:2],
        gw.astype(F32)[None],
        small[3:7].reshape(1, ff),
        small[2:3],
        gd.astype(F32)[None],
    )


def solution(mesh):
    n_sec, n_dp = mesh.shape["section"], mesh.shape["dp"]
    images = P(("section", "dp"), None, None)
    row = P("section", None)
    block = P("section", None, None)
    return jax.shard_map(
        functools.partial(on_device, n_sec, n_dp),
        mesh=mesh,
        in_specs=(images, images, images, P(("section", "dp")), row, row, block, row, row, block),
        out_specs=(images, images, row, row, block, row, row, block),
        check_vma=False,
    )
```

```python
import functools

import jax
import jax.numpy as jnp
from jax import lax
from jax.experimental import pallas as pl
from jax.experimental.pallas import tpu as pltpu
from jax.sharding import PartitionSpec as P

HEADS = 12
HEAD_DIM = 64
GROUP = 256
EPS = 1e-06
MESH = pl.DeviceIdType.MESH
BF = jnp.bfloat16
F32 = jnp.float32
HI = lax.Precision.HIGHEST
LAG_SIB, LAG_ONE, LAG_TWO, LAG_END = 1, 2, 4, 6
N_SUB = 2
SLOTS = 8
N_AWAY = 1


def nn(a, b, precision=None):
    return lax.dot_general(a, b, (((1,), (0,)), ((), ())), precision=precision, preferred_element_type=F32)


def nt(a, b, precision=None):
    return lax.dot_general(a, b, (((1,), (1,)), ((), ())), precision=precision, preferred_element_type=F32)


def tn(a, b, precision=None):
    return lax.dot_general(a, b, (((0,), (0,)), ((), ())), precision=precision, preferred_element_type=F32)


def normalise(x):
    centered = x - jnp.mean(x, axis=-1, keepdims=True)
    scale = lax.rsqrt(jnp.mean(centered * centered, axis=-1, keepdims=True) + EPS)
    return centered * scale, scale


def relay(
    n_sec, lines, tokens, width, ff,
    patches, cot, positions, counts, wm, wd, gain, bias, bm, sv,
    o_out, o_ig, o_w, o_d, o_small,
    hin, gin, act, big1, big2, big3, wv, dv, cs, tab, tabs, hout, gout, perm, bqk, freq,
    mine, zin, pin, sib, tmp, sg, sg_sib, sg_one, sg_two,
    w_sem, hin_r, gin_r, tab_r, hop_s, gop_s, ini_s, cot_r, wd_s, wd_r, det_s, det_r, out_r, ig_r,
    sib_s, sib_r, low_s, mine_r, za_s, zin_r, pb_s, pin_r, fin_l, fin_s, fin_r, guest_r, pass_s, pass_r, sg_s, sg_r,
):
    s = lax.axis_index("section")
    d = lax.axis_index("dp")
    core = lax.rem(d, 2)
    other = d + 1 - 2 * core
    even = lax.rem(s, 2) == 0
    odd = lax.rem(s, 2) == 1
    last = n_sec - 1
    half = tokens // 2
    n_main = (width // 256) * (ff // width)
    n_low = (ff // 2) // 256
    n_own = n_main + n_low
    n_chunk = n_own + n_low
    n_away = N_AWAY
    limit = jnp.where(
        s == 0, n_main, jnp.where(s == 1, n_own - n_away, jnp.where(s == last, n_chunk, n_own + n_away))
    )
    n_side = jnp.where(s == 1, n_low + n_away, jnp.where(s == last, n_low, 0))
    n_sub = N_SUB
    score_scale = HEAD_DIM ** (-0.5)

    def to_section(target):
        return {"section": target}

    def to_dp(target):
        return {"dp": target}

    def remote(src, dst, send, recv, device):
        return pltpu.make_async_remote_copy(
            src_ref=src, dst_ref=dst, send_sem=send, recv_sem=recv, device_id=device, device_id_type=MESH
        )

    spots = []
    for stride in lines:
        pos = lax.rem(d // stride, 4)
        near = d + (1 - 2 * lax.rem(pos, 2)) * stride
        across = d + (3 - 2 * pos) * stride
        inner = (pos == 1) | (pos == 2)
        outer = (pos == 0) | (pos == 3)
        spots.append((near, across, inner, outer))

    barrier = pltpu.get_barrier_semaphore()
    for step in range(1, n_sec):
        pl.semaphore_signal(barrier, inc=1, device_id=to_section(lax.rem(s + step, n_sec)), device_id_type=MESH)
    pl.semaphore_signal(barrier, inc=1, device_id=to_dp(other), device_id_type=MESH)
    for near, across, inner, outer in spots:
        pl.semaphore_signal(barrier, inc=1, device_id=to_dp(near), device_id_type=MESH)

        @pl.when(inner)
        def _():
            pl.semaphore_signal(barrier, inc=1, device_id=to_dp(across), device_id_type=MESH)

    load_w = pltpu.make_async_copy(wm.at[0], wv, w_sem.at[0])
    load_d = pltpu.make_async_copy(wd.at[0], dv.at[pl.ds(ff // 2, ff // 2)], w_sem.at[1])
    load_w.start()

    @pl.when(odd)
    def _():
        load_d.start()

    peers = n_sec + len(spots)
    for near, across, inner, outer in spots:
        peers = peers + jnp.where(inner, 1, 0)
    tab[...] = jnp.zeros_like(tab)
    tab[0, 0:2, :] = positions[0].astype(F32)
    tab[0, 2:3, :] = jnp.broadcast_to(counts[...].astype(F32), (1, tokens))
    pl.semaphore_wait(barrier, peers)

    tab_sends = []
    for step in range(1, n_sec):
        tab_sends.append(
            remote(tab.at[0], tabs.at[s], ini_s.at[step - 1], tab_r.at[s], to_section(lax.rem(s + step, n_sec)))
        )
    for send in tab_sends:
        send.start()
    tab_own = pltpu.make_async_copy(tab.at[0], tabs.at[s], tab_r.at[s])
    tab_own.start()
    def rows_of(h):
        return pl.ds(h * half, half)

    def patch_send(h):
        r = rows_of(h)
        return remote(patches.at[0, r], hin.at[s, r], ini_s.at[n_sec + h], hin_r.at[s, h], to_section(0))

    def patch_own(h):
        r = rows_of(h)
        return pltpu.make_async_copy(patches.at[0, r], hin.at[0, r], hin_r.at[0, h])

    def cot_send(h):
        r = rows_of(h)
        return remote(cot.at[0, r], gin.at[s, r], ini_s.at[n_sec + 2 + h], gin_r.at[s, h], to_section(last))

    def cot_own(h):
        r = rows_of(h)
        return pltpu.make_async_copy(cot.at[0, r], gin.at[last, r], gin_r.at[last, h])

    cot_out = remote(cot.at[0], gout.at[0], ini_s.at[n_sec + 2], cot_r, to_section(last - 1))

    def cot_on(h):
        r = rows_of(h)
        return remote(gout.at[0, r], gin.at[0, r], ini_s.at[n_sec + 4 + h], gin_r.at[0, h], to_section(last))

    @pl.when(s == 0)
    def _():
        for h in range(2):
            patch_own(h).start()

    @pl.when(s != 0)
    def _():
        for h in range(2):
            patch_send(h).start()

    @pl.when((s != 0) & (s != last))
    def _():
        for h in range(2):
            cot_send(h).start()

    @pl.when(s == last)
    def _():
        for h in range(2):
            cot_own(h).start()

    near0 = spots[0][0]
    side = lax.rem(d // lines[0], 2)
    n_part = 4
    part = (ff // 2) // 4 // n_part

    def down_rows(which_side, which_core, k):
        start = (which_side * 2 + which_core) * (n_part * part) + k * part
        return pl.ds(pl.multiple_of(start, part), part)

    def down_send(k):
        rows = down_rows(side, core, k)
        return remote(wd.at[0, rows], dv.at[rows], wd_s.at[0, k], wd_r.at[0, k], to_section(lax.rem(s + 1, n_sec)))

    def down_near(k):
        rows = down_rows(side, core, k)
        return remote(dv.at[rows], dv.at[rows], wd_s.at[1, k], wd_r.at[1, k], to_dp(near0))

    def down_pass(k):
        rows = down_rows(side, core, k)
        return remote(dv.at[rows], dv.at[rows], wd_s.at[2, k], wd_r.at[2, k], to_dp(other))

    def down_pass_far(k):
        rows = down_rows(1 - side, core, k)
        return remote(dv.at[rows], dv.at[rows], wd_s.at[3, k], wd_r.at[3, k], to_dp(other))

    n_direct = n_part // 2

    def down_out(k):
        to = hout.at[last, pl.ds((k - n_direct) * part, part)]
        send = remote(wd.at[0, down_rows(side, core, k)], to, wd_s.at[0, k], det_r.at[k - n_direct], to_section(last - 1))
        return send

    def down_on(k):
        held = hout.at[last, pl.ds((k - n_direct) * part, part)]
        to = dv.at[down_rows(side, core, k)]
        return remote(held, to, det_s.at[k - n_direct], wd_r.at[0, k], to_section(1))

    @pl.when(s == 0)
    def _():
        for k in range(n_direct):
            down_send(k).start()
            down_out(k + n_direct).start()

    @pl.when(s == last - 1)
    def _():
        for k in range(n_direct, n_part):
            down_out(k).wait_recv()
            down_on(k).start()
        for k in range(n_part):
            down_send(k).start()

    def table(i):
        pltpu.make_async_copy(tab.at[0], tabs.at[i], tab_r.at[i]).wait()
        angle = nn(jnp.transpose(tabs[i]), freq[...], HI)
        cs[i, 0] = jnp.cos(angle)
        cs[i, 1] = jnp.sin(angle)

    ahead = (s == 0) & (core == 0)

    @pl.when(even)
    def _():
        freq[...] = jnp.zeros_like(freq)
        freq[0:1, :] = sv[:, : width // 2]
        freq[1:2, :] = sv[:, width // 2 :]

        def early(i, carry):
            @pl.when((i == 0) | jnp.logical_not(ahead))
            def _():
                table(i)

            return carry

        lax.fori_loop(0, n_sec, early, 0)

    @pl.when(odd)
    def _():
        for i in range(n_sec):
            pltpu.make_async_copy(tab.at[0], tabs.at[i], tab_r.at[i]).wait()

    sg[...] = jnp.zeros_like(sg)

    @pl.when(even)
    def _():
        old = lax.broadcasted_iota(jnp.int32, (GROUP, GROUP), 0)
        new = lax.broadcasted_iota(jnp.int32, (GROUP, GROUP), 1)
        source = ((new & 127) >> 5) * 64 + (new >> 7) * 32 + (new & 31)
        perm[...] = jnp.where(old == source, 1.0, 0.0).astype(BF)
        moved = perm[...].astype(F32)
        for block in range(2 * width // GROUP):
            columns = slice(block * GROUP, (block + 1) * GROUP)
            row = jnp.broadcast_to(bm[:, columns], (8, GROUP))
            bqk[:, columns] = nn(row, moved, HI)

    load_w.wait()

    @pl.when(even)
    def _():
        moved = perm[...]
        for block in range(2 * width // GROUP):
            columns = slice(block * GROUP, (block + 1) * GROUP)
            wv[:, columns] = nn(wv[:, columns], moved).astype(BF)

    @pl.when(s == last - 1)
    def _():
        cot_out.wait_recv()
        for h in range(2):
            cot_on(h).start()
        for k in range(n_direct, n_part):
            down_on(k).wait_send()

    @pl.when(odd)
    def _():
        for k in [0, 2, 1, 3]:
            down_send(k).wait_recv()
            down_near(k).start()
            down_pass(k).start()

    lane = lax.broadcasted_iota(jnp.int32, (1, GROUP), 1)
    q_masks = [((lane & 127) >> 5) == e for e in range(4)]
    v_masks = [(lane >> 6) == e for e in range(4)]
    zero_low = jnp.zeros((), BF)

    def count_of(i):
        return tabs[i, 2:3, 0:1]

    def row_mask(i):
        ids = lax.broadcasted_iota(jnp.int32, (tokens, 1), 0).astype(F32)
        return jnp.where(ids < count_of(i), 1.0, 0.0)

    def key_mask(i):
        ids = lax.broadcasted_iota(jnp.int32, (1, tokens), 1).astype(F32)
        return ids < count_of(i)

    n_group = width // GROUP
    pairs = width // 2 // n_group

    def attention_forward(i, slot):
        x = hin[i].astype(F32)
        xhat, _ = normalise(x)
        a = (xhat * gain[...] + bias[...]).astype(BF)
        act[i] = a
        keys_on = key_mask(i)
        for g in range(n_group):
            cosine = cs[i, 0, :, g * pairs : (g + 1) * pairs]
            sine = cs[i, 1, :, g * pairs : (g + 1) * pairs]
            turned = []
            for which in range(2):
                lo = which * width + g * GROUP
                t = nn(a, wv[:, lo : lo + GROUP]) + bqk[0:1, lo : lo + GROUP]
                t1, t2 = t[:, :128], t[:, 128:]
                r = jnp.concatenate([t1 * cosine - t2 * sine, t1 * sine + t2 * cosine], axis=1)
                r = (r * score_scale if which == 0 else r).astype(BF)
                big1[i, :, lo : lo + GROUP] = r
                turned.append(r)
            lo = 2 * width + g * GROUP
            value = (nn(a, wv[:, lo : lo + GROUP]) + bm[:, lo : lo + GROUP]).astype(BF)
            big1[i, :, lo : lo + GROUP] = value
            query, key = turned
            weights = []
            for e in range(4):
                scores = nt(jnp.where(q_masks[e], query, zero_low), key)
                scores = jnp.where(keys_on, scores, -1e30)
                top = jnp.max(scores, axis=-1, keepdims=True)
                p = jnp.exp(scores - top)
                p = (p * (1.0 / jnp.sum(p, axis=-1, keepdims=True))).astype(BF)
                big2[i, :, (4 * g + e) * tokens : (4 * g + e + 1) * tokens] = p
                weights.append(p)
            stacked = jnp.concatenate([jnp.where(v_masks[e], value, zero_low) for e in range(4)], axis=0)
            context = nn(jnp.concatenate(weights, axis=1), stacked)
            lo = 3 * width + g * GROUP
            big1[i, :, lo : lo + GROUP] = context.astype(BF)
        for h in range(2):
            r = slice(h * half, (h + 1) * half)
            branch = nn(big1[i, r, 3 * width :], wv[:, 3 * width :]) + bm[:, 3 * width :]
            hout[slot, r] = (x[r] + row_mask(i)[r] * branch).astype(BF)
            send_hop(i, h)

    def norm_backward(x, g_up, gact):
        xhat, scale = normalise(x.astype(F32))
        sg[0:1, :] += jnp.sum(gact * xhat, axis=0, keepdims=True)
        sg[1:2, :] += jnp.sum(gact, axis=0, keepdims=True)
        gn = gact * gain[...]
        inside = gn - jnp.mean(gn, axis=-1, keepdims=True) - xhat * jnp.mean(gn * xhat, axis=-1, keepdims=True)
        return g_up + scale * inside

    def attention_backward(i, slot):
        g_up = gin[i].astype(F32)
        gb = row_mask(i) * g_up
        low = gb.astype(BF)
        dctx_all = nt(low, wv[:, 3 * width :]).astype(BF)
        for g in range(n_group):
            qlo, klo, vlo = g * GROUP, width + g * GROUP, 2 * width + g * GROUP
            query = big1[i, :, qlo : qlo + GROUP]
            key = big1[i, :, klo : klo + GROUP]
            value = big1[i, :, vlo : vlo + GROUP]
            dctx = dctx_all[:, g * GROUP : (g + 1) * GROUP]
            clo = 3 * width + g * GROUP
            both = dctx.astype(F32) * big1[i, :, clo : clo + GROUP].astype(F32)
            d_stack, p_stack, gs_list = [], [], []
            for e in range(4):
                d_e = jnp.where(v_masks[e], dctx, zero_low)
                gw = nt(d_e, value)
                p_low = big2[i, :, (4 * g + e) * tokens : (4 * g + e + 1) * tokens]
                inside = jnp.sum(jnp.where(v_masks[e], both, 0.0), axis=-1, keepdims=True)
                gs_list.append((p_low.astype(F32) * (gw - inside)).astype(BF))
                d_stack.append(d_e)
                p_stack.append(p_low)
            key_low = key * jnp.asarray(score_scale, BF)
            k_stack = jnp.concatenate([jnp.where(q_masks[e], key_low, zero_low) for e in range(4)], axis=0)
            q_stack = jnp.concatenate([jnp.where(q_masks[e], query, zero_low) for e in range(4)], axis=0)
            dq = nn(jnp.concatenate(gs_list, axis=1), k_stack)
            dk = tn(jnp.concatenate(gs_list, axis=0), q_stack)
            dval = tn(jnp.concatenate(p_stack, axis=0), jnp.concatenate(d_stack, axis=0))
            cosine = cs[i, 0, :, g * pairs : (g + 1) * pairs]
            sine = cs[i, 1, :, g * pairs : (g + 1) * pairs]
            turn = jnp.zeros((tokens, pairs), F32)
            for lo, grad, held, size in ((qlo, dq, query, 1.0 / score_scale), (klo, dk, key, 1.0)):
                g1, g2 = grad[:, :128], grad[:, 128:]
                r = held.astype(F32)
                turn = turn + (g2 * r[:, :128] - g1 * r[:, 128:]) * size
                raw = jnp.concatenate([g1 * cosine + g2 * sine, g2 * cosine - g1 * sine], axis=1).astype(BF)
                big3[i, :, lo : lo + GROUP] = raw
            big3[i, :, vlo : vlo + GROUP] = dval.astype(BF)
            sums = nn(tabs[i], turn, HI)
            at = g * pairs
            sg[2:3, at : at + pairs] += sums[0:1]
            at = width // 2 + g * pairs
            sg[2:3, at : at + pairs] += sums[1:2]
        gact = nt(big3[i, :, : 3 * width], wv[:, : 3 * width])
        gout[slot] = norm_backward(hin[i], g_up, gact).astype(BF)
        gin[i] = low

    piece = 512

    def down_ready(i):
        @pl.when(i == 0)
        def _():
            load_d.wait()
            for k in range(n_part):
                down_near(k).wait_recv()
                down_pass_far(k).start()
            for k in range(n_part):
                down_pass(k).wait_recv()
                down_pass_far(k).wait_recv()

    def dense_forward(i, h):
        r = slice(h * half, (h + 1) * half)
        x = hin[i, r].astype(F32)
        xhat, _ = normalise(x)
        a = (xhat * gain[...] + bias[...]).astype(BF)
        act[i, r] = a
        for k in range(ff // piece):
            lo = k * piece
            pre = nn(a, wv[:, lo : lo + piece]) + bm[:, lo : lo + piece]
            cdf = 0.5 + 0.5 * lax.erf(pre * (0.5**0.5))
            big1[i, r, lo : lo + piece] = (pre * cdf).astype(BF)
            pdf = jnp.exp(-0.5 * (pre * pre)) * 0.3989422804014327
            big2[i, r, lo : lo + piece] = (cdf + pre * pdf).astype(BF)
        if h == 0:
            down_ready(i)
        branch = nn(big1[i, r], dv[...]) + sv[...]
        hout[i, r] = (x + row_mask(i)[r] * branch).astype(BF)

    def dense_backward(i, slot):
        g_up = gin[i].astype(F32)
        gb = row_mask(i) * g_up
        low = gb.astype(BF)
        for k in range(ff // width):
            for m in range(width // GROUP):
                lo = k * width + m * GROUP
                gh = nt(low, dv[lo : lo + GROUP, :])
                gpre = (gh * big2[i, :, lo : lo + GROUP].astype(F32)).astype(BF)
                big3[i, :, lo : lo + GROUP] = gpre
        gact = nt(big3[i], wv[...])
        gout[slot] = norm_backward(hin[i], g_up, gact).astype(BF)
        gin[i] = low

    def hop_send(i, h):
        r = rows_of(h)
        to = to_section(lax.rem(s + 1, n_sec))
        return remote(hout.at[i, r], hin.at[i, r], hop_s.at[i, h], hin_r.at[i, h], to)

    def result_send(i):
        return remote(hout.at[i], o_out.at[0], hop_s.at[i, 0], out_r, to_section(i))

    def back_send(i, slot, h):
        r = rows_of(h)
        to = to_section(lax.rem(s + last, n_sec))
        return remote(gout.at[slot, r], gin.at[i, r], gop_s.at[i, h], gin_r.at[i, h], to)

    def input_send(i, slot):
        return remote(gout.at[slot], o_ig.at[0], gop_s.at[i, 0], ig_r, to_section(i))

    def send_hop(i, h):
        @pl.when((s != last) & (i >= 1))
        def _():
            hop_send(i - 1, h).wait_send()

        @pl.when(s != last)
        def _():
            hop_send(i, h).start()

    def send_back(i, slot, h):
        @pl.when((s != 0) & (i >= 1))
        def _():
            back_send(i - 1, 1 - slot, h).wait_send()

        @pl.when(s != 0)
        def _():
            back_send(i, slot, h).start()

    def forward(i):
        @pl.when(even)
        def _():
            for h in range(2):
                hop_send(i, h).wait_recv()
            attention_forward(i, i)

        @pl.when(odd)
        def _():
            for h in range(2):
                hop_send(i, h).wait_recv()
                dense_forward(i, h)
                send_hop(i, h)

    def backward(i):
        slot = lax.rem(i, 2)

        @pl.when((i == 0) & (s == last - 1))
        def _():
            for h in range(2):
                cot_on(h).wait_send()

        @pl.when((i == 2) & (s == 0))
        def _():
            pltpu.make_async_copy(gout.at[slot], o_ig.at[0], ig_r).wait()

        @pl.when(even)
        def _():
            for h in range(2):
                back_send(i, slot, h).wait_recv()
            attention_backward(i, slot)
            for h in range(2):
                send_back(i, slot, h)

        @pl.when(odd)
        def _():
            for h in range(2):
                back_send(i, slot, h).wait_recv()
            dense_backward(i, slot)
            for h in range(2):
                send_back(i, slot, h)

        @pl.when((s == 0) & (i >= 2))
        def _():
            input_send(i - 1, 1 - slot).wait_send()

        @pl.when((s == 0) & (i != 0))
        def _():
            input_send(i, slot).start()

        @pl.when((s == 0) & (i == 0))
        def _():
            pltpu.make_async_copy(gout.at[slot], o_ig.at[0], ig_r).start()

    def tick(j, carry):
        is_forward = jnp.where(s == last, lax.rem(j, 2) == 0, j < n_sec)
        i = jnp.where(s == last, j // 2, lax.rem(j, n_sec))

        @pl.when(is_forward)
        def _():
            forward(i)

        @pl.when((s == 0) & (j == 0))
        def _():
            cot_out.start()

        @pl.when(ahead & (j == 0))
        def _():
            lax.fori_loop(1, n_sec, lambda i, carry: (table(i), carry)[1], 0)

        @pl.when(jnp.logical_not(is_forward))
        def _():
            backward(i)

        return carry

    lax.fori_loop(0, 2 * n_sec, tick, 0)

    @pl.when(s == last)
    def _():
        for i in range(last):
            result_send(i).start()
        pltpu.make_async_copy(hout.at[last], o_out.at[0], out_r).start()

    def bias_sums():
        ones = jnp.ones((16, n_sec * tokens), BF)

        def column_sum(held):
            return nn(ones, held.reshape(n_sec * tokens, width))[0:1]

        masked = column_sum(gin[...])
        for k in range(3):
            sg[3 + k : 4 + k, :] = column_sum(big3[:, :, k * width : (k + 1) * width])

        @pl.when(odd)
        def _():
            sg[2:3, :] = masked
            sg[6:7, :] = column_sum(big3[:, :, 3 * width :])

        @pl.when(even)
        def _():
            sg[6:7, :] = masked
            back = perm[...].astype(F32)
            for block in range(2 * width // GROUP):
                row = 3 + block * GROUP // width
                lo = block * GROUP % width
                part = jnp.broadcast_to(sg[row : row + 1, lo : lo + GROUP], (8, GROUP))
                sg[row : row + 1, lo : lo + GROUP] = nt(part, back, HI)[0:1]

    my_half = pl.ds(core * n_sub, n_sub)
    their_half = pl.ds((1 - core) * n_sub, n_sub)

    def is_own(c):
        after = ((s == 1) & (c >= n_main) & (c < n_own - n_away)) | ((s == last) & (c >= n_own) & (c < n_chunk))
        return ((c >= 0) & (c < n_main)) | after

    def is_guest(c):
        return ((s >= 2) & (c >= n_main) & (c < n_own)) | ((s == last - 1) & (c >= n_own) & (c < n_own + n_away))

    def sib_slot(c):
        return jnp.where(c >= n_own, c - n_low, c)

    def sib_copy(c):
        slot = lax.rem(c, 2)
        at = sib_slot(c)
        return remote(tmp.at[slot, their_half], sib.at[at], sib_s.at[slot], sib_r.at[at], to_dp(other))

    def side_copy(b):
        slot = 2 + lax.rem(b, 2)
        at = n_own + b
        return remote(tmp.at[slot, their_half], sib.at[at], sib_s.at[slot], sib_r.at[at], to_dp(other))

    def side_send(b):
        to = jnp.where((s == 1) & (b < n_low), last, last - 1)
        return remote(
            sib.at[n_own + b], mine.at[pl.ds((n_main + b) * n_sub, n_sub)], low_s.at[b], mine_r.at[b], to_section(to)
        )

    def make_down(slot, row):
        rows = pl.ds(pl.multiple_of(row, 256), 256)
        left = big1[:, :, rows].reshape(n_sec * tokens, 256)
        right = gin[...].reshape(n_sec * tokens, width)
        keep(slot, tn(left, right))

    def keep(slot, block):
        tmp[slot] = block.astype(BF).reshape(2 * n_sub, half // n_sub, width)

    def make_side(b):
        slot = 2 + lax.rem(b, 2)

        @pl.when(b >= 2)
        def _():
            side_copy(b - 2).wait_send()

        make_down(slot, jnp.where(b < n_low, b, b + n_low - n_away) * 256)
        side_copy(b).start()

    def send_side(b):
        slot = 2 + lax.rem(b, 2)
        at = n_own + b
        side_copy(b).wait_recv()
        sib[at] = (tmp[slot, my_half].astype(F32) + sib[at].astype(F32)).astype(BF)
        side_send(b).start()

    def make_block(c):
        slot = lax.rem(c, 2)

        @pl.when(c >= 2)
        def _():
            sib_copy(c - 2).wait_send()

        column = lax.rem(c, ff // width)
        row = c // (ff // width)
        from_act = (c < n_main) & (odd | (column < 3))

        @pl.when(from_act)
        def _():
            rows = pl.ds(pl.multiple_of(row * 256, 256), 256)
            columns = pl.ds(pl.multiple_of(column * width, width), width)
            left = act[:, :, rows].reshape(n_sec * tokens, 256)
            right = big3[:, :, columns].reshape(n_sec * tokens, width)
            keep(slot, tn(left, right))

        @pl.when(from_act & even & (column < 2))
        def _():
            back = perm[...]
            held = tmp[slot].reshape(2 * half, width)
            keep(
                slot,
                jnp.concatenate(
                    [nt(held[:, k * GROUP : (k + 1) * GROUP], back) for k in range(width // GROUP)], axis=1
                ),
            )

        @pl.when(jnp.logical_not(from_act))
        def _():
            upper = ff // 2 + jnp.where(s == last, c - n_own, c - n_main) * 256
            make_down(slot, jnp.where(even, 3 * width + row * 256, upper))

        sib_copy(c).start()

    def spot_copies(k, u):
        near, across, inner, outer = spots[k]
        held = lax.rem(u, SLOTS)
        to_near = remote(mine.at[u], zin.at[k, held], za_s.at[k, u], zin_r.at[k, u], to_dp(near))
        to_across = remote(zin.at[k, held], pin.at[k, held], pb_s.at[k, u], pin_r.at[k, u], to_dp(across))
        return to_near, to_across

    piece_rows = half // n_sub

    def w_place(u):
        c = u // n_sub
        row = c // (ff // width)
        column = lax.rem(c, ff // width)
        start = row * 256 + core * half + lax.rem(u, n_sub) * piece_rows
        rows = pl.ds(pl.multiple_of(start, piece_rows), piece_rows)
        columns = pl.ds(pl.multiple_of(column * width, width), width)
        return o_w.at[rows, columns]

    def d_rows(block, sub):
        start = block * 256 + core * half + sub * piece_rows
        return o_d.at[pl.ds(pl.multiple_of(start, piece_rows), piece_rows), :]

    def d_place(u):
        c = u // n_sub
        late = jnp.where(s == last, c - n_own, c - n_own + n_low - n_away)
        return d_rows(jnp.where(c < n_own, c - n_main, late), lax.rem(u, n_sub))

    def finish_copies(u, place):
        here = pltpu.make_async_copy(mine.at[u], place, fin_l.at[u])
        there = remote(mine.at[u], place, fin_s.at[u], fin_r.at[u], to_dp(other))
        return here, there

    def is_away(u):
        return ((s == last) & (u < n_own * n_sub)) | ((s == last - 1) & (u >= n_own * n_sub))

    def guest_send(u):
        at = jnp.where(s == last, u - n_main * n_sub, u - n_own * n_sub)
        to = jnp.where(s == last, 0, 1)
        return remote(mine.at[u], d_place(u), fin_s.at[u], guest_r.at[at], to_section(to))

    def returned(g):
        block = g // n_sub + jnp.where(s == 0, 0, n_low - n_away)
        return d_rows(block, lax.rem(g, n_sub))

    def guest_take(g):
        return remote(mine.at[0], returned(g), pass_s.at[g], guest_r.at[g], to_dp(other))

    def guest_pass(g):
        return remote(returned(g), returned(g), pass_s.at[g], pass_r.at[g], to_dp(other))

    n_returned = jnp.where(s == 0, n_low * n_sub, jnp.where(s == 1, n_away * n_sub, 0))

    def finish(u):
        @pl.when(u < n_main * n_sub)
        def _():
            here, there = finish_copies(u, w_place(u))
            here.start()
            there.start()

        @pl.when((u >= n_main * n_sub) & jnp.logical_not(is_away(u)))
        def _():
            here, there = finish_copies(u, d_place(u))
            here.start()
            there.start()

        @pl.when((u >= n_main * n_sub) & is_away(u))
        def _():
            guest_send(u).start()

    small_sib = remote(sg, sg_sib, sg_s.at[0], sg_r.at[0], to_dp(other))

    def small_copies(k):
        near, across, inner, outer = spots[k]
        to_near = remote(sg, sg_one.at[k], sg_s.at[1 + 2 * k], sg_r.at[1 + 2 * k], to_dp(near))
        to_across = remote(sg_one.at[k], sg_two.at[k], sg_s.at[2 + 2 * k], sg_r.at[2 + 2 * k], to_dp(across))
        return to_near, to_across

    n_unit = n_chunk * n_sub
    my_units = limit * n_sub
    steps = my_units + n_sub * LAG_SIB + len(lines) * LAG_END + 1

    def sum_step(t, carry):
        c = t // n_sub
        first = lax.rem(t, n_sub) == 0
        second = lax.rem(t, n_sub) == 1

        @pl.when(first & is_own(c))
        def _():
            make_block(c)

        @pl.when(second & (c < n_side))
        def _():
            make_side(c)

        c1 = c - LAG_SIB

        @pl.when(first & is_own(c1))
        def _():
            slot = lax.rem(c1, 2)
            at = sib_slot(c1)
            sib_copy(c1).wait_recv()
            mine[pl.ds(c1 * n_sub, n_sub)] = (tmp[slot, my_half].astype(F32) + sib[at].astype(F32)).astype(BF)

        @pl.when(second & (c1 >= 0) & (c1 < n_side))
        def _():
            send_side(c1)

        @pl.when(first & is_guest(c1))
        def _():
            side_send(c1 - n_main).wait_recv()

        @pl.when(t == 5)
        def _():
            bias_sums()
            small_sib.start()

        @pl.when(t == 8)
        def _():
            small_sib.wait()
            sg[...] = sg[...] + sg_sib[...]

        for k in range(len(lines)):
            near, across, inner, outer = spots[k]
            small_near, small_across = small_copies(k)
            at = 8 + 9 * k

            @pl.when(outer & (t == at))
            def _():
                small_near.start()

            @pl.when(inner & (t == at + 3))
            def _():
                small_near.wait_recv()
                sg_one[k] = sg[...] + sg_one[k]
                small_across.start()

            @pl.when(inner & (t == at + 6))
            def _():
                small_across.wait()
                sg[...] = sg_one[k] + sg_two[k]
                small_near.start()
                small_near.wait_send()

            @pl.when(outer & (t == at + 9))
            def _():
                small_near.wait()
                sg[...] = sg_one[k]

        for k in range(len(lines)):
            near, across, inner, outer = spots[k]
            base = LAG_SIB * n_sub + k * LAG_END
            u0 = t - base

            @pl.when(outer & (u0 >= 0) & (u0 < my_units))
            def _():
                to_near, _ = spot_copies(k, u0)
                to_near.start()

            u2 = t - base - LAG_ONE

            @pl.when(inner & (u2 >= 0) & (u2 < my_units))
            def _():
                to_near, to_across = spot_copies(k, u2)
                to_near.wait_recv()
                held = lax.rem(u2, SLOTS)
                zin[k, held] = (mine[u2].astype(F32) + zin[k, held].astype(F32)).astype(BF)
                to_across.start()

            u3 = t - base - LAG_TWO

            @pl.when(inner & (u3 >= 0) & (u3 < my_units))
            def _():
                to_near, to_across = spot_copies(k, u3)
                to_across.wait()
                held = lax.rem(u3, SLOTS)
                mine[u3] = (zin[k, held].astype(F32) + pin[k, held].astype(F32)).astype(BF)
                to_near.start()
                if k == len(lines) - 1:
                    finish(u3)

            u4 = t - base - LAG_END

            @pl.when(outer & (u4 >= 0) & (u4 < my_units))
            def _():
                to_near, _ = spot_copies(k, u4)
                to_near.wait()
                mine[u4] = zin[k, lax.rem(u4, SLOTS)]
                if k == len(lines) - 1:
                    finish(u4)

        return carry

    lax.fori_loop(0, steps, sum_step, 0)

    def take(g, carry):
        guest_take(g).wait_recv()
        guest_pass(g).start()
        return carry

    lax.fori_loop(0, n_returned, take, 0)
    o_small[...] = sg[...]

    for send in tab_sends:
        send.wait_send()

    @pl.when(s != 0)
    def _():
        for h in range(2):
            patch_send(h).wait_send()

    @pl.when(s == 0)
    def _():
        cot_out.wait_send()

    @pl.when((s != 0) & (s != last))
    def _():
        for h in range(2):
            cot_send(h).wait_send()

    @pl.when(even)
    def _():
        for k in range(n_part):
            down_send(k).wait_send()

    sib_copy(0).wait_send()
    sib_copy(1).wait_send()

    @pl.when(odd)
    def _():
        for k in range(n_part):
            down_near(k).wait_send()
            down_pass(k).wait_send()
            down_pass_far(k).wait_send()
        side_copy(0).wait_send()
        side_copy(1).wait_send()
        for b in range(n_low):
            side_send(b).wait_send()

    @pl.when(s == 1)
    def _():
        for b in range(n_low, n_low + n_away):
            side_send(b).wait_send()

    @pl.when(s == 0)
    def _():
        input_send(last, last % 2).wait_send()

    @pl.when(s != 0)
    def _():
        for h in range(2):
            back_send(last, last % 2, h).wait_send()

    @pl.when(s != last)
    def _():
        for h in range(2):
            hop_send(last, h).wait_send()

    @pl.when(s == last)
    def _():
        for i in range(last):
            result_send(i).wait_send()

    pltpu.make_async_copy(hout.at[0], o_out.at[0], out_r).wait()

    @pl.when(s != 0)
    def _():
        pltpu.make_async_copy(gout.at[0], o_ig.at[0], ig_r).wait()

    for k in range(len(lines)):
        near, across, inner, outer = spots[k]

        @pl.when(inner)
        def _():
            def drain(u, carry):
                to_near, _ = spot_copies(k, u)
                to_near.wait_send()
                return carry

            lax.fori_loop(0, my_units, drain, 0)

    def drain_main(u, carry):
        here, there = finish_copies(u, w_place(u))
        here.wait()
        there.wait()
        return carry

    def drain_down(u, carry):
        here, there = finish_copies(u, d_place(u))
        here.wait()
        there.wait()
        return carry

    def drain_guest(u, carry):
        guest_send(u).wait_send()
        return carry

    def drain_pass(g, carry):
        guest_pass(g).wait()
        return carry

    lax.fori_loop(0, n_main * n_sub, drain_main, 0)
    lax.fori_loop(0, n_returned, drain_pass, 0)

    @pl.when(s == 1)
    def _():
        lax.fori_loop(n_main * n_sub, (n_own - n_away) * n_sub, drain_down, 0)

    @pl.when(s == last - 1)
    def _():
        lax.fori_loop(n_main * n_sub, n_own * n_sub, drain_down, 0)
        lax.fori_loop(n_own * n_sub, (n_own + n_away) * n_sub, drain_guest, 0)

    @pl.when(s == last)
    def _():
        lax.fori_loop(n_main * n_sub, n_own * n_sub, drain_guest, 0)
        lax.fori_loop(n_own * n_sub, n_unit, drain_down, 0)


def line_strides(n_dp):
    chips, stride, strides = n_dp // 2, 2, []
    while chips > 1:
        assert chips % 4 == 0
        strides.append(stride)
        stride, chips = stride * 4, chips // 4
    return strides


def on_device(n_sec, n_dp, patches, cot, positions, counts, gain, bias, wm, bm, sv, wd):
    _, tokens, width = patches.shape
    ff = wm.shape[2]
    lines = line_strides(n_dp)
    n_low = (ff // 2) // 256
    n_own = (width // 256) * (ff // width) + n_low
    n_chunk = n_own + n_low
    n_unit, rows = n_chunk * N_SUB, 128 // N_SUB
    any_spec = pl.BlockSpec(memory_space=pl.ANY)
    vmem_spec = pl.BlockSpec(memory_space=pltpu.VMEM)
    image = (n_sec, tokens, width)
    wide = (n_sec, tokens, ff)
    dma = pltpu.SemaphoreType.DMA
    n_line = len(lines)
    scratch = [
        pltpu.VMEM(image, BF),
        pltpu.VMEM(image, BF),
        pltpu.VMEM(image, BF),
        pltpu.VMEM(wide, BF),
        pltpu.VMEM(wide, BF),
        pltpu.VMEM(wide, BF),
        pltpu.VMEM((width, ff), BF),
        pltpu.VMEM((ff, width), BF),
        pltpu.VMEM((n_sec, 2, tokens, width // 2), F32),
        pltpu.VMEM((1, 8, tokens), F32),
        pltpu.VMEM((n_sec, 8, tokens), F32),
        pltpu.VMEM(image, BF),
        pltpu.VMEM((2, tokens, width), BF),
        pltpu.VMEM((GROUP, GROUP), BF),
        pltpu.VMEM((8, 2 * width), F32),
        pltpu.VMEM((8, width // 2), F32),
        pltpu.VMEM((n_unit, rows, width), BF),
        pltpu.VMEM((n_line, SLOTS, rows, width), BF),
        pltpu.VMEM((n_line, SLOTS, rows, width), BF),
        pltpu.VMEM((n_own + n_low + N_AWAY, N_SUB, rows, width), BF),
        pltpu.VMEM((4, 2 * N_SUB, rows, width), BF),
        pltpu.VMEM((8, width), F32),
        pltpu.VMEM((8, width), F32),
        pltpu.VMEM((n_line, 8, width), F32),
        pltpu.VMEM((n_line, 8, width), F32),
        dma((2,)),
        dma((n_sec, 2)),
        dma((n_sec, 2)),
        dma((n_sec,)),
        dma((n_sec, 2)),
        dma((n_sec, 2)),
        dma((n_sec + 6,)),
        dma,
        dma((4, 4)),
        dma((4, 4)),
        dma((2,)),
        dma((2,)),
        dma,
        dma,
        dma((4,)),
        dma((n_own + n_low + N_AWAY,)),
        dma((n_low + N_AWAY,)),
        dma((n_low + N_AWAY,)),
        dma((n_line, n_unit)),
        dma((n_line, n_unit)),
        dma((n_line, n_unit)),
        dma((n_line, n_unit)),
        dma((n_unit,)),
        dma((n_unit,)),
        dma((n_unit,)),
        dma((n_low * N_SUB,)),
        dma((n_low * N_SUB,)),
        dma((n_low * N_SUB,)),
        dma((1 + 2 * n_line,)),
        dma((1 + 2 * n_line,)),
    ]
    out, ig, gw, gd, small = pl.pallas_call(
        functools.partial(relay, n_sec, lines, tokens, width, ff),
        out_shape=(
            jax.ShapeDtypeStruct((1, tokens, width), BF),
            jax.ShapeDtypeStruct((1, tokens, width), BF),
            jax.ShapeDtypeStruct((width, ff), BF),
            jax.ShapeDtypeStruct((ff // 2, width), BF),
            jax.ShapeDtypeStruct((8, width), F32),
        ),
        in_specs=[any_spec] * 2 + [vmem_spec] * 2 + [any_spec] * 2 + [vmem_spec] * 4,
        out_specs=(any_spec, any_spec, any_spec, any_spec, vmem_spec),
        scratch_shapes=scratch,
        compiler_params=pltpu.CompilerParams(
            collective_id=0, has_side_effects=True, vmem_limit_bytes=63 * 2**20
        ),
    )(patches, cot, positions, counts.reshape(1, 1), wm, wd, gain, bias, bm, sv)
    return (
        out,
        ig,
        small[0:1],
        small[1:2],
        gw.astype(F32)[None],
        small[3:7].reshape(1, ff),
        small[2:3],
        gd.astype(F32)[None],
    )


def solution(mesh):
    n_sec, n_dp = mesh.shape["section"], mesh.shape["dp"]
    images = P(("section", "dp"), None, None)
    row = P("section", None)
    block = P("section", None, None)
    return jax.shard_map(
        functools.partial(on_device, n_sec, n_dp),
        mesh=mesh,
        in_specs=(images, images, images, P(("section", "dp")), row, row, block, row, row, block),
        out_specs=(images, images, row, row, block, row, row, block),
        check_vma=False,
    )
```
